512 devices in a mesh: group: 32 (over y, x), dev: 16 (over z, core).
Axes of the slice: x: 4, y: 8, z: 8, core: 2. Of those that a mesh axis runs over, the one named last changes fastest.
Arguments:
- tokens: bfloat16 [4096, 3584], P('group', 'dev'), may hold values from -6 to 6
- upstream: bfloat16 [4096, 3584], P('group', 'dev'), may hold values from -6 to 6
- route_probs: float32 [4096, 4], P('group'), may hold values from 0.05 to 1
- expert_ids: int32 [4096, 4], P('group'), may hold values from 0 to 31, all different within a row; in each aligned block of 128 rows (0 to 127, 128 to 255, ...) at most 18 rows name the same one
- w_gate: bfloat16 [32, 3584, 2048], P('group', None, 'dev'), may hold values from -0.09375 to 0.09375
- w_up: bfloat16 [32, 3584, 2048], P('group', None, 'dev'), may hold values from -0.09375 to 0.09375
- w_down: bfloat16 [32, 2048, 3584], P('group', 'dev'), may hold values from -0.125 to 0.125
Outputs:
- grad_tokens: bfloat16 [4096, 3584], P('group', 'dev')
- grad_probs: float32 [4096, 4], P('group')
The draws below stay inside these ranges and needn't reach their ends.
Inputs may be any that keep to these rules, and one draw needn't show every extreme that they name: `expert_ids`: in each block of 128 tokens (one index of group) no expert is named by more than 18 routes, a bound that some block reaches; a token's experts differ.
All inputs are finite; a program needn't handle non-finite values.
Results may differ from the reference program's by a relative error of at most 0.024.
Values may be sent and summed in bfloat16 or wider, within the bound.
A program may use at most 64 MiB of HBM per device.

```python
import math
import jax
import jax.numpy as jnp
import numpy as np
from jax import lax

D = 3584
FF = 2048
TOP = 4
TOK_G = 128
EXPERTS = 32
FF_DEV = 128
CAP = 18
TOKENS = 4096
N_GROUP = 32


def block_levels(rng, shape, pieces, smallest, high):
    loudness = 1.0
    for axis_at, shards_of in pieces:
        draws = jax.random.uniform(jax.random.fold_in(jax.random.fold_in(rng, 6), axis_at), (shards_of,), jnp.float32, smallest / len(pieces), high / len(pieces))
        loudness = loudness * jnp.repeat(jnp.exp(draws), shape[axis_at] // shards_of).reshape((-1,) + (1,) * (len(shape) - 1 - axis_at))
    return loudness


def routed_block(key, own, number, rows, number_of, top, bound, skew):
    order = jax.random.permutation(key, number_of)
    heavy_load, common = portions_of(number_of, rows * top, bound, skew, True), portions_of(number_of, rows * top, bound, skew, False)
    places = jnp.arange(number_of)

    def named(lengths, rotation):
        used = int((lengths > 0).sum())
        fixed = max(1, used // 4)
        moved = fixed + (places - fixed + rotation * (used - fixed)) % max(1, number_of - fixed)
        return jnp.zeros((number_of,), jnp.int32).at[order[jnp.where(places < fixed, places, moved)]].set(jnp.asarray(lengths, jnp.int32))

    lengths = jnp.where(number % 4 == 0, named(heavy_load, number // 4), named(common, number - number // 4 - 1))
    mixed = jax.random.permutation(jax.random.fold_in(own, 3), number_of)
    donor, receiver = mixed[0:number_of // 2 * 2:2], mixed[1:number_of // 2 * 2:2]
    slack = jnp.minimum(lengths[donor] - 1, bound - lengths[receiver]) // 2
    slack = jnp.where((donor == order[0]) | (receiver == order[0]) | (lengths[receiver] == 0), 0, jnp.maximum(slack, 0))
    moved = jax.random.randint(jax.random.fold_in(own, 4), (number_of // 2,), 0, 1 << 20) % (slack + 1)
    lengths = lengths.at[donor].add(-moved).at[receiver].add(moved)
    labels = jnp.searchsorted(jnp.cumsum(lengths), jnp.arange(rows * top), side="right").astype(jnp.int32)
    listing = labels.reshape(top, rows).T
    listing = listing[jax.random.permutation(jax.random.fold_in(own, 1), rows)]
    rotation = jax.random.randint(jax.random.fold_in(own, 2), (rows, 1), 0, top)
    return jnp.take_along_axis(listing, (jnp.arange(top)[None, :] + rotation) % top, axis=1)


def portions_of(number_of, total, bound, skew, full):
    portions = [(1 << 20) // math.isqrt(standing ** skew) + 1 for standing in range(1, number_of + 1)]
    largest = bound if full else min(bound, max(-(-total // number_of), total * portions[0] // sum(portions)))
    least = 1 if total - largest >= number_of - 1 else 0
    given, surplus = [largest] + [least] * (number_of - 1), total - largest - least * (number_of - 1)
    while surplus > 0:
        free = [i for i in range(1, number_of) if given[i] < largest] or [i for i in range(1, number_of) if given[i] < bound]
        whole, remaining = sum([portions[i] for i in free]), surplus
        for i in free:
            addition = min(bound - given[i], max(1, remaining * portions[i] // whole), surplus)
            given[i] = given[i] + addition
            surplus = surplus - addition
    return np.array(given)


def centred(stream_key, dims, spread, most, shards=(), held_as=jnp.bfloat16):
    level = block_levels(stream_key, dims, shards, -0.22, 0.18) if shards else 1.0
    values = jax.random.normal(stream_key, dims, jnp.float32) * spread * level
    return jnp.minimum(jnp.maximum(values, -most), most).astype(held_as)


def setup_inputs(seed: int = 0) -> dict:
    keys = jax.random.split(jax.random.key(seed), 8)
    tokens = centred(keys[0], (TOKENS, D), 1.0, 6.0, ((0, 32), (1, 16)))
    upstream = centred(keys[1], (TOKENS, D), 1.0, 6.0, ((0, 32), (1, 16)))
    route_probs = jnp.clip(jnp.exp(math.log(1.0) - 2.9957323 * jax.random.uniform(keys[2], (TOKENS, TOP), jnp.float32) ** block_levels(keys[2], (TOKENS, TOP), ((0, 32),), -0.2, 0.2)), 0.05, 1.0)
    expert_ids_keys = jax.random.split(jax.random.fold_in(keys[3], 1), TOKENS // TOK_G)
    expert_ids_turns = jax.random.permutation(jax.random.fold_in(keys[3], 3), TOKENS // TOK_G)
    expert_ids = jax.vmap(lambda own, number: routed_block(jax.random.fold_in(keys[3], 2), own, number, TOK_G, EXPERTS, TOP, CAP, 1))(expert_ids_keys, expert_ids_turns).reshape((TOKENS, TOP))
    w_gate = centred(keys[4], (EXPERTS, D, FF), D ** -0.5, 0.09375, ((0, 32), (2, 16)))
    w_up = centred(keys[5], (EXPERTS, D, FF), D ** -0.5, 0.09375, ((0, 32), (2, 16)))
    w_down = centred(keys[6], (EXPERTS, FF, D), FF ** -0.5, 0.125, ((0, 32), (1, 16)))
    return {"tokens": tokens, "upstream": upstream, "route_probs": route_probs, "expert_ids": expert_ids, "w_gate": w_gate, "w_up": w_up, "w_down": w_down}


def slot_index(expert_ids):
    flat = expert_ids.reshape(N_GROUP, TOK_G * TOP)
    onehot = (flat[:, :, None] == jnp.arange(EXPERTS, dtype=jnp.int32)).astype(jnp.int32)
    before = jnp.cumsum(onehot, axis=1) - onehot
    place = jnp.sum(before * onehot, axis=-1)
    source = jnp.arange(N_GROUP, dtype=jnp.int32)[:, None]
    return (flat * (N_GROUP * CAP) + source * CAP + place).reshape(-1).astype(jnp.int32)


def reference(tokens, upstream, route_probs, expert_ids, w_gate, w_up, w_down):
    routes = TOKENS * TOP
    rows_e = N_GROUP * CAP
    blocks = FF // FF_DEV
    slot = slot_index(expert_ids)
    table = jnp.full((EXPERTS * rows_e,), routes, jnp.int32).at[slot].set(jnp.arange(routes, dtype=jnp.int32))
    owner = jnp.where(table < routes, table // TOP, TOKENS).astype(jnp.int32)
    flat_probs = jnp.concatenate([route_probs.reshape(-1), jnp.zeros((1,), jnp.float32)])
    tok_ext = jnp.concatenate([tokens, jnp.zeros((1, D), jnp.bfloat16)])
    grad_ext = jnp.concatenate([upstream, jnp.zeros((1, D), jnp.bfloat16)])

    def one_expert(expert):
        owners = lax.dynamic_slice_in_dim(owner, expert * rows_e, rows_e)
        picks = lax.dynamic_slice_in_dim(table, expert * rows_e, rows_e)
        rows_x = tok_ext[owners]
        rows_dy = (flat_probs[picks][:, None] * grad_ext[owners].astype(jnp.float32)).astype(jnp.bfloat16)
        wgate = w_gate[expert]
        wup = w_up[expert]
        wdown = w_down[expert]
        gate = jnp.dot(rows_x, wgate, preferred_element_type=jnp.float32)
        upper = jnp.dot(rows_x, wup, preferred_element_type=jnp.float32)
        back = lax.dot_general(rows_dy, wdown, (((1,), (1,)), ((), ())), preferred_element_type=jnp.float32)
        sig = jax.nn.sigmoid(gate)
        act = gate * sig
        slope = sig * (1.0 + gate * (1.0 - sig))
        score = jnp.sum(act * upper * back, axis=-1)
        d_gate = (back * upper * slope).astype(jnp.bfloat16).astype(jnp.float32)
        d_up = (back * act).astype(jnp.bfloat16).astype(jnp.float32)
        term = jnp.einsum('rbf,dbf->rbd', d_gate.reshape(rows_e, blocks, FF_DEV), wgate.astype(jnp.float32).reshape(D, blocks, FF_DEV))
        term = term + jnp.einsum('rbf,dbf->rbd', d_up.reshape(rows_e, blocks, FF_DEV), wup.astype(jnp.float32).reshape(D, blocks, FF_DEV))
        rounded = lax.optimization_barrier(term.astype(jnp.bfloat16))
        return jnp.sum(rounded.astype(jnp.float32), axis=1), score

    rows_grad, scores = lax.map(one_expert, jnp.arange(EXPERTS, dtype=jnp.int32))
    per_route = rows_grad.reshape(-1, D)[slot].reshape(TOKENS, TOP, D)
    grad_tokens = jnp.sum(per_route, axis=1).astype(jnp.bfloat16)
    grad_probs = scores.reshape(-1)[slot].reshape(TOKENS, TOP) / route_probs
    return grad_tokens, grad_probs
```

```python
import functools

import jax
import jax.numpy as jnp
from jax import lax
from jax.experimental import pallas as pl
from jax.experimental.pallas import tpu as pltpu
from jax.sharding import PartitionSpec as P

BF16 = jnp.bfloat16
F32 = jnp.float32
I32 = jnp.int32
MESH = pl.DeviceIdType.MESH

NX = 4
MAIN = 16
CAP = 18
WIDE = 512
BACK = 256


def iota(shape, axis):
    return lax.broadcasted_iota(I32, shape, axis)


def flag(mask):
    return jnp.where(mask, 1.0, 0.0).astype(BF16)


def dot(a, b):
    return lax.dot_general(a, b, (((1,), (0,)), ((), ())), preferred_element_type=F32)


def dot_nt(a, b):
    return lax.dot_general(a, b, (((1,), (1,)), ((), ())), preferred_element_type=F32)


def dot_tn(a, b):
    return lax.dot_general(a, b, (((0,), (0,)), ((), ())), preferred_element_type=F32)


def kernel(
    ny,
    nz,
    x_ref,
    u_ref,
    prob_ref,
    ids_ref,
    wg_hbm,
    wu_hbm,
    wd_hbm,
    out_ref,
    gp_ref,
    tt,
    snd,
    rcv,
    place,
    hits,
    pick,
    pick2,
    ag,
    wgu,
    wdraw,
    wdt,
    acc_gu,
    acc_b,
    dgu,
    rs_snd,
    rs_rcv,
    scores,
    ret_snd,
    ret_rcv,
    load_sem,
    swap_send,
    swap_recv,
    fwd_send,
    fwd_recv,
    ag_send,
    ag_recv,
    rs_send,
    rs_recv,
    sc_send,
    sc_recv,
    ret_send,
    ret_recv,
):
    feats, toks = x_ref.shape
    top = ids_ref.shape[0]
    hid = wd_hbm.shape[0]
    wide_d = wd_hbm.shape[1]
    ngroup = ny * NX
    nslot = ngroup // 2
    nb = nslot // 2
    main = nb * MAIN
    rows = nb * CAP
    chunk = 2 * feats
    pad = WIDE - chunk

    g = lax.axis_index("group")
    d = lax.axis_index("dev")
    y, x = lax.div(g, NX), lax.rem(g, NX)
    z, c = lax.div(d, 2), lax.rem(d, 2)
    sib = {"group": g, "dev": z * 2 + 1 - c}

    def target(n):
        p, dx = lax.div(n, NX), lax.rem(n, NX)
        e = lax.rem(y + p + ny - 1, ny) * NX + lax.rem(x + dx, NX)
        return p, dx, e

    def home_of(s):
        p, dx = lax.div(s, 2), 2 * lax.rem(s, 2) + c
        h = lax.rem(y + ny + ny - (p + ny - 1), ny) * NX + lax.rem(x + NX - dx, NX)
        return p, dx, h

    barrier = pltpu.get_barrier_semaphore()

    def greet(n, carry):
        p, dx, e = target(n)
        own = jnp.logical_and(n == NX, c == 0)

        @pl.when(jnp.logical_not(own))
        def _():
            pl.semaphore_signal(
                barrier, inc=1, device_id={"group": e, "dev": z * 2 + lax.rem(dx, 2)}, device_id_type=MESH
            )

        @pl.when(lax.rem(dx, 2) == c)
        def _():
            pl.semaphore_signal(barrier, inc=1, device_id={"group": e, "dev": z * 2 + 1 - c}, device_id_type=MESH)

        return carry

    lax.fori_loop(0, ngroup, greet, 0)

    def greet_z(k, carry):
        pl.semaphore_signal(
            barrier, inc=1, device_id={"group": g, "dev": lax.rem(z + k, nz) * 2 + c}, device_id_type=MESH
        )
        return carry

    lax.fori_loop(1, nz, greet_z, 0)
    greeted = ngroup + nslot + nz - 1 - (1 - c)

    loads = [
        pltpu.make_async_copy(wd_hbm, wdraw, load_sem.at[0]),
        pltpu.make_async_copy(wg_hbm, wgu.at[pl.ds(0, wide_d), pl.ds(0, hid)], load_sem.at[1]),
        pltpu.make_async_copy(wu_hbm, wgu.at[pl.ds(0, wide_d), pl.ds(2 * hid, hid)], load_sem.at[2]),
    ]
    for copy in loads:
        copy.start()

    zero = jnp.zeros((pad, toks), BF16)
    tt[0, pl.ds(0, feats), :] = x_ref[...]
    tt[0, pl.ds(feats, feats), :] = u_ref[...]
    tt[0, pl.ds(chunk, pad), :] = zero
    tt[1, pl.ds(0, pad), :] = zero
    tt[1, pl.ds(pad, feats), :] = x_ref[...]
    tt[1, pl.ds(pad + feats, feats), :] = u_ref[...]

    n_col = iota((ngroup, 1), 0)
    p_col = lax.shift_right_logical(n_col, 2)
    dx_col = jnp.bitwise_and(n_col, NX - 1)
    e_col = jnp.bitwise_and(y + p_col + ny - 1, ny - 1) * NX + jnp.bitwise_and(x + dx_col, NX - 1)
    ids = ids_ref[...]
    probs = prob_ref[...]
    hit = jnp.zeros((ngroup, toks), F32)
    prob_n = jnp.zeros((ngroup, toks), F32)
    for k in range(top):
        same = jnp.broadcast_to(ids[k : k + 1, :], (ngroup, toks)) == jnp.broadcast_to(e_col, (ngroup, toks))
        hit = hit + jnp.where(same, 1.0, 0.0)
        prob_n = prob_n + jnp.where(same, jnp.broadcast_to(probs[k : k + 1, :], (ngroup, toks)), 0.0)
    earlier = flag(iota((toks, toks), 0) < iota((toks, toks), 1))
    place_n = jnp.where(hit > 0.5, dot(hit.astype(BF16), earlier), -1.0)
    hits[...] = place_n
    place_bf = place_n.astype(BF16)
    part1 = prob_n.astype(BF16)
    rest = prob_n - part1.astype(F32)
    part2 = rest.astype(BF16)
    part3 = (rest - part2.astype(F32)).astype(BF16)

    step_rows = min(8, ngroup) * MAIN

    def fill(i, carry):
        base = pl.multiple_of(i * step_rows, step_rows)
        row = iota((step_rows, 1), 0)
        rr = jnp.bitwise_and(row, MAIN - 1)
        spread = flag(lax.shift_right_logical(base + iota((step_rows, ngroup), 0), 4) == iota((step_rows, ngroup), 1))
        at = dot(spread, place_bf)
        pr = dot(spread, part1) + dot(spread, part2) + dot(spread, part3)
        m1 = at == jnp.broadcast_to(rr.astype(F32), at.shape)
        m2 = at == jnp.broadcast_to((MAIN + jnp.bitwise_and(rr, 1)).astype(F32), at.shape)
        pick1 = flag(m1)
        pickx = flag(m2)
        pick[pl.ds(base, step_rows), :] = pick1
        pick2[pl.ds(base, step_rows), :] = pickx
        pr1 = jnp.sum(jnp.where(m1, pr, 0.0), axis=1, keepdims=True)
        pr2 = jnp.sum(jnp.where(m2, pr, 0.0), axis=1, keepdims=True)
        got = dot_nt(pick1, tt[0])
        lane = iota((step_rows, WIDE), 1)
        got = jnp.where(jnp.logical_and(lane >= feats, lane < chunk), got * pr1, got)
        odd = dot_nt(pickx, tt[0])
        even = dot_nt(pickx, tt[1])
        part = lax.shift_right_logical(rr, 1)
        extra = jnp.zeros((step_rows, 128), F32)
        for tile in range(WIDE // 128):
            cut = slice(tile * 128, tile * 128 + 128)
            extra = jnp.where(part == 2 * tile, even[:, cut], extra)
            extra = jnp.where(part == 2 * tile + 1, odd[:, cut], extra)
        lane = iota((step_rows, 128), 1)
        extra = jnp.where(part * pad + lane - (128 - pad) >= feats, extra * pr2, extra)
        snd[pl.ds(base, step_rows), pl.ds(0, WIDE - 128)] = got[:, : WIDE - 128].astype(BF16)
        snd[pl.ds(base, step_rows), pl.ds(WIDE - 128, 128)] = jnp.where(
            lane >= 128 - pad, extra, got[:, WIDE - 128 :]
        ).astype(BF16)
        return carry

    lax.fori_loop(0, ngroup * MAIN // step_rows, fill, 0)

    pl.semaphore_wait(barrier, greeted)

    def fwd_copy(n, b, sem):
        p, dx, e = target(n)
        slot = p * 2 + lax.div(dx, 2) - b * nb
        return pltpu.make_async_remote_copy(
            src_ref=snd.at[pl.ds(pl.multiple_of(n * MAIN, MAIN), MAIN), :],
            dst_ref=rcv.at[b, c, pl.ds(pl.multiple_of(slot * MAIN, MAIN), MAIN), :],
            send_sem=sem,
            recv_sem=fwd_recv.at[b],
            device_id={"group": e, "dev": z * 2 + lax.rem(dx, 2)},
            device_id_type=MESH,
        )

    own_b, own_slot = (0, NX // 2) if ny > 2 else (1, 0)

    for b in range(2):

        def send_rows(n, carry, b=b):
            @pl.when(n != NX)
            def _():
                fwd_copy(n, b, fwd_send.at[0]).start()

            return carry

        lax.fori_loop(b * nslot, (b + 1) * nslot, send_rows, 0)
        if b == own_b:

            @pl.when(c == 0)
            def _():
                pltpu.make_async_copy(
                    snd.at[pl.ds(NX * MAIN, MAIN), :],
                    rcv.at[own_b, 0, pl.ds(own_slot * MAIN, MAIN), :],
                    fwd_recv.at[own_b],
                ).start()

            @pl.when(c == 1)
            def _():
                fwd_copy(NX, own_b, fwd_send.at[1]).start()

    swaps = [
        pltpu.make_async_remote_copy(
            src_ref=wg_hbm,
            dst_ref=wgu.at[pl.ds(0, wide_d), pl.ds(hid, hid)],
            send_sem=swap_send.at[0],
            recv_sem=swap_recv.at[0],
            device_id=sib,
            device_id_type=MESH,
        ),
        pltpu.make_async_remote_copy(
            src_ref=wu_hbm,
            dst_ref=wgu.at[pl.ds(0, wide_d), pl.ds(3 * hid, hid)],
            send_sem=swap_send.at[1],
            recv_sem=swap_recv.at[1],
            device_id=sib,
            device_id_type=MESH,
        ),
        pltpu.make_async_remote_copy(
            src_ref=wdt.at[pl.ds(pad, wide_d), pl.ds(0, hid)],
            dst_ref=wdt.at[pl.ds(pad, wide_d), pl.ds(hid, hid)],
            send_sem=swap_send.at[2],
            recv_sem=swap_recv.at[2],
            device_id=sib,
            device_id_type=MESH,
        ),
    ]
    swaps[0].start()
    swaps[1].start()

    loads[0].wait()

    def turn(i, carry):
        base = pl.multiple_of(i * 128, 128)
        wdt[pl.ds(pl.multiple_of(base + pad, pad), 128), pl.ds(0, hid)] = wdraw[:, pl.ds(base, 128)].T
        return carry

    lax.fori_loop(0, wide_d // 128, turn, 0)
    swaps[2].start()

    wgu[pl.ds(wide_d, pad), :] = jnp.zeros((pad, 4 * hid), BF16)
    wdt[pl.ds(0, pad), :] = jnp.zeros((pad, 2 * hid), BF16)
    acc_gu[...] = jnp.zeros_like(acc_gu)
    acc_b[...] = jnp.zeros_like(acc_b)

    def set_place(i, carry):
        base = pl.multiple_of(i * 128, 128)
        a = base + iota((128, 2 * chunk), 0)
        f = iota((128, 2 * chunk), 1)
        goal = a + jnp.where(a >= feats, feats, 0)
        keep = a < chunk
        place[0, pl.ds(base, 128), :] = flag(jnp.logical_and(keep, f == goal))
        place[1, pl.ds(base, 128), :] = flag(jnp.logical_and(keep, f == goal + feats))
        return carry

    lax.fori_loop(0, WIDE // 128, set_place, 0)

    def build(b):
        pltpu.make_async_copy(rcv.at[b], rcv.at[b], fwd_recv.at[b]).wait()
        widen = flag(iota((128, WIDE), 0) == 128 - pad + jnp.bitwise_and(iota((128, WIDE), 1), pad - 1))
        mine = lax.shift_right_logical(jnp.bitwise_and(iota((main, WIDE), 0), MAIN - 1), 1) == lax.shift_right_logical(
            iota((main, WIDE), 1), pad.bit_length() - 1
        )
        a, r = iota((2 * nb, main), 0), iota((2 * nb, main), 1)
        gather = flag(
            jnp.logical_and(
                lax.shift_right_logical(a, 1) == lax.shift_right_logical(r, 4),
                jnp.bitwise_and(a, 1) == jnp.bitwise_and(r, 1),
            )
        )
        whole, extra = 0.0, 0.0
        for h in range(2):
            got = rcv[b, h]
            wide = jnp.where(mine, dot(got[:, WIDE - 128 :], widen), 0.0).astype(BF16)
            last = dot(gather, wide).astype(BF16)
            whole = whole + dot(got, place[h])
            extra = extra + dot(last, place[h])
        ag[b, z, pl.ds(0, main), :] = whole.astype(BF16)
        ag[b, z, pl.ds(main, 2 * nb), :] = extra.astype(BF16)

    right = {"group": g, "dev": lax.rem(z + 1, nz) * 2 + c}
    left = {"group": g, "dev": lax.rem(z + nz - 1, nz) * 2 + c}
    half = nz // 2
    hops = [[half, nz - 1 - half], [nz - 1 - half, half]]

    def ag_copy(b, way, s):
        which = lax.rem(z + nz - s, nz) if way == 0 else lax.rem(z + s, nz)
        return pltpu.make_async_remote_copy(
            src_ref=ag.at[b, which],
            dst_ref=ag.at[b, which],
            send_sem=ag_send.at[b, way, s],
            recv_sem=ag_recv.at[b, way, s],
            device_id=right if way == 0 else left,
            device_id_type=MESH,
        )

    def multiply(b, which):
        lane = iota((rows, 128), 1)
        mid = ag[b, which, :, pl.ds(WIDE - 128, 128)]
        none = jnp.zeros_like(mid)
        first = jnp.concatenate(
            [ag[b, which, :, pl.ds(0, WIDE - 128)], jnp.where(lane < 128 - pad, mid, none)], axis=1
        )
        second = jnp.concatenate(
            [jnp.where(lane >= 128 - pad, mid, none), ag[b, which, :, pl.ds(WIDE, WIDE - 128)]], axis=1
        )
        at = pl.ds(pl.multiple_of(which * chunk, pad), WIDE)
        acc_gu[b] += dot(first, wgu[at, :])
        acc_b[b] += dot(second, wdt[at, :])

    for b in range(2):
        build(b)
        for way in range(2):
            if hops[b][way] > 0:
                ag_copy(b, way, 0).start()

    loads[1].wait()
    loads[2].wait()
    for copy in swaps:
        copy.wait_recv()

    def arrive(b, s):
        for way in range(2):
            if s < hops[b][way]:
                ag_copy(b, way, s).wait_recv()
                if s + 1 < hops[b][way]:
                    ag_copy(b, way, s + 1).start()
        for way in range(2):
            if s < hops[b][way]:
                multiply(b, lax.rem(z + nz - s - 1, nz) if way == 0 else lax.rem(z + s + 1, nz))

    for b in range(2):
        multiply(b, z)
    for s in range(half):
        for b in range(2):
            arrive(b, s)
            if s == half - 1:
                finish = functools.partial(middle, b, hid, acc_gu, acc_b, dgu)
                row = finish()
                if b == 0:
                    scores[z] = jnp.zeros(scores.shape[1:], F32)
                    scores[z, pl.ds(0, 4), pl.ds(0, rows)] = row[0:4]
                else:
                    scores[z, pl.ds(4, 4), pl.ds(0, rows)] = row[4:8]
                rs_step(b, 0, z, nz, hops, rows, chunk, pad, dgu, wgu, rs_snd, rs_rcv, rs_send, rs_recv, right, left)

    def sc_copy(k):
        return pltpu.make_async_remote_copy(
            src_ref=scores.at[z],
            dst_ref=scores.at[z],
            send_sem=sc_send.at[k],
            recv_sem=sc_recv.at[k],
            device_id={"group": g, "dev": lax.rem(z + k, nz) * 2 + c},
            device_id_type=MESH,
        )

    for k in range(1, nz):
        sc_copy(k).start()

    for s in range(1, half):
        for b in range(2):
            rs_step(b, s, z, nz, hops, rows, chunk, pad, dgu, wgu, rs_snd, rs_rcv, rs_send, rs_recv, right, left)

    for k in range(1, nz):
        sc_copy(k).wait_recv()
    score = scores[0]
    for k in range(1, nz):
        score = score + scores[k]

    def ret_copy(b, i, h, sem):
        p, dx, home = home_of(b * nb + i)
        n = p * NX + dx
        return pltpu.make_async_remote_copy(
            src_ref=ret_snd.at[b, h, pl.ds(pl.multiple_of(i * MAIN, MAIN), MAIN), :],
            dst_ref=ret_rcv.at[pl.ds(pl.multiple_of(n * MAIN, MAIN), MAIN), :],
            send_sem=sem,
            recv_sem=ret_recv.at[b],
            device_id={"group": home, "dev": z * 2 + h},
            device_id_type=MESH,
        )

    for b in range(2):
        total = dot_nt(dgu[b], wgu[pl.ds(pl.multiple_of(z * chunk, pad), WIDE), :])
        for way in range(2):
            if hops[b][way] > 0:
                s = hops[b][way] - 1
                rs_copy(b, way, s, z, nz, hops, rs_snd, rs_rcv, rs_send, rs_recv, right, left).wait_recv()
                total = total + rs_rcv[b, way, s].astype(F32)
        total = total.astype(BF16)
        whole, extra = total[:main], total[main:]

        row = iota((main, BACK), 0)
        lane = iota((main, BACK), 1)
        q = jnp.bitwise_and(row, MAIN - 1)
        value = jnp.broadcast_to(score[4 * b : 4 * b + 1, :], (main, BACK))
        upper = value.astype(BF16).astype(F32)
        lower = value - upper
        slot = jnp.where(lane < main, lax.shift_right_logical(lane, 4), lax.shift_right_logical(lane - main, 1))
        fits = jnp.logical_and(lax.shift_right_logical(row, 4) == slot, lane < rows)
        value = jnp.where(q == MAIN - 2, upper, jnp.where(q == MAIN - 1, lower, 0.0))
        value = jnp.where(fits, value, 0.0).astype(BF16)
        a, l = iota((BACK, BACK), 0), iota((BACK, BACK), 1)
        number = jnp.where(a < main, jnp.bitwise_and(a, MAIN - 1), MAIN + jnp.bitwise_and(a, 1))
        carried = dot(value, flag(l == feats + number))

        again = flag(
            jnp.logical_and(
                lax.shift_right_logical(iota((main, 2 * nb), 0), 4)
                == lax.shift_right_logical(iota((main, 2 * nb), 1), 1),
                jnp.bitwise_and(iota((main, 2 * nb), 0), 1) == jnp.bitwise_and(iota((main, 2 * nb), 1), 1),
            )
        )
        extra = dot(again, extra)
        room = BACK - feats
        for h in range(2):
            a, l = iota((WIDE, BACK), 0), iota((WIDE, BACK), 1)
            shift = flag(jnp.logical_and(a == l + feats * h, l < feats))
            rel = a - feats * h
            inside = jnp.logical_and(rel >= 0, rel < feats)
            tail = flag(jnp.logical_and(inside, jnp.bitwise_and(a, room - 1) == l - feats))
            lane = iota((main, WIDE), 1) - feats * h
            rr = lax.shift_right_logical(jnp.bitwise_and(iota((main, WIDE), 0), MAIN - 1), 1)
            mine = jnp.logical_and(lane >= rr * room, lane < rr * room + room)
            ends = jnp.where(jnp.logical_and(mine, lane < feats), extra, 0.0).astype(BF16)
            ret_snd[b, h] = (dot(whole, shift) + dot(ends, tail) + carried).astype(BF16)

        def send_back(i, carry, b=b):
            for h in range(2):
                own = jnp.logical_and(c == 0, i == own_slot) if (b == own_b and h == 0) else None
                if own is None:
                    ret_copy(b, i, h, ret_send.at[0]).start()
                else:

                    @pl.when(jnp.logical_not(own))
                    def _():
                        ret_copy(b, i, h, ret_send.at[0]).start()

            return carry

        lax.fori_loop(0, nb, send_back, 0)
        if b == own_b:

            @pl.when(c == 0)
            def _():
                pltpu.make_async_copy(
                    ret_snd.at[own_b, 0, pl.ds(own_slot * MAIN, MAIN), :],
                    ret_rcv.at[pl.ds(NX * MAIN, MAIN), :],
                    ret_recv.at[own_b],
                ).start()

    room = BACK - feats
    n_rows = nslot * MAIN
    total = 0.0
    sums = []
    for b in range(2):
        part = pl.ds(b * n_rows, n_rows)
        pltpu.make_async_copy(ret_rcv.at[part], ret_rcv.at[part], ret_recv.at[b]).wait()
        got = ret_rcv[part, :]
        end = got[:, BACK - 128 :]
        widen = flag(iota((128, BACK), 0) == 128 - room + jnp.bitwise_and(iota((128, BACK), 1), room - 1))
        mine = lax.shift_right_logical(
            jnp.bitwise_and(iota((n_rows, BACK), 0), MAIN - 1), 1
        ) == lax.shift_right_logical(iota((n_rows, BACK), 1), room.bit_length() - 1)
        wide = jnp.where(mine, dot(end, widen), 0.0).astype(BF16)
        total = total + dot_tn(got, pick[part, :]) + dot_tn(wide, pick2[part, :])
        a, r = iota((nslot, n_rows), 0), iota((nslot, n_rows), 1)
        this = a == lax.shift_right_logical(r, 4)
        r = jnp.bitwise_and(r, MAIN - 1)
        sums.append(
            dot(flag(jnp.logical_and(this, r == MAIN - 2)), end)
            + dot(flag(jnp.logical_and(this, r == MAIN - 1)), end)
        )
    out_ref[...] = total[:feats].astype(BF16)

    at = hits[...]
    score = jnp.concatenate(sums, axis=0)
    found = jnp.zeros((ngroup, toks), F32)
    for q in range(CAP):
        col = 128 - room + q
        found = jnp.where(at == float(q), jnp.broadcast_to(score[:, col : col + 1], found.shape), found)
    ids = ids_ref[...]
    for k in range(top):
        same = jnp.broadcast_to(ids[k : k + 1, :], (ngroup, toks)) == jnp.broadcast_to(e_col, (ngroup, toks))
        value = jnp.sum(jnp.where(same, found, 0.0), axis=0, keepdims=True)
        gp_ref[pl.ds(k, 1), :] = value / prob_ref[pl.ds(k, 1), :]

    most = 2 * nslot - 1
    part = snd.at[pl.ds(0, most * MAIN), :]
    pltpu.make_async_copy(part, part, fwd_send.at[0]).wait()
    for copy in swaps:
        copy.wait_send()
    for b in range(2):
        for way in range(2):
            for s in range(hops[b][way]):
                ag_copy(b, way, s).wait_send()
                rs_copy(b, way, s, z, nz, hops, rs_snd, rs_rcv, rs_send, rs_recv, right, left).wait_send()
    for k in range(1, nz):
        sc_copy(k).wait_send()
    part = ret_rcv.at[pl.ds(0, most * MAIN), :]
    pltpu.make_async_copy(part, part, ret_send.at[0]).wait()

    @pl.when(c == 1)
    def _():
        one = snd.at[pl.ds(0, MAIN), :]
        pltpu.make_async_copy(one, one, fwd_send.at[1]).wait()
        one = ret_rcv.at[pl.ds(0, MAIN), :]
        pltpu.make_async_copy(one, one, ret_send.at[0]).wait()


def middle(b, hid, acc_gu, acc_b, dgu):
    gate, upper = acc_gu[b, :, pl.ds(0, 2 * hid)], acc_gu[b, :, pl.ds(2 * hid, 2 * hid)]
    back = acc_b[b]
    sig = 1.0 / (1.0 + jnp.exp(-gate))
    act = gate * sig
    slope = sig * (1.0 + gate * (1.0 - sig))
    dgu[b, :, pl.ds(0, 2 * hid)] = (back * upper * slope).astype(BF16)
    dgu[b, :, pl.ds(2 * hid, 2 * hid)] = (back * act).astype(BF16)
    prod = act * upper * back
    return lax.dot_general(
        jnp.ones((8, 2 * hid), F32),
        prod,
        (((1,), (1,)), ((), ())),
        preferred_element_type=F32,
        precision=lax.Precision.HIGHEST,
    )


def rs_copy(b, way, s, z, nz, hops, rs_snd, rs_rcv, rs_send, rs_recv, right, left):
    return pltpu.make_async_remote_copy(
        src_ref=rs_snd.at[b, way, s],
        dst_ref=rs_rcv.at[b, way, s],
        send_sem=rs_send.at[b, way, s],
        recv_sem=rs_recv.at[b, way, s],
        device_id=right if way == 0 else left,
        device_id_type=MESH,
    )


def rs_step(b, s, z, nz, hops, rows, chunk, pad, dgu, wgu, rs_snd, rs_rcv, rs_send, rs_recv, right, left):
    for way in range(2):
        if s < hops[b][way]:
            left_over = hops[b][way] - s
            which = lax.rem(z + left_over, nz) if way == 0 else lax.rem(z + nz - left_over, nz)
            total = dot_nt(dgu[b], wgu[pl.ds(pl.multiple_of(which * chunk, pad), WIDE), :])
            if s > 0:
                rs_copy(b, way, s - 1, z, nz, hops, rs_snd, rs_rcv, rs_send, rs_recv, right, left).wait_recv()
                total = total + rs_rcv[b, way, s - 1].astype(F32)
            rs_snd[b, way, s] = total.astype(BF16)
            rs_copy(b, way, s, z, nz, hops, rs_snd, rs_rcv, rs_send, rs_recv, right, left).start()


def on_device(ny, nz, tokens, upstream, route_probs, expert_ids, w_gate, w_up, w_down):
    toks, feats = tokens.shape
    top = expert_ids.shape[1]
    wide_d, hid = w_gate.shape[1], w_gate.shape[2]
    ngroup = ny * NX
    nslot = ngroup // 2
    nb = nslot // 2
    main, rows = nb * MAIN, nb * CAP
    chunk = 2 * feats
    pad = WIDE - chunk
    half = nz // 2
    dma = pltpu.SemaphoreType.DMA
    vmem = pl.BlockSpec(memory_space=pltpu.VMEM)
    hbm = pl.BlockSpec(memory_space=pl.ANY)
    out, gp = pl.pallas_call(
        functools.partial(kernel, ny, nz),
        out_shape=(jax.ShapeDtypeStruct((feats, toks), BF16), jax.ShapeDtypeStruct((top, toks), F32)),
        in_specs=[vmem] * 4 + [hbm] * 3,
        out_specs=(vmem, vmem),
        scratch_shapes=[
            pltpu.VMEM((2, WIDE, toks), BF16),
            pltpu.VMEM((ngroup * MAIN, WIDE), BF16),
            pltpu.VMEM((2, 2, main, WIDE), BF16),
            pltpu.VMEM((2, WIDE, 2 * chunk), BF16),
            pltpu.VMEM((ngroup, toks), F32),
            pltpu.VMEM((ngroup * MAIN, toks), BF16),
            pltpu.VMEM((ngroup * MAIN, toks), BF16),
            pltpu.VMEM((2, nz, rows, 2 * chunk), BF16),
            pltpu.VMEM((wide_d + pad, 4 * hid), BF16),
            pltpu.VMEM((hid, wide_d), BF16),
            pltpu.VMEM((wide_d + pad, 2 * hid), BF16),
            pltpu.VMEM((2, rows, 4 * hid), F32),
            pltpu.VMEM((2, rows, 2 * hid), F32),
            pltpu.VMEM((2, rows, 4 * hid), BF16),
            pltpu.VMEM((2, 2, half, rows, WIDE), BF16),
            pltpu.VMEM((2, 2, half, rows, WIDE), BF16),
            pltpu.VMEM((nz, 8, BACK), F32),
            pltpu.VMEM((2, 2, main, BACK), BF16),
            pltpu.VMEM((ngroup * MAIN, BACK), BF16),
            dma((3,)),
            dma((3,)),
            dma((3,)),
            dma((2,)),
            dma((2,)),
            dma((2, 2, half)),
            dma((2, 2, half)),
            dma((2, 2, half)),
            dma((2, 2, half)),
            dma((nz,)),
            dma((nz,)),
            dma((1,)),
            dma((2,)),
        ],
        compiler_params=pltpu.CompilerParams(
            collective_id=0, has_side_effects=True, vmem_limit_bytes=48 * 1024 * 1024
        ),
    )(tokens.T, upstream.T, route_probs.T, expert_ids.T, w_gate[0], w_up[0], w_down[0])
    return out.T, gp.T


def solution(mesh):
    ny = mesh.shape["group"] // NX
    nz = mesh.shape["dev"] // 2
    placed = (
        P("group", "dev"),
        P("group", "dev"),
        P("group", None),
        P("group", None),
        P("group", None, "dev"),
        P("group", None, "dev"),
        P("group", "dev", None),
    )
    return jax.shard_map(
        functools.partial(on_device, ny, nz),
        mesh=mesh,
        in_specs=placed,
        out_specs=(P("group", "dev"), P("group", None)),
        check_vma=False,
    )
```

```python
import functools

import jax
import jax.numpy as jnp
from jax import lax
from jax.experimental import pallas as pl
from jax.experimental.pallas import tpu as pltpu
from jax.sharding import PartitionSpec as P

BF16 = jnp.bfloat16
F32 = jnp.float32
I32 = jnp.int32
MESH = pl.DeviceIdType.MESH

NX = 4
MAIN = 16
CAP = 18
WIDE = 512
BACK = 256


def iota(shape, axis):
    return lax.broadcasted_iota(I32, shape, axis)


def flag(mask):
    return jnp.where(mask, 1.0, 0.0).astype(BF16)


def dot(a, b):
    return lax.dot_general(a, b, (((1,), (0,)), ((), ())), preferred_element_type=F32)


def dot_nt(a, b):
    return lax.dot_general(a, b, (((1,), (1,)), ((), ())), preferred_element_type=F32)


def dot_tn(a, b):
    return lax.dot_general(a, b, (((0,), (0,)), ((), ())), preferred_element_type=F32)


def kernel(
    ny,
    nz,
    x_hbm,
    u_hbm,
    prob_hbm,
    ids_hbm,
    wg_hbm,
    wu_hbm,
    wd_hbm,
    out_ref,
    gp_ref,
    ids_ref,
    prob_ref,
    tt,
    snd,
    rcv,
    place,
    away,
    hits,
    pick,
    pick2,
    ag,
    wgu,
    wdraw,
    wdt,
    acc_gu,
    acc_b,
    dgu,
    rs_snd,
    rs_rcv,
    scores,
    ret_snd,
    ret_rcv,
    load_sem,
    swap_send,
    swap_recv,
    fwd_send,
    fwd_recv,
    ag_send,
    ag_recv,
    rs_send,
    rs_recv,
    sc_send,
    sc_recv,
    ret_send,
    ret_recv,
):
    feats, toks = x_hbm.shape
    top = ids_hbm.shape[0]
    hid = wd_hbm.shape[0]
    wide_d = wd_hbm.shape[1]
    ngroup = ny * NX
    nslot = ngroup // 2
    nb = nslot // 2
    main = nb * MAIN
    rows = nb * CAP
    chunk = 2 * feats
    pad = WIDE - chunk

    g = lax.axis_index("group")
    d = lax.axis_index("dev")
    y, x = lax.div(g, NX), lax.rem(g, NX)
    z, c = lax.div(d, 2), lax.rem(d, 2)
    sib = {"group": g, "dev": z * 2 + 1 - c}

    def target(n):
        p, dx = lax.div(n, NX), lax.rem(n, NX)
        e = lax.rem(y + p + ny - 1, ny) * NX + lax.rem(x + dx, NX)
        return p, dx, e

    def home_of(s):
        p, dx = lax.div(s, 2), 2 * lax.rem(s, 2) + c
        h = lax.rem(y + ny + ny - (p + ny - 1), ny) * NX + lax.rem(x + NX - dx, NX)
        return p, dx, h

    loads = [
        pltpu.make_async_copy(ids_hbm, ids_ref, load_sem.at[0]),
        pltpu.make_async_copy(prob_hbm, prob_ref, load_sem.at[1]),
        pltpu.make_async_copy(x_hbm, tt.at[0, pl.ds(0, feats), :], load_sem.at[2]),
        pltpu.make_async_copy(u_hbm, tt.at[0, pl.ds(feats, feats), :], load_sem.at[3]),
        pltpu.make_async_copy(x_hbm, tt.at[1, pl.ds(pad, feats), :], load_sem.at[4]),
        pltpu.make_async_copy(u_hbm, tt.at[1, pl.ds(pad + feats, feats), :], load_sem.at[5]),
        pltpu.make_async_copy(wd_hbm, wdraw, load_sem.at[6]),
        pltpu.make_async_copy(wg_hbm, wgu.at[pl.ds(0, wide_d), pl.ds(0, hid)], load_sem.at[7]),
        pltpu.make_async_copy(wu_hbm, wgu.at[pl.ds(0, wide_d), pl.ds(2 * hid, hid)], load_sem.at[8]),
    ]
    for copy in loads:
        copy.start()

    barrier = pltpu.get_barrier_semaphore()

    def greet(n, carry):
        p, dx, e = target(n)
        own = jnp.logical_and(n == NX, c == 0)

        @pl.when(jnp.logical_not(own))
        def _():
            pl.semaphore_signal(
                barrier, inc=1, device_id={"group": e, "dev": z * 2 + lax.rem(dx, 2)}, device_id_type=MESH
            )

        @pl.when(lax.rem(dx, 2) == c)
        def _():
            pl.semaphore_signal(barrier, inc=1, device_id={"group": e, "dev": z * 2 + 1 - c}, device_id_type=MESH)

        return carry

    lax.fori_loop(0, ngroup, greet, 0)

    def greet_z(k, carry):
        pl.semaphore_signal(
            barrier, inc=1, device_id={"group": g, "dev": lax.rem(z + k, nz) * 2 + c}, device_id_type=MESH
        )
        return carry

    lax.fori_loop(1, nz, greet_z, 0)
    greeted = ngroup + nslot + nz - 1 - (1 - c)

    zero = jnp.zeros((pad, toks), BF16)
    tt[0, pl.ds(chunk, pad), :] = zero
    tt[1, pl.ds(0, pad), :] = zero

    n_col = iota((ngroup, 1), 0)
    p_col = lax.shift_right_logical(n_col, 2)
    dx_col = jnp.bitwise_and(n_col, NX - 1)
    e_col = jnp.bitwise_and(y + p_col + ny - 1, ny - 1) * NX + jnp.bitwise_and(x + dx_col, NX - 1)
    loads[0].wait()
    loads[1].wait()
    ids = ids_ref[...]
    probs = prob_ref[...]
    hit = jnp.zeros((ngroup, toks), F32)
    prob_n = jnp.zeros((ngroup, toks), F32)
    for k in range(top):
        same = jnp.broadcast_to(ids[k : k + 1, :], (ngroup, toks)) == jnp.broadcast_to(e_col, (ngroup, toks))
        hit = hit + jnp.where(same, 1.0, 0.0)
        prob_n = prob_n + jnp.where(same, jnp.broadcast_to(probs[k : k + 1, :], (ngroup, toks)), 0.0)
    earlier = flag(iota((toks, toks), 0) < iota((toks, toks), 1))
    place_n = jnp.where(hit > 0.5, dot(hit.astype(BF16), earlier), -1.0)
    hits[...] = place_n
    place_bf = place_n.astype(BF16)
    part1 = prob_n.astype(BF16)
    rest = prob_n - part1.astype(F32)
    part2 = rest.astype(BF16)
    part3 = (rest - part2.astype(F32)).astype(BF16)

    step_rows = min(8, ngroup // 2) * MAIN

    def fill(i, carry):
        base = pl.multiple_of(i * step_rows, step_rows)
        row = iota((step_rows, 1), 0)
        rr = jnp.bitwise_and(row, MAIN - 1)
        spread = flag(lax.shift_right_logical(base + iota((step_rows, ngroup), 0), 4) == iota((step_rows, ngroup), 1))
        at = dot(spread, place_bf)
        pr = dot(spread, part1) + dot(spread, part2) + dot(spread, part3)
        m1 = at == jnp.broadcast_to(rr.astype(F32), at.shape)
        m2 = at == jnp.broadcast_to((MAIN + jnp.bitwise_and(rr, 1)).astype(F32), at.shape)
        pick1 = flag(m1)
        pickx = flag(m2)
        pick[pl.ds(base, step_rows), :] = pick1
        pick2[pl.ds(base, step_rows), :] = pickx
        pr1 = jnp.sum(jnp.where(m1, pr, 0.0), axis=1, keepdims=True)
        pr2 = jnp.sum(jnp.where(m2, pr, 0.0), axis=1, keepdims=True)
        got = dot_nt(pick1, tt[0])
        lane = iota((step_rows, WIDE), 1)
        got = jnp.where(jnp.logical_and(lane >= feats, lane < chunk), got * pr1, got)
        odd = dot_nt(pickx, tt[0])
        even = dot_nt(pickx, tt[1])
        part = lax.shift_right_logical(rr, 1)
        extra = jnp.zeros((step_rows, 128), F32)
        for tile in range(WIDE // 128):
            cut = slice(tile * 128, tile * 128 + 128)
            extra = jnp.where(part == 2 * tile, even[:, cut], extra)
            extra = jnp.where(part == 2 * tile + 1, odd[:, cut], extra)
        lane = iota((step_rows, 128), 1)
        extra = jnp.where(part * pad + lane - (128 - pad) >= feats, extra * pr2, extra)
        snd[pl.ds(base, step_rows), pl.ds(0, WIDE - 128)] = got[:, : WIDE - 128].astype(BF16)
        snd[pl.ds(base, step_rows), pl.ds(WIDE - 128, 128)] = jnp.where(
            lane >= 128 - pad, extra, got[:, WIDE - 128 :]
        ).astype(BF16)
        return carry

    for copy in loads[2:6]:
        copy.wait()
    steps = ngroup * MAIN // step_rows
    lax.fori_loop(0, steps // 2, fill, 0)
    pl.semaphore_wait(barrier, greeted)

    def fwd_copy(n, b, sem):
        p, dx, e = target(n)
        slot = p * 2 + lax.div(dx, 2) - b * nb
        return pltpu.make_async_remote_copy(
            src_ref=snd.at[pl.ds(pl.multiple_of(n * MAIN, MAIN), MAIN), :],
            dst_ref=rcv.at[b, c, pl.ds(pl.multiple_of(slot * MAIN, MAIN), MAIN), :],
            send_sem=sem,
            recv_sem=fwd_recv.at[b],
            device_id={"group": e, "dev": z * 2 + lax.rem(dx, 2)},
            device_id_type=MESH,
        )

    own_b, own_slot = (0, NX // 2) if ny > 2 else (1, 0)

    def send_batch(b):
        def send_rows(n, carry):
            @pl.when(n != NX)
            def _():
                fwd_copy(n, b, fwd_send.at[0]).start()

            return carry

        lax.fori_loop(b * nslot, (b + 1) * nslot, send_rows, 0)
        if b == own_b:

            @pl.when(c == 0)
            def _():
                pltpu.make_async_copy(
                    snd.at[pl.ds(NX * MAIN, MAIN), :],
                    rcv.at[own_b, 0, pl.ds(own_slot * MAIN, MAIN), :],
                    fwd_recv.at[own_b],
                ).start()

            @pl.when(c == 1)
            def _():
                fwd_copy(NX, own_b, fwd_send.at[1]).start()

    send_batch(0)
    lax.fori_loop(steps // 2, steps, fill, 0)

    swaps = [
        pltpu.make_async_remote_copy(
            src_ref=wg_hbm,
            dst_ref=wgu.at[pl.ds(0, wide_d), pl.ds(hid, hid)],
            send_sem=swap_send.at[0],
            recv_sem=swap_recv.at[0],
            device_id=sib,
            device_id_type=MESH,
        ),
        pltpu.make_async_remote_copy(
            src_ref=wu_hbm,
            dst_ref=wgu.at[pl.ds(0, wide_d), pl.ds(3 * hid, hid)],
            send_sem=swap_send.at[1],
            recv_sem=swap_recv.at[1],
            device_id=sib,
            device_id_type=MESH,
        ),
        pltpu.make_async_remote_copy(
            src_ref=wdt.at[pl.ds(pad, wide_d), pl.ds(0, hid)],
            dst_ref=wdt.at[pl.ds(pad, wide_d), pl.ds(hid, hid)],
            send_sem=swap_send.at[2],
            recv_sem=swap_recv.at[2],
            device_id=sib,
            device_id_type=MESH,
        ),
    ]
    swaps[0].start()
    swaps[1].start()

    loads[6].wait()

    def turn(i, carry):
        base = pl.multiple_of(i * 128, 128)
        wdt[pl.ds(pl.multiple_of(base + pad, pad), 128), pl.ds(0, hid)] = wdraw[:, pl.ds(base, 128)].T
        return carry

    lax.fori_loop(0, wide_d // 128, turn, 0)
    swaps[2].start()

    wgu[pl.ds(wide_d, pad), :] = jnp.zeros((pad, 4 * hid), BF16)
    wdt[pl.ds(0, pad), :] = jnp.zeros((pad, 2 * hid), BF16)
    acc_gu[...] = jnp.zeros_like(acc_gu)
    acc_b[...] = jnp.zeros_like(acc_b)

    def set_place(i, carry):
        base = pl.multiple_of(i * 128, 128)
        a = base + iota((128, 2 * chunk), 0)
        f = iota((128, 2 * chunk), 1)
        goal = a + jnp.where(a >= feats, feats, 0)
        keep = a < chunk
        place[0, pl.ds(base, 128), :] = flag(jnp.logical_and(keep, f == goal))
        place[1, pl.ds(base, 128), :] = flag(jnp.logical_and(keep, f == goal + feats))
        return carry

    lax.fori_loop(0, WIDE // 128, set_place, 0)

    room = BACK - feats

    def set_away(h, carry):
        a, l = iota((WIDE, BACK), 0) - feats * h, iota((WIDE, BACK), 1)
        away[h, pl.ds(0, WIDE), :] = flag(jnp.logical_and(a == l, l < feats))
        inside = jnp.logical_and(a >= 0, a < feats)
        away[h, pl.ds(WIDE, WIDE), :] = flag(jnp.logical_and(inside, jnp.bitwise_and(a, room - 1) == l - feats))
        return carry

    def build(b):
        pltpu.make_async_copy(rcv.at[b], rcv.at[b], fwd_recv.at[b]).wait()
        widen = flag(iota((128, WIDE), 0) == 128 - pad + jnp.bitwise_and(iota((128, WIDE), 1), pad - 1))
        mine = lax.shift_right_logical(jnp.bitwise_and(iota((main, WIDE), 0), MAIN - 1), 1) == lax.shift_right_logical(
            iota((main, WIDE), 1), pad.bit_length() - 1
        )
        a, r = iota((2 * nb, main), 0), iota((2 * nb, main), 1)
        gather = flag(
            jnp.logical_and(
                lax.shift_right_logical(a, 1) == lax.shift_right_logical(r, 4),
                jnp.bitwise_and(a, 1) == jnp.bitwise_and(r, 1),
            )
        )
        whole, extra = 0.0, 0.0
        for h in range(2):
            got = rcv[b, h]
            wide = jnp.where(mine, dot(got[:, WIDE - 128 :], widen), 0.0).astype(BF16)
            last = dot(gather, wide).astype(BF16)
            whole = whole + dot(got, place[h])
            extra = extra + dot(last, place[h])
        ag[b, z, pl.ds(0, main), :] = whole.astype(BF16)
        ag[b, z, pl.ds(main, 2 * nb), :] = extra.astype(BF16)

    right = {"group": g, "dev": lax.rem(z + 1, nz) * 2 + c}
    left = {"group": g, "dev": lax.rem(z + nz - 1, nz) * 2 + c}
    half = nz // 2
    hops = [[half, nz - 1 - half], [nz - 1 - half, half]]

    def ag_copy(b, way, s):
        which = lax.rem(z + nz - s, nz) if way == 0 else lax.rem(z + s, nz)
        return pltpu.make_async_remote_copy(
            src_ref=ag.at[b, which],
            dst_ref=ag.at[b, which],
            send_sem=ag_send.at[b, way, s],
            recv_sem=ag_recv.at[b, way, s],
            device_id=right if way == 0 else left,
            device_id_type=MESH,
        )

    def multiply(b, which):
        lane = iota((rows, 128), 1)
        mid = ag[b, which, :, pl.ds(WIDE - 128, 128)]
        none = jnp.zeros_like(mid)
        first = jnp.concatenate(
            [ag[b, which, :, pl.ds(0, WIDE - 128)], jnp.where(lane < 128 - pad, mid, none)], axis=1
        )
        second = jnp.concatenate(
            [jnp.where(lane >= 128 - pad, mid, none), ag[b, which, :, pl.ds(WIDE, WIDE - 128)]], axis=1
        )
        at = pl.ds(pl.multiple_of(which * chunk, pad), WIDE)
        acc_gu[b] += dot(first, wgu[at, :])
        acc_b[b] += dot(second, wdt[at, :])

    def ag_wait(b, way, s):
        if s < hops[b][way]:
            ag_copy(b, way, s).wait_recv()

    def ag_start(b, way, s):
        if s < hops[b][way]:
            ag_copy(b, way, s).start()

    def ag_use(b, way, s):
        if s < hops[b][way]:
            multiply(b, lax.rem(z + nz - s - 1, nz) if way == 0 else lax.rem(z + s + 1, nz))

    def rs_copy(b, way, s):
        return pltpu.make_async_remote_copy(
            src_ref=rs_snd.at[b, way, s],
            dst_ref=rs_rcv.at[b, way, s],
            send_sem=rs_send.at[b, way, s],
            recv_sem=rs_recv.at[b, way, s],
            device_id=right if way == 0 else left,
            device_id_type=MESH,
        )

    def term(b, which):
        return dot_nt(dgu[b], wgu[pl.ds(pl.multiple_of(which * chunk, pad), WIDE), :])

    tiles = WIDE // 128 - 1
    fold = rs_snd.shape[3] - tiles * rows
    again_at = rows - fold

    def folded(total):
        tail = total[:, tiles * 128 :]
        lane = iota((fold, 128), 1)
        return jnp.where(lane < pad, tail[:fold], pltpu.roll(tail[again_at:], pad, 1))

    def rs_step(b, s):
        ways = [w for w in range(2) if s < hops[b][w]]
        totals = []
        for way in ways:
            over = hops[b][way] - s
            totals.append(term(b, lax.rem(z + over, nz) if way == 0 else lax.rem(z + nz - over, nz)))
        for way, total in zip(ways, totals):
            tail = folded(total)
            if s > 0:
                rs_copy(b, way, s - 1).wait_recv()
            for i in range(tiles + 1):
                at = pl.ds(i * rows, rows if i < tiles else fold)
                value = total[:, i * 128 : i * 128 + 128] if i < tiles else tail
                if s > 0:
                    value = value + rs_rcv[b, way, s - 1, at, :].astype(F32)
                rs_snd[b, way, s, at, :] = value.astype(BF16)
            rs_copy(b, way, s).start()

    def middle(b):
        gate, upper = acc_gu[b, :, pl.ds(0, 2 * hid)], acc_gu[b, :, pl.ds(2 * hid, 2 * hid)]
        back = acc_b[b]
        sig = 1.0 / (1.0 + jnp.exp(-gate))
        act = gate * sig
        slope = sig * (1.0 + gate * (1.0 - sig))
        dgu[b, :, pl.ds(0, 2 * hid)] = (back * upper * slope).astype(BF16)
        dgu[b, :, pl.ds(2 * hid, 2 * hid)] = (back * act).astype(BF16)
        acc_b[b] = act * upper * back

    def set_scores(b):
        row = lax.dot_general(
            jnp.ones((8, 2 * hid), F32),
            acc_b[b],
            (((1,), (1,)), ((), ())),
            preferred_element_type=F32,
            precision=lax.Precision.HIGHEST,
        )
        scores[z, pl.ds(4 * b, 4), pl.ds(0, rows)] = row[:4]

    def sc_copy(k):
        return pltpu.make_async_remote_copy(
            src_ref=scores.at[z],
            dst_ref=scores.at[z],
            send_sem=sc_send.at[k],
            recv_sem=sc_recv.at[k],
            device_id={"group": g, "dev": lax.rem(z + k, nz) * 2 + c},
            device_id_type=MESH,
        )

    build(0)
    ag_start(0, 0, 0)
    ag_start(0, 1, 0)
    send_batch(1)
    scores[z] = jnp.zeros(scores.shape[1:], F32)
    lax.fori_loop(0, 2, set_away, 0)
    loads[7].wait()
    loads[8].wait()
    for copy in swaps:
        copy.wait_recv()
    multiply(0, z)

    for s in range(half):
        for way in range(2):
            ag_wait(0, way, s)
            ag_start(0, way, s + 1)
        if s == 0:
            ag_use(0, 0, s)
            ag_use(0, 1, s)
            build(1)
        if s == max(half - 3, 0):
            ag_start(1, 1, 0)
        if s == max(half - 2, 0):
            ag_start(1, 0, 0)
        if s == 0:
            multiply(1, z)
        else:
            if s == half - 1:
                ag_wait(1, 1, 0)
                ag_start(1, 1, 1)
            ag_use(0, 0, s)
            ag_use(0, 1, s)
    if half == 1:
        ag_wait(1, 1, 0)
    middle(0)
    rs_step(0, 0)
    ag_use(1, 1, 0)
    for i in range(half - 1):
        ag_wait(1, 0, i)
        ag_start(1, 0, i + 1)
        ag_wait(1, 1, i + 1)
        ag_start(1, 1, i + 2)
        if i == 0:
            set_scores(0)
        ag_use(1, 0, i)
        ag_use(1, 1, i + 1)
        if i < half - 2:
            rs_step(0, i + 1)
    middle(1)
    rs_step(1, 0)
    if half > 1:
        rs_step(0, half - 1)
    else:
        set_scores(0)
    set_scores(1)
    for k in range(1, nz):
        sc_copy(k).start()
    for s in range(1, half):
        rs_step(1, s)

    for k in range(1, nz):
        sc_copy(k).wait_recv()
    score = scores[0]
    for k in range(1, nz):
        score = score + scores[k]

    def ret_copy(b, i, h, sem):
        p, dx, home = home_of(b * nb + i)
        n = p * NX + dx
        return pltpu.make_async_remote_copy(
            src_ref=ret_snd.at[b, h, pl.ds(pl.multiple_of(i * MAIN, MAIN), MAIN), :],
            dst_ref=ret_rcv.at[pl.ds(pl.multiple_of(n * MAIN, MAIN), MAIN), :],
            send_sem=sem,
            recv_sem=ret_recv.at[b],
            device_id={"group": home, "dev": z * 2 + h},
            device_id_type=MESH,
        )

    for b in range(2):
        total = term(b, z)
        tail = folded(total)
        parts = [total[:, i * 128 : i * 128 + 128] for i in range(tiles)] + [tail]
        for way in range(2):
            if hops[b][way] > 0:
                s = hops[b][way] - 1
                rs_copy(b, way, s).wait_recv()
                for i in range(tiles + 1):
                    at = pl.ds(i * rows, rows if i < tiles else fold)
                    parts[i] = parts[i] + rs_rcv[b, way, s, at, :].astype(F32)
        tail = parts.pop()
        lane = iota((rows, 128), 1)
        tail = jnp.concatenate([tail, pltpu.roll(tail, pad, 1)[fold - again_at :]], axis=0)
        parts.append(jnp.where(lane < pad, tail, 0.0))
        total = jnp.concatenate([part.astype(BF16) for part in parts], axis=1)
        whole, extra = total[:main], total[main:]

        row = iota((main, BACK), 0)
        lane = iota((main, BACK), 1)
        q = jnp.bitwise_and(row, MAIN - 1)
        value = jnp.broadcast_to(score[4 * b : 4 * b + 1, :], (main, BACK))
        upper = value.astype(BF16).astype(F32)
        lower = value - upper
        slot = jnp.where(lane < main, lax.shift_right_logical(lane, 4), lax.shift_right_logical(lane - main, 1))
        fits = jnp.logical_and(lax.shift_right_logical(row, 4) == slot, lane < rows)
        value = jnp.where(q == MAIN - 2, upper, jnp.where(q == MAIN - 1, lower, 0.0))
        value = jnp.where(fits, value, 0.0).astype(BF16)
        a, l = iota((BACK, BACK), 0), iota((BACK, BACK), 1)
        number = jnp.where(a < main, jnp.bitwise_and(a, MAIN - 1), MAIN + jnp.bitwise_and(a, 1))
        carried = dot(value, flag(l == feats + number))

        again = flag(
            jnp.logical_and(
                lax.shift_right_logical(iota((main, 2 * nb), 0), 4)
                == lax.shift_right_logical(iota((main, 2 * nb), 1), 1),
                jnp.bitwise_and(iota((main, 2 * nb), 0), 1) == jnp.bitwise_and(iota((main, 2 * nb), 1), 1),
            )
        )
        extra = dot(again, extra)
        for h in range(2):
            lane = iota((main, WIDE), 1) - feats * h
            rr = lax.shift_right_logical(jnp.bitwise_and(iota((main, WIDE), 0), MAIN - 1), 1)
            mine = jnp.logical_and(lane >= rr * room, lane < rr * room + room)
            ends = jnp.where(jnp.logical_and(mine, lane < feats), extra, 0.0).astype(BF16)
            ret_snd[b, h] = (
                dot(whole, away[h, pl.ds(0, WIDE), :]) + dot(ends, away[h, pl.ds(WIDE, WIDE), :]) + carried
            ).astype(BF16)

        def send_back(i, carry, b=b):
            for h in range(2):
                own = jnp.logical_and(c == 0, i == own_slot) if (b == own_b and h == 0) else None
                if own is None:
                    ret_copy(b, i, h, ret_send.at[0]).start()
                else:

                    @pl.when(jnp.logical_not(own))
                    def _():
                        ret_copy(b, i, h, ret_send.at[0]).start()

            return carry

        lax.fori_loop(0, nb, send_back, 0)
        if b == own_b:

            @pl.when(c == 0)
            def _():
                pltpu.make_async_copy(
                    ret_snd.at[own_b, 0, pl.ds(own_slot * MAIN, MAIN), :],
                    ret_rcv.at[pl.ds(NX * MAIN, MAIN), :],
                    ret_recv.at[own_b],
                ).start()

    n_rows = nslot * MAIN
    total = 0.0
    sums = []
    for b in range(2):
        part = pl.ds(b * n_rows, n_rows)
        pltpu.make_async_copy(ret_rcv.at[part], ret_rcv.at[part], ret_recv.at[b]).wait()
        got = ret_rcv[part, :]
        end = got[:, BACK - 128 :]
        widen = flag(iota((128, BACK), 0) == 128 - room + jnp.bitwise_and(iota((128, BACK), 1), room - 1))
        mine = lax.shift_right_logical(
            jnp.bitwise_and(iota((n_rows, BACK), 0), MAIN - 1), 1
        ) == lax.shift_right_logical(iota((n_rows, BACK), 1), room.bit_length() - 1)
        wide = jnp.where(mine, dot(end, widen), 0.0).astype(BF16)
        total = total + dot_tn(got, pick[part, :]) + dot_tn(wide, pick2[part, :])
        a, r = iota((nslot, n_rows), 0), iota((nslot, n_rows), 1)
        this = a == lax.shift_right_logical(r, 4)
        r = jnp.bitwise_and(r, MAIN - 1)
        sums.append(
            dot(flag(jnp.logical_and(this, r == MAIN - 2)), end)
            + dot(flag(jnp.logical_and(this, r == MAIN - 1)), end)
        )
    out_ref[...] = total[:feats].astype(BF16)

    at = hits[...]
    score = jnp.concatenate(sums, axis=0)
    found = jnp.zeros((ngroup, toks), F32)
    for q in range(CAP):
        col = 128 - room + q
        found = jnp.where(at == float(q), jnp.broadcast_to(score[:, col : col + 1], found.shape), found)
    ids = ids_ref[...]
    for k in range(top):
        same = jnp.broadcast_to(ids[k : k + 1, :], (ngroup, toks)) == jnp.broadcast_to(e_col, (ngroup, toks))
        value = jnp.sum(jnp.where(same, found, 0.0), axis=0, keepdims=True)
        gp_ref[pl.ds(k, 1), :] = value / prob_ref[pl.ds(k, 1), :]

    most = 2 * nslot - 1
    part = snd.at[pl.ds(0, most * MAIN), :]
    pltpu.make_async_copy(part, part, fwd_send.at[0]).wait()
    for copy in swaps:
        copy.wait_send()
    for b in range(2):
        for way in range(2):
            for s in range(hops[b][way]):
                ag_copy(b, way, s).wait_send()
                rs_copy(b, way, s).wait_send()
    for k in range(1, nz):
        sc_copy(k).wait_send()
    part = ret_rcv.at[pl.ds(0, most * MAIN), :]
    pltpu.make_async_copy(part, part, ret_send.at[0]).wait()

    @pl.when(c == 1)
    def _():
        one = snd.at[pl.ds(0, MAIN), :]
        pltpu.make_async_copy(one, one, fwd_send.at[1]).wait()
        one = ret_rcv.at[pl.ds(0, MAIN), :]
        pltpu.make_async_copy(one, one, ret_send.at[0]).wait()


def on_device(ny, nz, tokens, upstream, route_probs, expert_ids, w_gate, w_up, w_down):
    toks, feats = tokens.shape
    top = expert_ids.shape[1]
    wide_d, hid = w_gate.shape[1], w_gate.shape[2]
    ngroup = ny * NX
    nslot = ngroup // 2
    nb = nslot // 2
    main, rows = nb * MAIN, nb * CAP
    chunk = 2 * feats
    pad = WIDE - chunk
    half = nz // 2
    message = (WIDE // 128 - 1) * rows + -(-rows // 32) * 16
    dma = pltpu.SemaphoreType.DMA
    vmem = pl.BlockSpec(memory_space=pltpu.VMEM)
    hbm = pl.BlockSpec(memory_space=pltpu.HBM)
    out, gp = pl.pallas_call(
        functools.partial(kernel, ny, nz),
        out_shape=(jax.ShapeDtypeStruct((feats, toks), BF16), jax.ShapeDtypeStruct((top, toks), F32)),
        in_specs=[hbm] * 7,
        out_specs=(vmem, vmem),
        scratch_shapes=[
            pltpu.VMEM((top, toks), I32),
            pltpu.VMEM((top, toks), F32),
            pltpu.VMEM((2, WIDE, toks), BF16),
            pltpu.VMEM((ngroup * MAIN, WIDE), BF16),
            pltpu.VMEM((2, 2, main, WIDE), BF16),
            pltpu.VMEM((2, WIDE, 2 * chunk), BF16),
            pltpu.VMEM((2, 2 * WIDE, BACK), BF16),
            pltpu.VMEM((ngroup, toks), F32),
            pltpu.VMEM((ngroup * MAIN, toks), BF16),
            pltpu.VMEM((ngroup * MAIN, toks), BF16),
            pltpu.VMEM((2, nz, rows, 2 * chunk), BF16),
            pltpu.VMEM((wide_d + pad, 4 * hid), BF16),
            pltpu.VMEM((hid, wide_d), BF16),
            pltpu.VMEM((wide_d + pad, 2 * hid), BF16),
            pltpu.VMEM((2, rows, 4 * hid), F32),
            pltpu.VMEM((2, rows, 2 * hid), F32),
            pltpu.VMEM((2, rows, 4 * hid), BF16),
            pltpu.VMEM((2, 2, half, message, 128), BF16),
            pltpu.VMEM((2, 2, half, message, 128), BF16),
            pltpu.VMEM((nz, 8, BACK), F32),
            pltpu.VMEM((2, 2, main, BACK), BF16),
            pltpu.VMEM((ngroup * MAIN, BACK), BF16),
            dma((9,)),
            dma((3,)),
            dma((3,)),
            dma((2,)),
            dma((2,)),
            dma((2, 2, half)),
            dma((2, 2, half)),
            dma((2, 2, half)),
            dma((2, 2, half)),
            dma((nz,)),
            dma((nz,)),
            dma((1,)),
            dma((2,)),
        ],
        compiler_params=pltpu.CompilerParams(
            collective_id=0, has_side_effects=True, vmem_limit_bytes=60 * 1024 * 1024
        ),
    )(tokens.T, upstream.T, route_probs.T, expert_ids.T, w_gate[0], w_up[0], w_down[0])
    return out.T, gp.T


def solution(mesh):
    ny = mesh.shape["group"] // NX
    nz = mesh.shape["dev"] // 2
    placed = (
        P("group", "dev"),
        P("group", "dev"),
        P("group", None),
        P("group", None),
        P("group", None, "dev"),
        P("group", None, "dev"),
        P("group", "dev", None),
    )
    return jax.shard_map(
        functools.partial(on_device, ny, nz),
        mesh=mesh,
        in_specs=placed,
        out_specs=(P("group", "dev"), P("group", None)),
        check_vma=False,
    )
```

```python
import functools

import jax
import jax.numpy as jnp
from jax import lax
from jax.experimental import pallas as pl
from jax.experimental.pallas import tpu as pltpu
from jax.sharding import PartitionSpec as P

BF16 = jnp.bfloat16
F32 = jnp.float32
I32 = jnp.int32
MESH = pl.DeviceIdType.MESH

NX = 4
MAIN = 16
CAP = 18
WIDE = 512
BACK = 256


def iota(shape, axis):
    return lax.broadcasted_iota(I32, shape, axis)


def flag(mask):
    return jnp.where(mask, 1.0, 0.0).astype(BF16)


def dot(a, b):
    return lax.dot_general(a, b, (((1,), (0,)), ((), ())), preferred_element_type=F32)


def dot_nt(a, b):
    return lax.dot_general(a, b, (((1,), (1,)), ((), ())), preferred_element_type=F32)


def dot_tn(a, b):
    return lax.dot_general(a, b, (((0,), (0,)), ((), ())), preferred_element_type=F32)


def kernel(
    ny,
    nz,
    x_hbm,
    u_hbm,
    prob_hbm,
    ids_hbm,
    wg_hbm,
    wu_hbm,
    wd_hbm,
    out_ref,
    gp_ref,
    ids_ref,
    prob_ref,
    tt,
    snd,
    rcv,
    place,
    away,
    hits,
    pick,
    pick2,
    ag,
    wgu,
    wdraw,
    wdt,
    acc_gu,
    acc_b,
    dgu,
    rs_snd,
    rs_rcv,
    scores,
    ret_snd,
    ret_rcv,
    load_sem,
    swap_send,
    swap_recv,
    fwd_send,
    fwd_recv,
    ag_send,
    ag_recv,
    rs_send,
    rs_recv,
    sc_send,
    sc_recv,
    ret_send,
    ret_recv,
):
    feats, toks = x_hbm.shape
    top = ids_hbm.shape[0]
    hid = wd_hbm.shape[0]
    wide_d = wd_hbm.shape[1]
    ngroup = ny * NX
    nslot = ngroup // 2
    nb = nslot // 2
    main = nb * MAIN
    rows = nb * CAP
    chunk = 2 * feats
    pad = WIDE - chunk

    g = lax.axis_index("group")
    d = lax.axis_index("dev")
    y, x = lax.div(g, NX), lax.rem(g, NX)
    z, c = lax.div(d, 2), lax.rem(d, 2)
    sib = {"group": g, "dev": z * 2 + 1 - c}

    ys = [lax.rem(y + k, ny) * NX for k in range(ny)]
    xs = [lax.rem(x + k, NX) for k in range(NX)]
    back_x = [lax.rem(x + 2 * NX - 2 * k - c, NX) for k in range(NX // 2)]

    def target(n):
        p, dx = n // NX, n % NX
        return p, dx, ys[(p + ny - 1) % ny] + xs[dx]

    def home_of(s):
        p, k = s // 2, s % 2
        return p * NX + 2 * k + c, ys[(1 - p) % ny] + back_x[k]

    loads = [
        pltpu.make_async_copy(ids_hbm, ids_ref, load_sem.at[0]),
        pltpu.make_async_copy(prob_hbm, prob_ref, load_sem.at[1]),
        pltpu.make_async_copy(x_hbm, tt.at[0, pl.ds(0, feats), :], load_sem.at[2]),
        pltpu.make_async_copy(u_hbm, tt.at[0, pl.ds(feats, feats), :], load_sem.at[3]),
        pltpu.make_async_copy(x_hbm, tt.at[1, pl.ds(pad, feats), :], load_sem.at[4]),
        pltpu.make_async_copy(u_hbm, tt.at[1, pl.ds(pad + feats, feats), :], load_sem.at[5]),
        pltpu.make_async_copy(wd_hbm, wdraw, load_sem.at[6]),
        pltpu.make_async_copy(wg_hbm, wgu.at[pl.ds(0, wide_d), pl.ds(0, hid)], load_sem.at[7]),
        pltpu.make_async_copy(wu_hbm, wgu.at[pl.ds(0, wide_d), pl.ds(2 * hid, hid)], load_sem.at[8]),
    ]
    for copy in loads:
        copy.start()

    barrier = pltpu.get_barrier_semaphore()

    for n in range(ngroup):
        p, dx, e = target(n)

        def hello(e=e, core=dx % 2):
            pl.semaphore_signal(barrier, inc=1, device_id={"group": e, "dev": z * 2 + core}, device_id_type=MESH)

        if n == NX:
            pl.when(c == 1)(hello)
        else:
            hello()
    for n in range(ngroup // 2):
        p, k = n // 2, n % 2
        e = ys[p] + lax.rem(x + 2 * k + c, NX)
        pl.semaphore_signal(barrier, inc=1, device_id={"group": e, "dev": z * 2 + 1 - c}, device_id_type=MESH)
    for k in range(1, nz):
        pl.semaphore_signal(
            barrier, inc=1, device_id={"group": g, "dev": lax.rem(z + k, nz) * 2 + c}, device_id_type=MESH
        )
    greeted = ngroup + nslot + nz - 1 - (1 - c)

    zero = jnp.zeros((pad, toks), BF16)
    tt[0, pl.ds(chunk, pad), :] = zero
    tt[1, pl.ds(0, pad), :] = zero

    n_col = iota((ngroup, 1), 0)
    p_col = lax.shift_right_logical(n_col, 2)
    dx_col = jnp.bitwise_and(n_col, NX - 1)
    e_col = jnp.bitwise_and(y + p_col + ny - 1, ny - 1) * NX + jnp.bitwise_and(x + dx_col, NX - 1)
    loads[0].wait()
    loads[1].wait()
    ids = ids_ref[...]
    probs = prob_ref[...]
    hit = jnp.zeros((ngroup, toks), F32)
    prob_n = jnp.zeros((ngroup, toks), F32)
    for k in range(top):
        same = jnp.broadcast_to(ids[k : k + 1, :], (ngroup, toks)) == jnp.broadcast_to(e_col, (ngroup, toks))
        hit = hit + jnp.where(same, 1.0, 0.0)
        prob_n = prob_n + jnp.where(same, jnp.broadcast_to(probs[k : k + 1, :], (ngroup, toks)), 0.0)
    earlier = flag(iota((toks, toks), 0) < iota((toks, toks), 1))
    place_n = jnp.where(hit > 0.5, dot(hit.astype(BF16), earlier), -1.0)
    hits[...] = place_n
    place_bf = place_n.astype(BF16)
    part1 = prob_n.astype(BF16)
    rest = prob_n - part1.astype(F32)
    part2 = rest.astype(BF16)
    part3 = (rest - part2.astype(F32)).astype(BF16)

    step_rows = min(8, ngroup // 2) * MAIN

    def fill(i, carry):
        base = pl.multiple_of(i * step_rows, step_rows)
        row = iota((step_rows, 1), 0)
        rr = jnp.bitwise_and(row, MAIN - 1)
        spread = flag(lax.shift_right_logical(base + iota((step_rows, ngroup), 0), 4) == iota((step_rows, ngroup), 1))
        at = dot(spread, place_bf)
        pr = dot(spread, part1) + dot(spread, part2) + dot(spread, part3)
        m1 = at == jnp.broadcast_to(rr.astype(F32), at.shape)
        m2 = at == jnp.broadcast_to((MAIN + jnp.bitwise_and(rr, 1)).astype(F32), at.shape)
        pick1 = flag(m1)
        pickx = flag(m2)
        pick[pl.ds(base, step_rows), :] = pick1
        pick2[pl.ds(base, step_rows), :] = pickx
        pr1 = jnp.sum(jnp.where(m1, pr, 0.0), axis=1, keepdims=True)
        pr2 = jnp.sum(jnp.where(m2, pr, 0.0), axis=1, keepdims=True)
        got = dot_nt(pick1, tt[0])
        lane = iota((step_rows, WIDE), 1)
        got = jnp.where(jnp.logical_and(lane >= feats, lane < chunk), got * pr1, got)
        odd = dot_nt(pickx, tt[0])
        even = dot_nt(pickx, tt[1])
        part = lax.shift_right_logical(rr, 1)
        extra = jnp.zeros((step_rows, 128), F32)
        for tile in range(WIDE // 128):
            cut = slice(tile * 128, tile * 128 + 128)
            extra = jnp.where(part == 2 * tile, even[:, cut], extra)
            extra = jnp.where(part == 2 * tile + 1, odd[:, cut], extra)
        lane = iota((step_rows, 128), 1)
        extra = jnp.where(part * pad + lane - (128 - pad) >= feats, extra * pr2, extra)
        snd[pl.ds(base, step_rows), pl.ds(0, WIDE - 128)] = got[:, : WIDE - 128].astype(BF16)
        snd[pl.ds(base, step_rows), pl.ds(WIDE - 128, 128)] = jnp.where(
            lane >= 128 - pad, extra, got[:, WIDE - 128 :]
        ).astype(BF16)
        return carry

    for copy in loads[2:6]:
        copy.wait()
    steps = ngroup * MAIN // step_rows
    lax.fori_loop(0, steps // 2, fill, 0)
    pl.semaphore_wait(barrier, greeted)

    def fwd_copy(n, b, sem):
        p, dx, e = target(n)
        slot = p * 2 + dx // 2 - b * nb
        return pltpu.make_async_remote_copy(
            src_ref=snd.at[pl.ds(n * MAIN, MAIN), :],
            dst_ref=rcv.at[b, c, pl.ds(slot * MAIN, MAIN), :],
            send_sem=sem,
            recv_sem=fwd_recv.at[b],
            device_id={"group": e, "dev": z * 2 + dx % 2},
            device_id_type=MESH,
        )

    own_b, own_slot = (0, NX // 2) if ny > 2 else (1, 0)

    def send_batch(b):
        for n in range(b * nslot, (b + 1) * nslot):
            if n != NX:
                fwd_copy(n, b, fwd_send.at[0]).start()
        if b == own_b:

            @pl.when(c == 0)
            def _():
                pltpu.make_async_copy(
                    snd.at[pl.ds(NX * MAIN, MAIN), :],
                    rcv.at[own_b, 0, pl.ds(own_slot * MAIN, MAIN), :],
                    fwd_recv.at[own_b],
                ).start()

            @pl.when(c == 1)
            def _():
                fwd_copy(NX, own_b, fwd_send.at[1]).start()

    send_batch(0)
    lax.fori_loop(steps // 2, steps, fill, 0)

    swaps = [
        pltpu.make_async_remote_copy(
            src_ref=wg_hbm,
            dst_ref=wgu.at[pl.ds(0, wide_d), pl.ds(hid, hid)],
            send_sem=swap_send.at[0],
            recv_sem=swap_recv.at[0],
            device_id=sib,
            device_id_type=MESH,
        ),
        pltpu.make_async_remote_copy(
            src_ref=wu_hbm,
            dst_ref=wgu.at[pl.ds(0, wide_d), pl.ds(3 * hid, hid)],
            send_sem=swap_send.at[1],
            recv_sem=swap_recv.at[1],
            device_id=sib,
            device_id_type=MESH,
        ),
        pltpu.make_async_remote_copy(
            src_ref=wdt.at[pl.ds(pad, wide_d), pl.ds(0, hid)],
            dst_ref=wdt.at[pl.ds(pad, wide_d), pl.ds(hid, hid)],
            send_sem=swap_send.at[2],
            recv_sem=swap_recv.at[2],
            device_id=sib,
            device_id_type=MESH,
        ),
    ]
    swaps[0].start()
    swaps[1].start()

    loads[6].wait()

    def turn(i, carry):
        base = pl.multiple_of(i * 128, 128)
        wdt[pl.ds(pl.multiple_of(base + pad, pad), 128), pl.ds(0, hid)] = wdraw[:, pl.ds(base, 128)].T
        return carry

    lax.fori_loop(0, wide_d // 128, turn, 0)
    swaps[2].start()
    send_batch(1)

    wgu[pl.ds(wide_d, pad), :] = jnp.zeros((pad, 4 * hid), BF16)
    wdt[pl.ds(0, pad), :] = jnp.zeros((pad, 2 * hid), BF16)
    acc_gu[...] = jnp.zeros_like(acc_gu)
    acc_b[...] = jnp.zeros_like(acc_b)

    def set_place(i, carry):
        base = pl.multiple_of(i * 128, 128)
        a = base + iota((128, 2 * chunk), 0)
        f = iota((128, 2 * chunk), 1)
        goal = a + jnp.where(a >= feats, feats, 0)
        keep = a < chunk
        place[0, pl.ds(base, 128), :] = flag(jnp.logical_and(keep, f == goal))
        place[1, pl.ds(base, 128), :] = flag(jnp.logical_and(keep, f == goal + feats))
        return carry

    lax.fori_loop(0, WIDE // 128, set_place, 0)

    room = BACK - feats

    def set_away(h, carry):
        a, l = iota((WIDE, BACK), 0) - feats * h, iota((WIDE, BACK), 1)
        away[h, pl.ds(0, WIDE), :] = flag(jnp.logical_and(a == l, l < feats))
        inside = jnp.logical_and(a >= 0, a < feats)
        away[h, pl.ds(WIDE, WIDE), :] = flag(jnp.logical_and(inside, jnp.bitwise_and(a, room - 1) == l - feats))
        return carry

    def build(b):
        pltpu.make_async_copy(rcv.at[b], rcv.at[b], fwd_recv.at[b]).wait()
        widen = flag(iota((128, WIDE), 0) == 128 - pad + jnp.bitwise_and(iota((128, WIDE), 1), pad - 1))
        mine = lax.shift_right_logical(jnp.bitwise_and(iota((main, WIDE), 0), MAIN - 1), 1) == lax.shift_right_logical(
            iota((main, WIDE), 1), pad.bit_length() - 1
        )
        a, r = iota((2 * nb, main), 0), iota((2 * nb, main), 1)
        gather = flag(
            jnp.logical_and(
                lax.shift_right_logical(a, 1) == lax.shift_right_logical(r, 4),
                jnp.bitwise_and(a, 1) == jnp.bitwise_and(r, 1),
            )
        )
        whole, extra = 0.0, 0.0
        for h in range(2):
            got = rcv[b, h]
            wide = jnp.where(mine, dot(got[:, WIDE - 128 :], widen), 0.0).astype(BF16)
            last = dot(gather, wide).astype(BF16)
            whole = whole + dot(got, place[h])
            extra = extra + dot(last, place[h])
        ag[b, z, pl.ds(0, main), :] = whole.astype(BF16)
        ag[b, z, pl.ds(main, 2 * nb), :] = extra.astype(BF16)

    right = {"group": g, "dev": lax.rem(z + 1, nz) * 2 + c}
    left = {"group": g, "dev": lax.rem(z + nz - 1, nz) * 2 + c}
    half = nz // 2
    hops = [[half, nz - 1 - half], [nz - 1 - half, half]]

    fold = -(-rows // 32) * 16
    cuts = [pl.ds(0, fold), pl.ds(fold, rows - fold)]

    def ag_copy(b, way, s, part):
        which = lax.rem(z + nz - s, nz) if way == 0 else lax.rem(z + s, nz)
        return pltpu.make_async_remote_copy(
            src_ref=ag.at[b, which, cuts[part], :],
            dst_ref=ag.at[b, which, cuts[part], :],
            send_sem=ag_send.at[b, way, s, part],
            recv_sem=ag_recv.at[b, way, s, part],
            device_id=right if way == 0 else left,
            device_id_type=MESH,
        )

    def multiply(b, which):
        lane = iota((rows, 128), 1)
        mid = ag[b, which, :, pl.ds(WIDE - 128, 128)]
        none = jnp.zeros_like(mid)
        first = jnp.concatenate(
            [ag[b, which, :, pl.ds(0, WIDE - 128)], jnp.where(lane < 128 - pad, mid, none)], axis=1
        )
        second = jnp.concatenate(
            [jnp.where(lane >= 128 - pad, mid, none), ag[b, which, :, pl.ds(WIDE, WIDE - 128)]], axis=1
        )
        at = pl.ds(pl.multiple_of(which * chunk, pad), WIDE)
        acc_gu[b] += dot(first, wgu[at, :])
        acc_b[b] += dot(second, wdt[at, :])

    def ag_start(b, way):
        if hops[b][way] > 0:
            for part in range(2):
                ag_copy(b, way, 0, part).start()

    def ag_pass(*which):
        for part in range(2):
            for b, way, s in which:
                if s < hops[b][way]:
                    ag_copy(b, way, s, part).wait_recv()
                    if s + 1 < hops[b][way]:
                        ag_copy(b, way, s + 1, part).start()

    def ag_use(b, way, s):
        if s < hops[b][way]:
            multiply(b, lax.rem(z + nz - s - 1, nz) if way == 0 else lax.rem(z + s + 1, nz))

    tiles = WIDE // 128 - 1
    again_at = rows - fold
    halves = [pl.ds(0, 2 * rows), pl.ds(2 * rows, rs_snd.shape[3] - 2 * rows)]

    def rs_copy(b, way, s, part):
        return pltpu.make_async_remote_copy(
            src_ref=rs_snd.at[b, way, s, halves[part], :],
            dst_ref=rs_rcv.at[b, way, s, halves[part], :],
            send_sem=rs_send.at[b, way, s, part],
            recv_sem=rs_recv.at[b, way, s, part],
            device_id=right if way == 0 else left,
            device_id_type=MESH,
        )

    def term(b, which):
        return dot_nt(dgu[b], wgu[pl.ds(pl.multiple_of(which * chunk, pad), WIDE), :])

    def folded(total):
        tail = total[:, tiles * 128 :]
        lane = iota((fold, 128), 1)
        return jnp.where(lane < pad, tail[:fold], pltpu.roll(tail[again_at:], pad, 1))

    def rs_step(b, s):
        ways = [w for w in range(2) if s < hops[b][w]]
        totals = []
        for way in ways:
            over = hops[b][way] - s
            totals.append(term(b, lax.rem(z + over, nz) if way == 0 else lax.rem(z + nz - over, nz)))
        pieces = [[total[:, i * 128 : i * 128 + 128] for i in range(tiles)] + [folded(total)] for total in totals]
        for part in range(2):
            for way, piece in zip(ways, pieces):
                if s > 0:
                    rs_copy(b, way, s - 1, part).wait_recv()
                for i in (2 * part, 2 * part + 1):
                    at = pl.ds(i * rows, rows if i < tiles else fold)
                    value = piece[i]
                    if s > 0:
                        value = value + rs_rcv[b, way, s - 1, at, :].astype(F32)
                    rs_snd[b, way, s, at, :] = value.astype(BF16)
                rs_copy(b, way, s, part).start()

    def middle(b):
        gate, upper = acc_gu[b, :, pl.ds(0, 2 * hid)], acc_gu[b, :, pl.ds(2 * hid, 2 * hid)]
        back = acc_b[b]
        sig = 1.0 / (1.0 + jnp.exp(-gate))
        act = gate * sig
        slope = sig * (1.0 + gate * (1.0 - sig))
        dgu[b, :, pl.ds(0, 2 * hid)] = (back * upper * slope).astype(BF16)
        dgu[b, :, pl.ds(2 * hid, 2 * hid)] = (back * act).astype(BF16)
        acc_b[b] = act * upper * back

    def set_scores(b):
        row = lax.dot_general(
            jnp.ones((8, 2 * hid), F32),
            acc_b[b],
            (((1,), (1,)), ((), ())),
            preferred_element_type=F32,
            precision=lax.Precision.HIGHEST,
        )
        scores[z, pl.ds(4 * b, 4), pl.ds(0, rows)] = row[:4]

    def sc_copy(k):
        return pltpu.make_async_remote_copy(
            src_ref=scores.at[z],
            dst_ref=scores.at[z],
            send_sem=sc_send.at[k],
            recv_sem=sc_recv.at[k],
            device_id={"group": g, "dev": lax.rem(z + k, nz) * 2 + c},
            device_id_type=MESH,
        )

    build(0)
    ag_start(0, 0)
    ag_start(0, 1)
    scores[z] = jnp.zeros(scores.shape[1:], F32)
    lax.fori_loop(0, 2, set_away, 0)
    loads[7].wait()
    loads[8].wait()
    for copy in swaps:
        copy.wait_recv()
    multiply(0, z)

    for s in range(half):
        ag_pass((0, 0, s), (0, 1, s))
        if s == 0:
            ag_use(0, 0, s)
            ag_use(0, 1, s)
            build(1)
        if s == max(half - 3, 0):
            ag_start(1, 1)
        if s == max(half - 2, 0):
            ag_start(1, 0)
        if s == 0:
            multiply(1, z)
        else:
            if s == half - 1:
                ag_pass((1, 1, 0))
            ag_use(0, 0, s)
            ag_use(0, 1, s)
    if half == 1:
        ag_pass((1, 1, 0))
    middle(0)
    rs_step(0, 0)
    ag_use(1, 1, 0)
    for i in range(half - 1):
        ag_pass((1, 0, i), (1, 1, i + 1))
        if i == 0:
            set_scores(0)
        ag_use(1, 0, i)
        ag_use(1, 1, i + 1)
        if i < half - 2:
            rs_step(0, i + 1)
    middle(1)
    rs_step(1, 0)
    if half > 1:
        rs_step(0, half - 1)
    else:
        set_scores(0)
    set_scores(1)
    for k in range(1, nz):
        sc_copy(k).start()
    for s in range(1, half):
        rs_step(1, s)

    for k in range(1, nz):
        sc_copy(k).wait_recv()
    score = scores[0]
    for k in range(1, nz):
        score = score + scores[k]

    def ret_copy(b, i, h, sem):
        n, home = home_of(b * nb + i)
        return pltpu.make_async_remote_copy(
            src_ref=ret_snd.at[b, h, pl.ds(i * MAIN, MAIN), :],
            dst_ref=ret_rcv.at[pl.ds(pl.multiple_of(n * MAIN, MAIN), MAIN), :],
            send_sem=sem,
            recv_sem=ret_recv.at[b],
            device_id={"group": home, "dev": z * 2 + h},
            device_id_type=MESH,
        )

    for b in range(2):
        total = term(b, z)
        tail = folded(total)
        parts = [total[:, i * 128 : i * 128 + 128] for i in range(tiles)] + [tail]
        for part in range(2):
            for way in range(2):
                if hops[b][way] > 0:
                    s = hops[b][way] - 1
                    rs_copy(b, way, s, part).wait_recv()
                    for i in (2 * part, 2 * part + 1):
                        at = pl.ds(i * rows, rows if i < tiles else fold)
                        parts[i] = parts[i] + rs_rcv[b, way, s, at, :].astype(F32)
        tail = parts.pop()
        lane = iota((rows, 128), 1)
        tail = jnp.concatenate([tail, pltpu.roll(tail, pad, 1)[fold - again_at :]], axis=0)
        parts.append(jnp.where(lane < pad, tail, 0.0))
        total = jnp.concatenate([part.astype(BF16) for part in parts], axis=1)
        whole, extra = total[:main], total[main:]

        row = iota((main, BACK), 0)
        lane = iota((main, BACK), 1)
        q = jnp.bitwise_and(row, MAIN - 1)
        value = jnp.broadcast_to(score[4 * b : 4 * b + 1, :], (main, BACK))
        upper = value.astype(BF16).astype(F32)
        lower = value - upper
        slot = jnp.where(lane < main, lax.shift_right_logical(lane, 4), lax.shift_right_logical(lane - main, 1))
        fits = jnp.logical_and(lax.shift_right_logical(row, 4) == slot, lane < rows)
        value = jnp.where(q == MAIN - 2, upper, jnp.where(q == MAIN - 1, lower, 0.0))
        value = jnp.where(fits, value, 0.0).astype(BF16)
        a, l = iota((BACK, BACK), 0), iota((BACK, BACK), 1)
        number = jnp.where(a < main, jnp.bitwise_and(a, MAIN - 1), MAIN + jnp.bitwise_and(a, 1))
        carried = dot(value, flag(l == feats + number))

        again = flag(
            jnp.logical_and(
                lax.shift_right_logical(iota((main, 2 * nb), 0), 4)
                == lax.shift_right_logical(iota((main, 2 * nb), 1), 1),
                jnp.bitwise_and(iota((main, 2 * nb), 0), 1) == jnp.bitwise_and(iota((main, 2 * nb), 1), 1),
            )
        )
        extra = dot(again, extra)
        for h in range(2):
            lane = iota((main, WIDE), 1) - feats * h
            rr = lax.shift_right_logical(jnp.bitwise_and(iota((main, WIDE), 0), MAIN - 1), 1)
            mine = jnp.logical_and(lane >= rr * room, lane < rr * room + room)
            ends = jnp.where(jnp.logical_and(mine, lane < feats), extra, 0.0).astype(BF16)
            ret_snd[b, h] = (
                dot(whole, away[h, pl.ds(0, WIDE), :]) + dot(ends, away[h, pl.ds(WIDE, WIDE), :]) + carried
            ).astype(BF16)

        for i in range(nb):
            for h in range(2):

                def away_go(b=b, i=i, h=h):
                    ret_copy(b, i, h, ret_send.at[0]).start()

                if (b, i, h) == (own_b, own_slot, 0):
                    pl.when(c == 1)(away_go)
                else:
                    away_go()
        if b == own_b:

            @pl.when(c == 0)
            def _():
                pltpu.make_async_copy(
                    ret_snd.at[own_b, 0, pl.ds(own_slot * MAIN, MAIN), :],
                    ret_rcv.at[pl.ds(NX * MAIN, MAIN), :],
                    ret_recv.at[own_b],
                ).start()

    n_rows = nslot * MAIN
    total = 0.0
    sums = []
    for b in range(2):
        part = pl.ds(b * n_rows, n_rows)
        pltpu.make_async_copy(ret_rcv.at[part], ret_rcv.at[part], ret_recv.at[b]).wait()
        got = ret_rcv[part, :]
        end = got[:, BACK - 128 :]
        widen = flag(iota((128, BACK), 0) == 128 - room + jnp.bitwise_and(iota((128, BACK), 1), room - 1))
        mine = lax.shift_right_logical(
            jnp.bitwise_and(iota((n_rows, BACK), 0), MAIN - 1), 1
        ) == lax.shift_right_logical(iota((n_rows, BACK), 1), room.bit_length() - 1)
        wide = jnp.where(mine, dot(end, widen), 0.0).astype(BF16)
        total = total + dot_tn(got, pick[part, :]) + dot_tn(wide, pick2[part, :])
        a, r = iota((nslot, n_rows), 0), iota((nslot, n_rows), 1)
        this = a == lax.shift_right_logical(r, 4)
        r = jnp.bitwise_and(r, MAIN - 1)
        sums.append(
            dot(flag(jnp.logical_and(this, r == MAIN - 2)), end)
            + dot(flag(jnp.logical_and(this, r == MAIN - 1)), end)
        )
    out_ref[...] = total[:feats].astype(BF16)

    at = hits[...]
    score = jnp.concatenate(sums, axis=0)
    found = jnp.zeros((ngroup, toks), F32)
    for q in range(CAP):
        col = 128 - room + q
        found = jnp.where(at == float(q), jnp.broadcast_to(score[:, col : col + 1], found.shape), found)
    ids = ids_ref[...]
    for k in range(top):
        same = jnp.broadcast_to(ids[k : k + 1, :], (ngroup, toks)) == jnp.broadcast_to(e_col, (ngroup, toks))
        value = jnp.sum(jnp.where(same, found, 0.0), axis=0, keepdims=True)
        gp_ref[pl.ds(k, 1), :] = value / prob_ref[pl.ds(k, 1), :]

    most = 2 * nslot - 1
    part = snd.at[pl.ds(0, most * MAIN), :]
    pltpu.make_async_copy(part, part, fwd_send.at[0]).wait()
    for copy in swaps:
        copy.wait_send()
    for b in range(2):
        for way in range(2):
            for s in range(hops[b][way]):
                for part in range(2):
                    ag_copy(b, way, s, part).wait_send()
                    rs_copy(b, way, s, part).wait_send()
    for k in range(1, nz):
        sc_copy(k).wait_send()
    part = ret_rcv.at[pl.ds(0, most * MAIN), :]
    pltpu.make_async_copy(part, part, ret_send.at[0]).wait()

    @pl.when(c == 1)
    def _():
        one = snd.at[pl.ds(0, MAIN), :]
        pltpu.make_async_copy(one, one, fwd_send.at[1]).wait()
        one = ret_rcv.at[pl.ds(0, MAIN), :]
        pltpu.make_async_copy(one, one, ret_send.at[0]).wait()


def on_device(ny, nz, tokens, upstream, route_probs, expert_ids, w_gate, w_up, w_down):
    toks, feats = tokens.shape
    top = expert_ids.shape[1]
    wide_d, hid = w_gate.shape[1], w_gate.shape[2]
    ngroup = ny * NX
    nslot = ngroup // 2
    nb = nslot // 2
    main, rows = nb * MAIN, nb * CAP
    chunk = 2 * feats
    pad = WIDE - chunk
    half = nz // 2
    message = (WIDE // 128 - 1) * rows + -(-rows // 32) * 16
    dma = pltpu.SemaphoreType.DMA
    vmem = pl.BlockSpec(memory_space=pltpu.VMEM)
    hbm = pl.BlockSpec(memory_space=pltpu.HBM)
    out, gp = pl.pallas_call(
        functools.partial(kernel, ny, nz),
        out_shape=(jax.ShapeDtypeStruct((feats, toks), BF16), jax.ShapeDtypeStruct((top, toks), F32)),
        in_specs=[hbm] * 7,
        out_specs=(vmem, vmem),
        scratch_shapes=[
            pltpu.VMEM((top, toks), I32),
            pltpu.VMEM((top, toks), F32),
            pltpu.VMEM((2, WIDE, toks), BF16),
            pltpu.VMEM((ngroup * MAIN, WIDE), BF16),
            pltpu.VMEM((2, 2, main, WIDE), BF16),
            pltpu.VMEM((2, WIDE, 2 * chunk), BF16),
            pltpu.VMEM((2, 2 * WIDE, BACK), BF16),
            pltpu.VMEM((ngroup, toks), F32),
            pltpu.VMEM((ngroup * MAIN, toks), BF16),
            pltpu.VMEM((ngroup * MAIN, toks), BF16),
            pltpu.VMEM((2, nz, rows, 2 * chunk), BF16),
            pltpu.VMEM((wide_d + pad, 4 * hid), BF16),
            pltpu.VMEM((hid, wide_d), BF16),
            pltpu.VMEM((wide_d + pad, 2 * hid), BF16),
            pltpu.VMEM((2, rows, 4 * hid), F32),
            pltpu.VMEM((2, rows, 2 * hid), F32),
            pltpu.VMEM((2, rows, 4 * hid), BF16),
            pltpu.VMEM((2, 2, half, message, 128), BF16),
            pltpu.VMEM((2, 2, half, message, 128), BF16),
            pltpu.VMEM((nz, 8, BACK), F32),
            pltpu.VMEM((2, 2, main, BACK), BF16),
            pltpu.VMEM((ngroup * MAIN, BACK), BF16),
            dma((9,)),
            dma((3,)),
            dma((3,)),
            dma((2,)),
            dma((2,)),
            dma((2, 2, half, 2)),
            dma((2, 2, half, 2)),
            dma((2, 2, half, 2)),
            dma((2, 2, half, 2)),
            dma((nz,)),
            dma((nz,)),
            dma((1,)),
            dma((2,)),
        ],
        compiler_params=pltpu.CompilerParams(
            collective_id=0, has_side_effects=True, vmem_limit_bytes=60 * 1024 * 1024
        ),
    )(tokens.T, upstream.T, route_probs.T, expert_ids.T, w_gate[0], w_up[0], w_down[0])
    return out.T, gp.T


def solution(mesh):
    ny = mesh.shape["group"] // NX
    nz = mesh.shape["dev"] // 2
    placed = (
        P("group", "dev"),
        P("group", "dev"),
        P("group", None),
        P("group", None),
        P("group", None, "dev"),
        P("group", None, "dev"),
        P("group", "dev", None),
    )
    return jax.shard_map(
        functools.partial(on_device, ny, nz),
        mesh=mesh,
        in_specs=placed,
        out_specs=(P("group", "dev"), P("group", None)),
        check_vma=False,
    )
```

```python
import functools

import jax
import jax.numpy as jnp
from jax import lax
from jax.experimental import pallas as pl
from jax.experimental.pallas import tpu as pltpu
from jax.sharding import PartitionSpec as P

BF16 = jnp.bfloat16
F32 = jnp.float32
I32 = jnp.int32
MESH = pl.DeviceIdType.MESH

NX = 4
MAIN = 16
CAP = 18
WIDE = 512
BACK = 256


def iota(shape, axis):
    return lax.broadcasted_iota(I32, shape, axis)


def flag(mask):
    return jnp.where(mask, 1.0, 0.0).astype(BF16)


def dot(a, b):
    return lax.dot_general(a, b, (((1,), (0,)), ((), ())), preferred_element_type=F32)


def dot_nt(a, b):
    return lax.dot_general(a, b, (((1,), (1,)), ((), ())), preferred_element_type=F32)


def dot_tn(a, b):
    return lax.dot_general(a, b, (((0,), (0,)), ((), ())), preferred_element_type=F32)


def kernel(
    ny,
    nz,
    x_hbm,
    u_hbm,
    prob_hbm,
    ids_hbm,
    wg_hbm,
    wu_hbm,
    wd_hbm,
    out_ref,
    gp_ref,
    ids_ref,
    prob_ref,
    tt,
    snd,
    rcv,
    place,
    away,
    hits,
    pick,
    pick2,
    ag,
    wgu,
    wdraw,
    wdt,
    acc_gu,
    acc_b,
    dgu,
    rs_snd,
    rs_rcv,
    scores,
    ret_snd,
    ret_rcv,
    load_sem,
    swap_send,
    swap_recv,
    fwd_send,
    fwd_recv,
    ag_send,
    ag_recv,
    rs_send,
    rs_recv,
    sc_send,
    sc_recv,
    ret_send,
    ret_recv,
):
    feats, toks = x_hbm.shape
    top = ids_hbm.shape[0]
    hid = wd_hbm.shape[0]
    wide_d = wd_hbm.shape[1]
    ngroup = ny * NX
    nslot = ngroup // 2
    nb = nslot // 2
    main = nb * MAIN
    rows = nb * CAP
    chunk = 2 * feats
    pad = WIDE - chunk

    g = lax.axis_index("group")
    d = lax.axis_index("dev")
    y, x = lax.div(g, NX), lax.rem(g, NX)
    z, c = lax.div(d, 2), lax.rem(d, 2)
    sib = {"group": g, "dev": z * 2 + 1 - c}

    ys = [lax.rem(y + k, ny) * NX for k in range(ny)]
    xs = [lax.rem(x + k, NX) for k in range(NX)]
    back_x = [lax.rem(x + 2 * NX - 2 * k - c, NX) for k in range(NX // 2)]

    def target(n):
        p, dx = n // NX, n % NX
        return p, dx, ys[(p + ny - 1) % ny] + xs[dx]

    def home_of(s):
        p, k = s // 2, s % 2
        return p * NX + 2 * k + c, ys[(1 - p) % ny] + back_x[k]

    loads = [
        pltpu.make_async_copy(ids_hbm, ids_ref, load_sem.at[0]),
        pltpu.make_async_copy(prob_hbm, prob_ref, load_sem.at[1]),
        pltpu.make_async_copy(x_hbm, tt.at[0, pl.ds(0, feats), :], load_sem.at[2]),
        pltpu.make_async_copy(u_hbm, tt.at[0, pl.ds(feats, feats), :], load_sem.at[3]),
        pltpu.make_async_copy(x_hbm, tt.at[1, pl.ds(pad, feats), :], load_sem.at[4]),
        pltpu.make_async_copy(u_hbm, tt.at[1, pl.ds(pad + feats, feats), :], load_sem.at[5]),
        pltpu.make_async_copy(wd_hbm, wdraw, load_sem.at[6]),
        pltpu.make_async_copy(wg_hbm, wgu.at[pl.ds(0, wide_d), pl.ds(0, hid)], load_sem.at[7]),
        pltpu.make_async_copy(wu_hbm, wgu.at[pl.ds(0, wide_d), pl.ds(2 * hid, hid)], load_sem.at[8]),
    ]
    for copy in loads:
        copy.start()

    barrier = pltpu.get_barrier_semaphore()

    for n in range(ngroup):
        p, dx, e = target(n)

        def hello(e=e, core=dx % 2):
            pl.semaphore_signal(barrier, inc=1, device_id={"group": e, "dev": z * 2 + core}, device_id_type=MESH)

        if n == NX:
            pl.when(c == 1)(hello)
        else:
            hello()
    for n in range(ngroup // 2):
        p, k = n // 2, n % 2
        e = ys[p] + lax.rem(x + 2 * k + c, NX)
        pl.semaphore_signal(barrier, inc=1, device_id={"group": e, "dev": z * 2 + 1 - c}, device_id_type=MESH)
    for k in range(1, nz):
        pl.semaphore_signal(
            barrier, inc=1, device_id={"group": g, "dev": lax.rem(z + k, nz) * 2 + c}, device_id_type=MESH
        )
    greeted = ngroup + nslot + nz - 1 - (1 - c)

    zero = jnp.zeros((pad, toks), BF16)
    tt[0, pl.ds(chunk, pad), :] = zero
    tt[1, pl.ds(0, pad), :] = zero

    n_col = iota((ngroup, 1), 0)
    p_col = lax.shift_right_logical(n_col, 2)
    dx_col = jnp.bitwise_and(n_col, NX - 1)
    e_col = jnp.bitwise_and(y + p_col + ny - 1, ny - 1) * NX + jnp.bitwise_and(x + dx_col, NX - 1)
    loads[0].wait()
    loads[1].wait()
    ids = ids_ref[...]
    probs = prob_ref[...]
    hit = jnp.zeros((ngroup, toks), F32)
    prob_n = jnp.zeros((ngroup, toks), F32)
    for k in range(top):
        same = jnp.broadcast_to(ids[k : k + 1, :], (ngroup, toks)) == jnp.broadcast_to(e_col, (ngroup, toks))
        hit = hit + jnp.where(same, 1.0, 0.0)
        prob_n = prob_n + jnp.where(same, jnp.broadcast_to(probs[k : k + 1, :], (ngroup, toks)), 0.0)
    earlier = flag(iota((toks, toks), 0) < iota((toks, toks), 1))
    place_n = jnp.where(hit > 0.5, dot(hit.astype(BF16), earlier), -1.0)
    hits[...] = place_n
    place_bf = place_n.astype(BF16)
    part1 = prob_n.astype(BF16)
    rest = prob_n - part1.astype(F32)
    part2 = rest.astype(BF16)
    part3 = (rest - part2.astype(F32)).astype(BF16)

    step_rows = min(8, ngroup // 2) * MAIN

    def fill(i, carry):
        base = pl.multiple_of(i * step_rows, step_rows)
        row = iota((step_rows, 1), 0)
        rr = jnp.bitwise_and(row, MAIN - 1)
        spread = flag(lax.shift_right_logical(base + iota((step_rows, ngroup), 0), 4) == iota((step_rows, ngroup), 1))
        at = dot(spread, place_bf)
        pr = dot(spread, part1) + dot(spread, part2) + dot(spread, part3)
        m1 = at == jnp.broadcast_to(rr.astype(F32), at.shape)
        m2 = at == jnp.broadcast_to((MAIN + jnp.bitwise_and(rr, 1)).astype(F32), at.shape)
        pick1 = flag(m1)
        pickx = flag(m2)
        pick[pl.ds(base, step_rows), :] = pick1
        pick2[pl.ds(base, step_rows), :] = pickx
        pr1 = jnp.sum(jnp.where(m1, pr, 0.0), axis=1, keepdims=True)
        pr2 = jnp.sum(jnp.where(m2, pr, 0.0), axis=1, keepdims=True)
        got = dot_nt(pick1, tt[0])
        lane = iota((step_rows, WIDE), 1)
        got = jnp.where(jnp.logical_and(lane >= feats, lane < chunk), got * pr1, got)
        odd = dot_nt(pickx, tt[0])
        even = dot_nt(pickx, tt[1])
        part = lax.shift_right_logical(rr, 1)
        extra = jnp.zeros((step_rows, 128), F32)
        for tile in range(WIDE // 128):
            cut = slice(tile * 128, tile * 128 + 128)
            extra = jnp.where(part == 2 * tile, even[:, cut], extra)
            extra = jnp.where(part == 2 * tile + 1, odd[:, cut], extra)
        lane = iota((step_rows, 128), 1)
        extra = jnp.where(part * pad + lane - (128 - pad) >= feats, extra * pr2, extra)
        snd[pl.ds(base, step_rows), pl.ds(0, WIDE - 128)] = got[:, : WIDE - 128].astype(BF16)
        snd[pl.ds(base, step_rows), pl.ds(WIDE - 128, 128)] = jnp.where(
            lane >= 128 - pad, extra, got[:, WIDE - 128 :]
        ).astype(BF16)
        return carry

    for copy in loads[2:6]:
        copy.wait()
    steps = ngroup * MAIN // step_rows
    lax.fori_loop(0, steps // 2, fill, 0)
    pl.semaphore_wait(barrier, greeted)

    def fwd_copy(n, b, sem):
        p, dx, e = target(n)
        slot = p * 2 + dx // 2 - b * nb
        return pltpu.make_async_remote_copy(
            src_ref=snd.at[pl.ds(n * MAIN, MAIN), :],
            dst_ref=rcv.at[b, c, pl.ds(slot * MAIN, MAIN), :],
            send_sem=sem,
            recv_sem=fwd_recv.at[b],
            device_id={"group": e, "dev": z * 2 + dx % 2},
            device_id_type=MESH,
        )

    own_b, own_slot = (0, NX // 2) if ny > 2 else (1, 0)

    def send_batch(b):
        for n in range(b * nslot, (b + 1) * nslot):
            if n != NX:
                fwd_copy(n, b, fwd_send.at[0]).start()
        if b == own_b:

            @pl.when(c == 0)
            def _():
                pltpu.make_async_copy(
                    snd.at[pl.ds(NX * MAIN, MAIN), :],
                    rcv.at[own_b, 0, pl.ds(own_slot * MAIN, MAIN), :],
                    fwd_recv.at[own_b],
                ).start()

            @pl.when(c == 1)
            def _():
                fwd_copy(NX, own_b, fwd_send.at[1]).start()

    send_batch(0)
    lax.fori_loop(steps // 2, steps, fill, 0)

    swaps = [
        pltpu.make_async_remote_copy(
            src_ref=wg_hbm,
            dst_ref=wgu.at[pl.ds(0, wide_d), pl.ds(hid, hid)],
            send_sem=swap_send.at[0],
            recv_sem=swap_recv.at[0],
            device_id=sib,
            device_id_type=MESH,
        ),
        pltpu.make_async_remote_copy(
            src_ref=wu_hbm,
            dst_ref=wgu.at[pl.ds(0, wide_d), pl.ds(3 * hid, hid)],
            send_sem=swap_send.at[1],
            recv_sem=swap_recv.at[1],
            device_id=sib,
            device_id_type=MESH,
        ),
        pltpu.make_async_remote_copy(
            src_ref=wdt.at[pl.ds(pad, wide_d), pl.ds(0, hid)],
            dst_ref=wdt.at[pl.ds(pad, wide_d), pl.ds(hid, hid)],
            send_sem=swap_send.at[2],
            recv_sem=swap_recv.at[2],
            device_id=sib,
            device_id_type=MESH,
        ),
    ]
    swaps[0].start()
    swaps[1].start()

    loads[6].wait()

    def turn(i, carry):
        base = pl.multiple_of(i * 128, 128)
        wdt[pl.ds(pl.multiple_of(base + pad, pad), 128), pl.ds(0, hid)] = wdraw[:, pl.ds(base, 128)].T
        return carry

    lax.fori_loop(0, wide_d // 128, turn, 0)
    swaps[2].start()
    send_batch(1)

    wgu[pl.ds(wide_d, pad), :] = jnp.zeros((pad, 4 * hid), BF16)
    wdt[pl.ds(0, pad), :] = jnp.zeros((pad, 2 * hid), BF16)
    acc_gu[...] = jnp.zeros_like(acc_gu)
    acc_b[...] = jnp.zeros_like(acc_b)

    def set_place(i, carry):
        base = pl.multiple_of(i * 128, 128)
        a = base + iota((128, 2 * chunk), 0)
        f = iota((128, 2 * chunk), 1)
        goal = a + jnp.where(a >= feats, feats, 0)
        keep = a < chunk
        place[0, pl.ds(base, 128), :] = flag(jnp.logical_and(keep, f == goal))
        place[1, pl.ds(base, 128), :] = flag(jnp.logical_and(keep, f == goal + feats))
        return carry

    lax.fori_loop(0, WIDE // 128, set_place, 0)

    room = BACK - feats

    def set_away(h, carry):
        a, l = iota((WIDE, BACK), 0) - feats * h, iota((WIDE, BACK), 1)
        away[h, pl.ds(0, WIDE), :] = flag(jnp.logical_and(a == l, l < feats))
        inside = jnp.logical_and(a >= 0, a < feats)
        away[h, pl.ds(WIDE, WIDE), :] = flag(jnp.logical_and(inside, jnp.bitwise_and(a, room - 1) == l - feats))
        return carry

    def build(b):
        pltpu.make_async_copy(rcv.at[b], rcv.at[b], fwd_recv.at[b]).wait()
        widen = flag(iota((128, WIDE), 0) == 128 - pad + jnp.bitwise_and(iota((128, WIDE), 1), pad - 1))
        mine = lax.shift_right_logical(jnp.bitwise_and(iota((main, WIDE), 0), MAIN - 1), 1) == lax.shift_right_logical(
            iota((main, WIDE), 1), pad.bit_length() - 1
        )
        a, r = iota((2 * nb, main), 0), iota((2 * nb, main), 1)
        gather = flag(
            jnp.logical_and(
                lax.shift_right_logical(a, 1) == lax.shift_right_logical(r, 4),
                jnp.bitwise_and(a, 1) == jnp.bitwise_and(r, 1),
            )
        )
        whole, extra = 0.0, 0.0
        for h in range(2):
            got = rcv[b, h]
            wide = jnp.where(mine, dot(got[:, WIDE - 128 :], widen), 0.0).astype(BF16)
            last = dot(gather, wide).astype(BF16)
            whole = whole + dot(got, place[h])
            extra = extra + dot(last, place[h])
        ag[b, z, pl.ds(0, main), :] = whole.astype(BF16)
        ag[b, z, pl.ds(main, 2 * nb), :] = extra.astype(BF16)

    right = {"group": g, "dev": lax.rem(z + 1, nz) * 2 + c}
    left = {"group": g, "dev": lax.rem(z + nz - 1, nz) * 2 + c}
    half = nz // 2
    hops = [[half, nz - 1 - half], [nz - 1 - half, half]]

    fold = -(-rows // 32) * 16
    cuts = [pl.ds(0, fold), pl.ds(fold, rows - fold)]

    def ag_copy(b, way, s, part):
        which = lax.rem(z + nz - s, nz) if way == 0 else lax.rem(z + s, nz)
        return pltpu.make_async_remote_copy(
            src_ref=ag.at[b, which, cuts[part], :],
            dst_ref=ag.at[b, which, cuts[part], :],
            send_sem=ag_send.at[b, way, s, part],
            recv_sem=ag_recv.at[b, way, s, part],
            device_id=right if way == 0 else left,
            device_id_type=MESH,
        )

    def multiply(b, which):
        lane = iota((rows, 128), 1)
        mid = ag[b, which, :, pl.ds(WIDE - 128, 128)]
        none = jnp.zeros_like(mid)
        first = jnp.concatenate(
            [ag[b, which, :, pl.ds(0, WIDE - 128)], jnp.where(lane < 128 - pad, mid, none)], axis=1
        )
        second = jnp.concatenate(
            [jnp.where(lane >= 128 - pad, mid, none), ag[b, which, :, pl.ds(WIDE, WIDE - 128)]], axis=1
        )
        at = pl.ds(pl.multiple_of(which * chunk, pad), WIDE)
        acc_gu[b] += dot(first, wgu[at, :])
        acc_b[b] += dot(second, wdt[at, :])

    def ag_start(b, way):
        if hops[b][way] > 0:
            for part in range(2):
                ag_copy(b, way, 0, part).start()

    def ag_pass(*which):
        for part in range(2):
            for b, way, s in which:
                if s < hops[b][way]:
                    ag_copy(b, way, s, part).wait_recv()
                    if s + 1 < hops[b][way]:
                        ag_copy(b, way, s + 1, part).start()

    def ag_use(b, way, s):
        if s < hops[b][way]:
            multiply(b, lax.rem(z + nz - s - 1, nz) if way == 0 else lax.rem(z + s + 1, nz))

    tiles = WIDE // 128 - 1
    again_at = rows - fold
    halves = [pl.ds(0, 2 * rows), pl.ds(2 * rows, rs_snd.shape[3] - 2 * rows)]

    def rs_copy(b, way, s, part):
        return pltpu.make_async_remote_copy(
            src_ref=rs_snd.at[b, way, s, halves[part], :],
            dst_ref=rs_rcv.at[b, way, s, halves[part], :],
            send_sem=rs_send.at[b, way, s, part],
            recv_sem=rs_recv.at[b, way, s, part],
            device_id=right if way == 0 else left,
            device_id_type=MESH,
        )

    def term(b, which):
        return dot_nt(dgu[b], wgu[pl.ds(pl.multiple_of(which * chunk, pad), WIDE), :])

    def folded(total):
        tail = total[:, tiles * 128 :]
        lane = iota((fold, 128), 1)
        return jnp.where(lane < pad, tail[:fold], pltpu.roll(tail[again_at:], pad, 1))

    def rs_step(b, s):
        ways = [w for w in range(2) if s < hops[b][w]]
        totals = []
        for way in ways:
            over = hops[b][way] - s
            totals.append(term(b, lax.rem(z + over, nz) if way == 0 else lax.rem(z + nz - over, nz)))
        pieces = [[total[:, i * 128 : i * 128 + 128] for i in range(tiles)] + [folded(total)] for total in totals]
        for part in range(2):
            for way, piece in zip(ways, pieces):
                if s > 0:
                    rs_copy(b, way, s - 1, part).wait_recv()
                for i in (2 * part, 2 * part + 1):
                    at = pl.ds(i * rows, rows if i < tiles else fold)
                    value = piece[i]
                    if s > 0:
                        value = value + rs_rcv[b, way, s - 1, at, :].astype(F32)
                    rs_snd[b, way, s, at, :] = value.astype(BF16)
                rs_copy(b, way, s, part).start()

    def middle(b):
        gate, upper = acc_gu[b, :, pl.ds(0, 2 * hid)], acc_gu[b, :, pl.ds(2 * hid, 2 * hid)]
        back = acc_b[b]
        sig = 1.0 / (1.0 + jnp.exp(-gate))
        act = gate * sig
        slope = sig * (1.0 + gate * (1.0 - sig))
        dgu[b, :, pl.ds(0, 2 * hid)] = (back * upper * slope).astype(BF16)
        dgu[b, :, pl.ds(2 * hid, 2 * hid)] = (back * act).astype(BF16)
        acc_b[b] = act * upper * back

    def set_scores(b):
        row = lax.dot_general(
            jnp.ones((8, 2 * hid), F32),
            acc_b[b],
            (((1,), (1,)), ((), ())),
            preferred_element_type=F32,
            precision=lax.Precision.HIGHEST,
        )
        scores[z, pl.ds(4 * b, 4), pl.ds(0, rows)] = row[:4]

    def sc_copy(k):
        return pltpu.make_async_remote_copy(
            src_ref=scores.at[z],
            dst_ref=scores.at[z],
            send_sem=sc_send.at[k],
            recv_sem=sc_recv.at[k],
            device_id={"group": g, "dev": lax.rem(z + k, nz) * 2 + c},
            device_id_type=MESH,
        )

    build(0)
    ag_start(0, 0)
    ag_start(0, 1)
    scores[z] = jnp.zeros(scores.shape[1:], F32)
    lax.fori_loop(0, 2, set_away, 0)
    loads[7].wait()
    loads[8].wait()
    for copy in swaps:
        copy.wait_recv()
    multiply(0, z)

    ag_pass((0, 0, 0), (0, 1, 0))
    ag_use(0, 0, 0)
    ag_use(0, 1, 0)
    build(1)
    ag_start(1, 0)
    ag_start(1, 1)
    multiply(1, z)
    for s in range(1, half):
        ag_pass((0, 0, s), (0, 1, s))
        ag_use(0, 0, s)
        ag_use(0, 1, s)
        if s < half - 1:
            ag_pass((1, 0, s - 1), (1, 1, s - 1))
            ag_use(1, 0, s - 1)
            ag_use(1, 1, s - 1)
    middle(0)
    rs_step(0, 0)
    for s in range(max(half - 2, 0), half):
        ag_pass((1, 0, s), (1, 1, s))
        ag_use(1, 0, s)
        ag_use(1, 1, s)
        if s == half - 2:
            set_scores(0)
    if half == 1:
        set_scores(0)
    middle(1)
    rs_step(1, 0)
    if half > 1:
        rs_step(0, 1)
    set_scores(1)
    for k in range(1, nz):
        sc_copy(k).start()
    for s in range(1, half):
        rs_step(1, s)
        if s + 1 < half:
            rs_step(0, s + 1)

    for k in range(1, nz):
        sc_copy(k).wait_recv()
    score = scores[0]
    for k in range(1, nz):
        score = score + scores[k]

    def ret_copy(b, i, h, sem):
        n, home = home_of(b * nb + i)
        return pltpu.make_async_remote_copy(
            src_ref=ret_snd.at[b, h, pl.ds(i * MAIN, MAIN), :],
            dst_ref=ret_rcv.at[pl.ds(pl.multiple_of(n * MAIN, MAIN), MAIN), :],
            send_sem=sem,
            recv_sem=ret_recv.at[b],
            device_id={"group": home, "dev": z * 2 + h},
            device_id_type=MESH,
        )

    for b in range(2):
        total = term(b, z)
        tail = folded(total)
        parts = [total[:, i * 128 : i * 128 + 128] for i in range(tiles)] + [tail]
        for part in range(2):
            for way in range(2):
                if hops[b][way] > 0:
                    s = hops[b][way] - 1
                    rs_copy(b, way, s, part).wait_recv()
                    for i in (2 * part, 2 * part + 1):
                        at = pl.ds(i * rows, rows if i < tiles else fold)
                        parts[i] = parts[i] + rs_rcv[b, way, s, at, :].astype(F32)
        tail = parts.pop()
        lane = iota((rows, 128), 1)
        tail = jnp.concatenate([tail, pltpu.roll(tail, pad, 1)[fold - again_at :]], axis=0)
        parts.append(jnp.where(lane < pad, tail, 0.0))
        total = jnp.concatenate([part.astype(BF16) for part in parts], axis=1)
        whole, extra = total[:main], total[main:]

        row = iota((main, BACK), 0)
        lane = iota((main, BACK), 1)
        q = jnp.bitwise_and(row, MAIN - 1)
        value = jnp.broadcast_to(score[4 * b : 4 * b + 1, :], (main, BACK))
        upper = value.astype(BF16).astype(F32)
        lower = value - upper
        slot = jnp.where(lane < main, lax.shift_right_logical(lane, 4), lax.shift_right_logical(lane - main, 1))
        fits = jnp.logical_and(lax.shift_right_logical(row, 4) == slot, lane < rows)
        value = jnp.where(q == MAIN - 2, upper, jnp.where(q == MAIN - 1, lower, 0.0))
        value = jnp.where(fits, value, 0.0).astype(BF16)
        a, l = iota((BACK, BACK), 0), iota((BACK, BACK), 1)
        number = jnp.where(a < main, jnp.bitwise_and(a, MAIN - 1), MAIN + jnp.bitwise_and(a, 1))
        carried = dot(value, flag(l == feats + number))

        again = flag(
            jnp.logical_and(
                lax.shift_right_logical(iota((main, 2 * nb), 0), 4)
                == lax.shift_right_logical(iota((main, 2 * nb), 1), 1),
                jnp.bitwise_and(iota((main, 2 * nb), 0), 1) == jnp.bitwise_and(iota((main, 2 * nb), 1), 1),
            )
        )
        extra = dot(again, extra)
        for h in range(2):
            lane = iota((main, WIDE), 1) - feats * h
            rr = lax.shift_right_logical(jnp.bitwise_and(iota((main, WIDE), 0), MAIN - 1), 1)
            mine = jnp.logical_and(lane >= rr * room, lane < rr * room + room)
            ends = jnp.where(jnp.logical_and(mine, lane < feats), extra, 0.0).astype(BF16)
            ret_snd[b, h] = (
                dot(whole, away[h, pl.ds(0, WIDE), :]) + dot(ends, away[h, pl.ds(WIDE, WIDE), :]) + carried
            ).astype(BF16)

        for i in range(nb):
            for h in range(2):

                def away_go(b=b, i=i, h=h):
                    ret_copy(b, i, h, ret_send.at[0]).start()

                if (b, i, h) == (own_b, own_slot, 0):
                    pl.when(c == 1)(away_go)
                else:
                    away_go()
        if b == own_b:

            @pl.when(c == 0)
            def _():
                pltpu.make_async_copy(
                    ret_snd.at[own_b, 0, pl.ds(own_slot * MAIN, MAIN), :],
                    ret_rcv.at[pl.ds(NX * MAIN, MAIN), :],
                    ret_recv.at[own_b],
                ).start()

    n_rows = nslot * MAIN
    total = 0.0
    sums = []
    for b in range(2):
        part = pl.ds(b * n_rows, n_rows)
        pltpu.make_async_copy(ret_rcv.at[part], ret_rcv.at[part], ret_recv.at[b]).wait()
        got = ret_rcv[part, :]
        end = got[:, BACK - 128 :]
        widen = flag(iota((128, BACK), 0) == 128 - room + jnp.bitwise_and(iota((128, BACK), 1), room - 1))
        mine = lax.shift_right_logical(
            jnp.bitwise_and(iota((n_rows, BACK), 0), MAIN - 1), 1
        ) == lax.shift_right_logical(iota((n_rows, BACK), 1), room.bit_length() - 1)
        wide = jnp.where(mine, dot(end, widen), 0.0).astype(BF16)
        total = total + dot_tn(got, pick[part, :]) + dot_tn(wide, pick2[part, :])
        a, r = iota((nslot, n_rows), 0), iota((nslot, n_rows), 1)
        this = a == lax.shift_right_logical(r, 4)
        r = jnp.bitwise_and(r, MAIN - 1)
        sums.append(
            dot(flag(jnp.logical_and(this, r == MAIN - 2)), end)
            + dot(flag(jnp.logical_and(this, r == MAIN - 1)), end)
        )
    out_ref[...] = total[:feats].astype(BF16)

    at = hits[...]
    score = jnp.concatenate(sums, axis=0)
    found = jnp.zeros((ngroup, toks), F32)
    for q in range(CAP):
        col = 128 - room + q
        found = jnp.where(at == float(q), jnp.broadcast_to(score[:, col : col + 1], found.shape), found)
    ids = ids_ref[...]
    for k in range(top):
        same = jnp.broadcast_to(ids[k : k + 1, :], (ngroup, toks)) == jnp.broadcast_to(e_col, (ngroup, toks))
        value = jnp.sum(jnp.where(same, found, 0.0), axis=0, keepdims=True)
        gp_ref[pl.ds(k, 1), :] = value / prob_ref[pl.ds(k, 1), :]

    most = 2 * nslot - 1
    part = snd.at[pl.ds(0, most * MAIN), :]
    pltpu.make_async_copy(part, part, fwd_send.at[0]).wait()
    for copy in swaps:
        copy.wait_send()
    for b in range(2):
        for way in range(2):
            for s in range(hops[b][way]):
                for part in range(2):
                    ag_copy(b, way, s, part).wait_send()
                    rs_copy(b, way, s, part).wait_send()
    for k in range(1, nz):
        sc_copy(k).wait_send()
    part = ret_rcv.at[pl.ds(0, most * MAIN), :]
    pltpu.make_async_copy(part, part, ret_send.at[0]).wait()

    @pl.when(c == 1)
    def _():
        one = snd.at[pl.ds(0, MAIN), :]
        pltpu.make_async_copy(one, one, fwd_send.at[1]).wait()
        one = ret_rcv.at[pl.ds(0, MAIN), :]
        pltpu.make_async_copy(one, one, ret_send.at[0]).wait()


def on_device(ny, nz, tokens, upstream, route_probs, expert_ids, w_gate, w_up, w_down):
    toks, feats = tokens.shape
    top = expert_ids.shape[1]
    wide_d, hid = w_gate.shape[1], w_gate.shape[2]
    ngroup = ny * NX
    nslot = ngroup // 2
    nb = nslot // 2
    main, rows = nb * MAIN, nb * CAP
    chunk = 2 * feats
    pad = WIDE - chunk
    half = nz // 2
    message = (WIDE // 128 - 1) * rows + -(-rows // 32) * 16
    dma = pltpu.SemaphoreType.DMA
    vmem = pl.BlockSpec(memory_space=pltpu.VMEM)
    hbm = pl.BlockSpec(memory_space=pltpu.HBM)
    out, gp = pl.pallas_call(
        functools.partial(kernel, ny, nz),
        out_shape=(jax.ShapeDtypeStruct((feats, toks), BF16), jax.ShapeDtypeStruct((top, toks), F32)),
        in_specs=[hbm] * 7,
        out_specs=(vmem, vmem),
        scratch_shapes=[
            pltpu.VMEM((top, toks), I32),
            pltpu.VMEM((top, toks), F32),
            pltpu.VMEM((2, WIDE, toks), BF16),
            pltpu.VMEM((ngroup * MAIN, WIDE), BF16),
            pltpu.VMEM((2, 2, main, WIDE), BF16),
            pltpu.VMEM((2, WIDE, 2 * chunk), BF16),
            pltpu.VMEM((2, 2 * WIDE, BACK), BF16),
            pltpu.VMEM((ngroup, toks), F32),
            pltpu.VMEM((ngroup * MAIN, toks), BF16),
            pltpu.VMEM((ngroup * MAIN, toks), BF16),
            pltpu.VMEM((2, nz, rows, 2 * chunk), BF16),
            pltpu.VMEM((wide_d + pad, 4 * hid), BF16),
            pltpu.VMEM((hid, wide_d), BF16),
            pltpu.VMEM((wide_d + pad, 2 * hid), BF16),
            pltpu.VMEM((2, rows, 4 * hid), F32),
            pltpu.VMEM((2, rows, 2 * hid), F32),
            pltpu.VMEM((2, rows, 4 * hid), BF16),
            pltpu.VMEM((2, 2, half, message, 128), BF16),
            pltpu.VMEM((2, 2, half, message, 128), BF16),
            pltpu.VMEM((nz, 8, BACK), F32),
            pltpu.VMEM((2, 2, main, BACK), BF16),
            pltpu.VMEM((ngroup * MAIN, BACK), BF16),
            dma((9,)),
            dma((3,)),
            dma((3,)),
            dma((2,)),
            dma((2,)),
            dma((2, 2, half, 2)),
            dma((2, 2, half, 2)),
            dma((2, 2, half, 2)),
            dma((2, 2, half, 2)),
            dma((nz,)),
            dma((nz,)),
            dma((1,)),
            dma((2,)),
        ],
        compiler_params=pltpu.CompilerParams(
            collective_id=0, has_side_effects=True, vmem_limit_bytes=60 * 1024 * 1024
        ),
    )(tokens.T, upstream.T, route_probs.T, expert_ids.T, w_gate[0], w_up[0], w_down[0])
    return out.T, gp.T


def solution(mesh):
    ny = mesh.shape["group"] // NX
    nz = mesh.shape["dev"] // 2
    placed = (
        P("group", "dev"),
        P("group", "dev"),
        P("group", None),
        P("group", None),
        P("group", None, "dev"),
        P("group", None, "dev"),
        P("group", "dev", None),
    )
    return jax.shard_map(
        functools.partial(on_device, ny, nz),
        mesh=mesh,
        in_specs=placed,
        out_specs=(P("group", "dev"), P("group", None)),
        check_vma=False,
    )
```

```python
import functools

import jax
import jax.numpy as jnp
from jax import lax
from jax.experimental import pallas as pl
from jax.experimental.pallas import tpu as pltpu
from jax.sharding import PartitionSpec as P

BF16 = jnp.bfloat16
F32 = jnp.float32
I32 = jnp.int32
MESH = pl.DeviceIdType.MESH

NX = 4
MAIN = 16
CAP = 18
WIDE = 512
BACK = 256


def iota(shape, axis):
    return lax.broadcasted_iota(I32, shape, axis)


def flag(mask):
    return jnp.where(mask, 1.0, 0.0).astype(BF16)


def dot(a, b):
    return lax.dot_general(a, b, (((1,), (0,)), ((), ())), preferred_element_type=F32)


def dot_nt(a, b):
    return lax.dot_general(a, b, (((1,), (1,)), ((), ())), preferred_element_type=F32)


def dot_tn(a, b):
    return lax.dot_general(a, b, (((0,), (0,)), ((), ())), preferred_element_type=F32)


def kernel(
    ny,
    nz,
    x_hbm,
    u_hbm,
    prob_hbm,
    ids_hbm,
    wg_hbm,
    wu_hbm,
    wd_hbm,
    out_ref,
    gp_ref,
    ids_ref,
    prob_ref,
    tt,
    snd,
    snd_n,
    rcv,
    rcv_n,
    place,
    away,
    hits,
    pick,
    pick2,
    ag,
    wgu,
    wdraw,
    wdt,
    acc_gu,
    acc_b,
    dgu,
    rs_snd,
    rs_rcv,
    scores,
    ret_snd,
    ret_rcv,
    load_sem,
    swap_send,
    swap_recv,
    fwd_send,
    fwd_recv,
    near_send,
    near_recv,
    nbr_send,
    nbr_recv,
    ag_send,
    ag_recv,
    rs_send,
    rs_recv,
    sc_send,
    sc_recv,
    ret_send,
    ret_recv,
):
    feats, toks = x_hbm.shape
    top = ids_hbm.shape[0]
    hid = wd_hbm.shape[0]
    wide_d = wd_hbm.shape[1]
    ngroup = ny * NX
    nslot = ngroup // 2
    nb = nslot // 2
    main = nb * MAIN
    rows = nb * CAP
    chunk = 2 * feats
    pad = WIDE - chunk

    g = lax.axis_index("group")
    d = lax.axis_index("dev")
    y, x = lax.div(g, NX), lax.rem(g, NX)
    z, c = lax.div(d, 2), lax.rem(d, 2)
    sib = {"group": g, "dev": z * 2 + 1 - c}

    ys = [lax.rem(y + k, ny) * NX for k in range(ny)]
    xs = [lax.rem(x + k, NX) for k in range(NX)]
    back_x = [lax.rem(x + 2 * NX - 2 * k - c, NX) for k in range(NX // 2)]

    def target(n):
        p, dx = n // NX, n % NX
        return p, dx, ys[(p + ny - 1) % ny] + xs[dx]

    def home_of(s):
        p, k = s // 2, s % 2
        return p * NX + 2 * k + c, ys[(1 - p) % ny] + back_x[k]

    loads = [
        pltpu.make_async_copy(ids_hbm, ids_ref, load_sem.at[0]),
        pltpu.make_async_copy(prob_hbm, prob_ref, load_sem.at[1]),
        pltpu.make_async_copy(x_hbm, tt.at[0, 0, pl.ds(0, feats), :], load_sem.at[2]),
        pltpu.make_async_copy(u_hbm, tt.at[0, 0, pl.ds(feats, feats), :], load_sem.at[3]),
        pltpu.make_async_copy(x_hbm, tt.at[0, 1, pl.ds(pad, feats), :], load_sem.at[4]),
        pltpu.make_async_copy(u_hbm, tt.at[0, 1, pl.ds(pad + feats, feats), :], load_sem.at[5]),
        pltpu.make_async_copy(wd_hbm, wdraw, load_sem.at[6]),
        pltpu.make_async_copy(wg_hbm, wgu.at[pl.ds(0, wide_d), pl.ds(0, hid)], load_sem.at[7]),
        pltpu.make_async_copy(wu_hbm, wgu.at[pl.ds(0, wide_d), pl.ds(2 * hid, hid)], load_sem.at[8]),
    ]
    for copy in loads:
        copy.start()

    barrier = pltpu.get_barrier_semaphore()

    for n in range(ngroup):
        p, dx, e = target(n)

        def hello(e=e, core=dx % 2):
            pl.semaphore_signal(barrier, inc=1, device_id={"group": e, "dev": z * 2 + core}, device_id_type=MESH)

        if n == NX:
            pl.when(c == 1)(hello)
        else:
            hello()
    for n in range(ngroup // 2):
        p, k = n // 2, n % 2
        e = ys[p] + lax.rem(x + 2 * k + c, NX)
        pl.semaphore_signal(barrier, inc=1, device_id={"group": e, "dev": z * 2 + 1 - c}, device_id_type=MESH)
    for k in range(1, nz):
        pl.semaphore_signal(
            barrier, inc=1, device_id={"group": g, "dev": lax.rem(z + k, nz) * 2 + c}, device_id_type=MESH
        )
    greeted = ngroup + nslot + nz - 1 - (1 - c)

    zero = jnp.zeros((pad, toks), BF16)
    for k in range(3):
        tt[k, 0, pl.ds(chunk, pad), :] = zero
        tt[k, 1, pl.ds(0, pad), :] = zero

    n_col = iota((ngroup, 1), 0)
    p_col = lax.shift_right_logical(n_col, 2)
    dx_col = jnp.bitwise_and(n_col, NX - 1)
    e_col = jnp.bitwise_and(y + p_col + ny - 1, ny - 1) * NX + jnp.bitwise_and(x + dx_col, NX - 1)
    loads[0].wait()
    loads[1].wait()
    ids = ids_ref[...]
    probs = prob_ref[...]
    hit = jnp.zeros((ngroup, toks), F32)
    prob_n = jnp.zeros((ngroup, toks), F32)
    for k in range(top):
        same = jnp.broadcast_to(ids[k : k + 1, :], (ngroup, toks)) == jnp.broadcast_to(e_col, (ngroup, toks))
        hit = hit + jnp.where(same, 1.0, 0.0)
        prob_n = prob_n + jnp.where(same, jnp.broadcast_to(probs[k : k + 1, :], (ngroup, toks)), 0.0)
    earlier = flag(iota((toks, toks), 0) < iota((toks, toks), 1))
    place_n = jnp.where(hit > 0.5, dot(hit.astype(BF16), earlier), -1.0)
    hits[...] = place_n
    place_bf = place_n.astype(BF16)
    part1 = prob_n.astype(BF16)
    rest = prob_n - part1.astype(F32)
    part2 = rest.astype(BF16)
    part3 = (rest - part2.astype(F32)).astype(BF16)

    step_rows = min(8, ngroup // 2) * MAIN

    def fill(k, i, to, first):
        base = pl.multiple_of(i * step_rows, step_rows)
        row = iota((step_rows, 1), 0)
        rr = jnp.bitwise_and(row, MAIN - 1)
        spread = flag(lax.shift_right_logical(base + iota((step_rows, ngroup), 0), 4) == iota((step_rows, ngroup), 1))
        at = dot(spread, place_bf)
        pr = dot(spread, part1) + dot(spread, part2) + dot(spread, part3)
        m1 = at == jnp.broadcast_to(rr.astype(F32), at.shape)
        m2 = at == jnp.broadcast_to((MAIN + jnp.bitwise_and(rr, 1)).astype(F32), at.shape)
        pick1 = flag(m1)
        pickx = flag(m2)
        if k == 0:
            pick[pl.ds(base, step_rows), :] = pick1
            pick2[pl.ds(base, step_rows), :] = pickx
        pr1 = jnp.sum(jnp.where(m1, pr, 0.0), axis=1, keepdims=True)
        pr2 = jnp.sum(jnp.where(m2, pr, 0.0), axis=1, keepdims=True)
        got = dot_nt(pick1, tt[k, 0])
        lane = iota((step_rows, WIDE), 1)
        got = jnp.where(jnp.logical_and(lane >= feats, lane < chunk), got * pr1, got)
        odd = dot_nt(pickx, tt[k, 0])
        even = dot_nt(pickx, tt[k, 1])
        part = lax.shift_right_logical(rr, 1)
        extra = jnp.zeros((step_rows, 128), F32)
        for tile in range(WIDE // 128):
            cut = slice(tile * 128, tile * 128 + 128)
            extra = jnp.where(part == 2 * tile, even[:, cut], extra)
            extra = jnp.where(part == 2 * tile + 1, odd[:, cut], extra)
        lane = iota((step_rows, 128), 1)
        extra = jnp.where(part * pad + lane - (128 - pad) >= feats, extra * pr2, extra)
        to[pl.ds(base, step_rows), pl.ds(first, WIDE - 128)] = got[:, : WIDE - 128].astype(BF16)
        to[pl.ds(base, step_rows), pl.ds(first + WIDE - 128, 128)] = jnp.where(
            lane >= 128 - pad, extra, got[:, WIDE - 128 :]
        ).astype(BF16)

    steps = ngroup * MAIN // step_rows

    def fill_batch(b, k):
        def one(i, carry):
            fill(k, i, snd if k == 0 else snd_n, 0 if k < 2 else WIDE)
            return carry

        lax.fori_loop(b * (steps // 2), (b + 1) * (steps // 2), one, 0)

    for copy in loads[2:6]:
        copy.wait()
    fill_batch(0, 0)
    pl.semaphore_wait(barrier, greeted)

    right = {"group": g, "dev": lax.rem(z + 1, nz) * 2 + c}
    left = {"group": g, "dev": lax.rem(z + nz - 1, nz) * 2 + c}
    mine = tt.at[0, 0, pl.ds(0, chunk), :]
    near = [
        pltpu.make_async_remote_copy(
            src_ref=mine,
            dst_ref=tt.at[k, 0, pl.ds(0, chunk), :],
            send_sem=near_send.at[k - 1],
            recv_sem=near_recv.at[k - 1],
            device_id=right if k == 1 else left,
            device_id_type=MESH,
        )
        for k in (1, 2)
    ]
    for copy in near:
        copy.start()

    def fwd_copy(n, b, sem, wide=False):
        p, dx, e = target(n)
        slot = p * 2 + dx // 2 - b * nb
        return pltpu.make_async_remote_copy(
            src_ref=(snd_n if wide else snd).at[pl.ds(n * MAIN, MAIN), :],
            dst_ref=(rcv_n if wide else rcv).at[b, c, pl.ds(slot * MAIN, MAIN), :],
            send_sem=sem,
            recv_sem=(nbr_recv if wide else fwd_recv).at[b],
            device_id={"group": e, "dev": z * 2 + dx % 2},
            device_id_type=MESH,
        )

    own_b, own_slot = (0, NX // 2) if ny > 2 else (1, 0)

    def send_batch(b, wide=False):
        sem = nbr_send if wide else fwd_send
        for n in range(b * nslot, (b + 1) * nslot):
            if n != NX:
                fwd_copy(n, b, sem.at[0], wide).start()
        if b == own_b:

            @pl.when(c == 0)
            def _():
                pltpu.make_async_copy(
                    (snd_n if wide else snd).at[pl.ds(NX * MAIN, MAIN), :],
                    (rcv_n if wide else rcv).at[own_b, 0, pl.ds(own_slot * MAIN, MAIN), :],
                    (nbr_recv if wide else fwd_recv).at[own_b],
                ).start()

            @pl.when(c == 1)
            def _():
                fwd_copy(NX, own_b, sem.at[1], wide).start()

    send_batch(0)

    swaps = [
        pltpu.make_async_remote_copy(
            src_ref=wg_hbm,
            dst_ref=wgu.at[pl.ds(0, wide_d), pl.ds(hid, hid)],
            send_sem=swap_send.at[0],
            recv_sem=swap_recv.at[0],
            device_id=sib,
            device_id_type=MESH,
        ),
        pltpu.make_async_remote_copy(
            src_ref=wu_hbm,
            dst_ref=wgu.at[pl.ds(0, wide_d), pl.ds(3 * hid, hid)],
            send_sem=swap_send.at[1],
            recv_sem=swap_recv.at[1],
            device_id=sib,
            device_id_type=MESH,
        ),
        pltpu.make_async_remote_copy(
            src_ref=wdt.at[pl.ds(pad, wide_d), pl.ds(0, hid)],
            dst_ref=wdt.at[pl.ds(pad, wide_d), pl.ds(hid, hid)],
            send_sem=swap_send.at[2],
            recv_sem=swap_recv.at[2],
            device_id=sib,
            device_id_type=MESH,
        ),
    ]
    swaps[0].start()
    swaps[1].start()
    fill_batch(1, 0)

    loads[6].wait()

    def turn(i, carry):
        base = pl.multiple_of(i * 128, 128)
        wdt[pl.ds(pl.multiple_of(base + pad, pad), 128), pl.ds(0, hid)] = wdraw[:, pl.ds(base, 128)].T
        return carry

    lax.fori_loop(0, wide_d // 128, turn, 0)
    swaps[2].start()

    for copy in near:
        copy.wait_recv()
    for k in (1, 2):
        tt[k, 1, pl.ds(pad, chunk), :] = tt[k, 0, pl.ds(0, chunk), :]
    for b in range(2):
        for k in (1, 2):
            fill_batch(b, k)
        send_batch(b, True)
    send_batch(1)

    wgu[pl.ds(wide_d, pad), :] = jnp.zeros((pad, 4 * hid), BF16)
    wdt[pl.ds(0, pad), :] = jnp.zeros((pad, 2 * hid), BF16)
    acc_gu[...] = jnp.zeros_like(acc_gu)
    acc_b[...] = jnp.zeros_like(acc_b)

    def set_place(i, carry):
        base = pl.multiple_of(i * 128, 128)
        a = base + iota((128, 2 * chunk), 0)
        f = iota((128, 2 * chunk), 1)
        goal = a + jnp.where(a >= feats, feats, 0)
        keep = a < chunk
        place[0, pl.ds(base, 128), :] = flag(jnp.logical_and(keep, f == goal))
        place[1, pl.ds(base, 128), :] = flag(jnp.logical_and(keep, f == goal + feats))
        return carry

    lax.fori_loop(0, WIDE // 128, set_place, 0)

    room = BACK - feats

    def set_away(h, carry):
        a, l = iota((WIDE, BACK), 0) - feats * h, iota((WIDE, BACK), 1)
        away[h, pl.ds(0, WIDE), :] = flag(jnp.logical_and(a == l, l < feats))
        inside = jnp.logical_and(a >= 0, a < feats)
        away[h, pl.ds(WIDE, WIDE), :] = flag(jnp.logical_and(inside, jnp.bitwise_and(a, room - 1) == l - feats))
        return carry

    def build(b):
        pltpu.make_async_copy(rcv.at[b], rcv.at[b], fwd_recv.at[b]).wait()
        arrange(b, z, rcv, 0)

    def build_next(b):
        pltpu.make_async_copy(rcv_n.at[b], rcv_n.at[b], nbr_recv.at[b]).wait()
        arrange(b, before, rcv_n, 0)
        arrange(b, after, rcv_n, WIDE)

    before, after = lax.rem(z + nz - 1, nz), lax.rem(z + 1, nz)

    def arrange(b, which, came, first):
        widen = flag(iota((128, WIDE), 0) == 128 - pad + jnp.bitwise_and(iota((128, WIDE), 1), pad - 1))
        mine = lax.shift_right_logical(jnp.bitwise_and(iota((main, WIDE), 0), MAIN - 1), 1) == lax.shift_right_logical(
            iota((main, WIDE), 1), pad.bit_length() - 1
        )
        a, r = iota((2 * nb, main), 0), iota((2 * nb, main), 1)
        gather = flag(
            jnp.logical_and(
                lax.shift_right_logical(a, 1) == lax.shift_right_logical(r, 4),
                jnp.bitwise_and(a, 1) == jnp.bitwise_and(r, 1),
            )
        )
        whole, extra = 0.0, 0.0
        for h in range(2):
            got = came[b, h, :, pl.ds(first, WIDE)]
            wide = jnp.where(mine, dot(got[:, WIDE - 128 :], widen), 0.0).astype(BF16)
            last = dot(gather, wide).astype(BF16)
            whole = whole + dot(got, place[h])
            extra = extra + dot(last, place[h])
        ag[b, which, pl.ds(0, main), :] = whole.astype(BF16)
        ag[b, which, pl.ds(main, 2 * nb), :] = extra.astype(BF16)

    half = nz // 2
    hops = [[half, nz - 1 - half], [nz - 1 - half, half]]
    ag_hops = [[half - 1, half - 2], [half - 2, half - 1]]

    fold = -(-rows // 32) * 16
    cuts = [pl.ds(0, fold), pl.ds(fold, rows - fold)]

    def ag_copy(b, way, s, part):
        which = lax.rem(z + 2 * nz - 1 - s, nz) if way == 0 else lax.rem(z + 1 + s, nz)
        return pltpu.make_async_remote_copy(
            src_ref=ag.at[b, which, cuts[part], :],
            dst_ref=ag.at[b, which, cuts[part], :],
            send_sem=ag_send.at[b, way, s, part],
            recv_sem=ag_recv.at[b, way, s, part],
            device_id=right if way == 0 else left,
            device_id_type=MESH,
        )

    def multiply(b, which):
        lane = iota((rows, 128), 1)
        mid = ag[b, which, :, pl.ds(WIDE - 128, 128)]
        none = jnp.zeros_like(mid)
        first = jnp.concatenate(
            [ag[b, which, :, pl.ds(0, WIDE - 128)], jnp.where(lane < 128 - pad, mid, none)], axis=1
        )
        second = jnp.concatenate(
            [jnp.where(lane >= 128 - pad, mid, none), ag[b, which, :, pl.ds(WIDE, WIDE - 128)]], axis=1
        )
        at = pl.ds(pl.multiple_of(which * chunk, pad), WIDE)
        acc_gu[b] += dot(first, wgu[at, :])
        acc_b[b] += dot(second, wdt[at, :])

    def ag_start(b, way):
        if ag_hops[b][way] > 0:
            for part in range(2):
                ag_copy(b, way, 0, part).start()

    def ag_pass(*which):
        for part in range(2):
            for b, way, s in which:
                if s < ag_hops[b][way]:
                    ag_copy(b, way, s, part).wait_recv()
                    if s + 1 < ag_hops[b][way]:
                        ag_copy(b, way, s + 1, part).start()

    def ag_use(b, way, s):
        if s < ag_hops[b][way]:
            multiply(b, lax.rem(z + 2 * nz - s - 2, nz) if way == 0 else lax.rem(z + s + 2, nz))

    tiles = WIDE // 128 - 1
    again_at = rows - fold
    halves = [pl.ds(0, 2 * rows), pl.ds(2 * rows, rs_snd.shape[3] - 2 * rows)]

    def rs_copy(b, way, s, part):
        return pltpu.make_async_remote_copy(
            src_ref=rs_snd.at[b, way, s, halves[part], :],
            dst_ref=rs_rcv.at[b, way, s, halves[part], :],
            send_sem=rs_send.at[b, way, s, part],
            recv_sem=rs_recv.at[b, way, s, part],
            device_id=right if way == 0 else left,
            device_id_type=MESH,
        )

    def term(b, which):
        return dot_nt(dgu[b], wgu[pl.ds(pl.multiple_of(which * chunk, pad), WIDE), :])

    def folded(total):
        tail = total[:, tiles * 128 :]
        lane = iota((fold, 128), 1)
        return jnp.where(lane < pad, tail[:fold], pltpu.roll(tail[again_at:], pad, 1))

    def rs_step(b, s):
        ways = [w for w in range(2) if s < hops[b][w]]
        totals = []
        for way in ways:
            over = hops[b][way] - s
            totals.append(term(b, lax.rem(z + over, nz) if way == 0 else lax.rem(z + nz - over, nz)))
        pieces = [[total[:, i * 128 : i * 128 + 128] for i in range(tiles)] + [folded(total)] for total in totals]
        for part in range(2):
            for way, piece in zip(ways, pieces):
                if s > 0:
                    rs_copy(b, way, s - 1, part).wait_recv()
                for i in (2 * part, 2 * part + 1):
                    at = pl.ds(i * rows, rows if i < tiles else fold)
                    value = piece[i]
                    if s > 0:
                        value = value + rs_rcv[b, way, s - 1, at, :].astype(F32)
                    rs_snd[b, way, s, at, :] = value.astype(BF16)
                rs_copy(b, way, s, part).start()

    def middle(b):
        gate, upper = acc_gu[b, :, pl.ds(0, 2 * hid)], acc_gu[b, :, pl.ds(2 * hid, 2 * hid)]
        back = acc_b[b]
        sig = 1.0 / (1.0 + jnp.exp(-gate))
        act = gate * sig
        slope = sig * (1.0 + gate * (1.0 - sig))
        dgu[b, :, pl.ds(0, 2 * hid)] = (back * upper * slope).astype(BF16)
        dgu[b, :, pl.ds(2 * hid, 2 * hid)] = (back * act).astype(BF16)
        acc_b[b] = act * upper * back

    def set_scores(b):
        row = lax.dot_general(
            jnp.ones((8, 2 * hid), F32),
            acc_b[b],
            (((1,), (1,)), ((), ())),
            preferred_element_type=F32,
            precision=lax.Precision.HIGHEST,
        )
        scores[z, pl.ds(4 * b, 4), pl.ds(0, rows)] = row[:4]

    def sc_copy(k):
        return pltpu.make_async_remote_copy(
            src_ref=scores.at[z],
            dst_ref=scores.at[z],
            send_sem=sc_send.at[k],
            recv_sem=sc_recv.at[k],
            device_id={"group": g, "dev": lax.rem(z + k, nz) * 2 + c},
            device_id_type=MESH,
        )

    build_next(0)
    ag_start(0, 0)
    ag_start(0, 1)
    build(0)
    scores[z] = jnp.zeros(scores.shape[1:], F32)
    lax.fori_loop(0, 2, set_away, 0)
    loads[7].wait()
    loads[8].wait()
    for copy in swaps:
        copy.wait_recv()
    for which in (z, before, after):
        multiply(0, which)

    last = half - 1
    ag_pass((0, 0, 0), (0, 1, 0))
    ag_use(0, 0, 0)
    ag_use(0, 1, 0)
    build_next(1)
    ag_start(1, 0)
    ag_start(1, 1)
    build(1)
    for which in (z, before, after):
        multiply(1, which)
    for s in range(1, last):
        ag_pass((0, 0, s), (0, 1, s))
        ag_use(0, 0, s)
        ag_use(0, 1, s)
        if s < last - 1:
            ag_pass((1, 0, s - 1), (1, 1, s - 1))
            ag_use(1, 0, s - 1)
            ag_use(1, 1, s - 1)
    middle(0)
    rs_step(0, 0)
    for s in range(max(last - 2, 0), last):
        ag_pass((1, 0, s), (1, 1, s))
        ag_use(1, 0, s)
        ag_use(1, 1, s)
        if s == max(last - 2, 0):
            set_scores(0)
    middle(1)
    rs_step(1, 0)
    if half > 1:
        rs_step(0, 1)
    set_scores(1)
    for k in range(1, nz):
        sc_copy(k).start()
    for s in range(1, half):
        rs_step(1, s)
        if s + 1 < half:
            rs_step(0, s + 1)

    for k in range(1, nz):
        sc_copy(k).wait_recv()
    score = scores[0]
    for k in range(1, nz):
        score = score + scores[k]

    def ret_copy(b, i, h, sem):
        n, home = home_of(b * nb + i)
        return pltpu.make_async_remote_copy(
            src_ref=ret_snd.at[b, h, pl.ds(i * MAIN, MAIN), :],
            dst_ref=ret_rcv.at[pl.ds(pl.multiple_of(n * MAIN, MAIN), MAIN), :],
            send_sem=sem,
            recv_sem=ret_recv.at[b],
            device_id={"group": home, "dev": z * 2 + h},
            device_id_type=MESH,
        )

    for b in range(2):
        total = term(b, z)
        tail = folded(total)
        parts = [total[:, i * 128 : i * 128 + 128] for i in range(tiles)] + [tail]
        for part in range(2):
            for way in range(2):
                if hops[b][way] > 0:
                    s = hops[b][way] - 1
                    rs_copy(b, way, s, part).wait_recv()
                    for i in (2 * part, 2 * part + 1):
                        at = pl.ds(i * rows, rows if i < tiles else fold)
                        parts[i] = parts[i] + rs_rcv[b, way, s, at, :].astype(F32)
        tail = parts.pop()
        lane = iota((rows, 128), 1)
        tail = jnp.concatenate([tail, pltpu.roll(tail, pad, 1)[fold - again_at :]], axis=0)
        parts.append(jnp.where(lane < pad, tail, 0.0))
        total = jnp.concatenate([part.astype(BF16) for part in parts], axis=1)
        whole, extra = total[:main], total[main:]

        row = iota((main, BACK), 0)
        lane = iota((main, BACK), 1)
        q = jnp.bitwise_and(row, MAIN - 1)
        value = jnp.broadcast_to(score[4 * b : 4 * b + 1, :], (main, BACK))
        upper = value.astype(BF16).astype(F32)
        lower = value - upper
        slot = jnp.where(lane < main, lax.shift_right_logical(lane, 4), lax.shift_right_logical(lane - main, 1))
        fits = jnp.logical_and(lax.shift_right_logical(row, 4) == slot, lane < rows)
        value = jnp.where(q == MAIN - 2, upper, jnp.where(q == MAIN - 1, lower, 0.0))
        value = jnp.where(fits, value, 0.0).astype(BF16)
        a, l = iota((BACK, BACK), 0), iota((BACK, BACK), 1)
        number = jnp.where(a < main, jnp.bitwise_and(a, MAIN - 1), MAIN + jnp.bitwise_and(a, 1))
        carried = dot(value, flag(l == feats + number))

        again = flag(
            jnp.logical_and(
                lax.shift_right_logical(iota((main, 2 * nb), 0), 4)
                == lax.shift_right_logical(iota((main, 2 * nb), 1), 1),
                jnp.bitwise_and(iota((main, 2 * nb), 0), 1) == jnp.bitwise_and(iota((main, 2 * nb), 1), 1),
            )
        )
        extra = dot(again, extra)
        for h in range(2):
            lane = iota((main, WIDE), 1) - feats * h
            rr = lax.shift_right_logical(jnp.bitwise_and(iota((main, WIDE), 0), MAIN - 1), 1)
            mine = jnp.logical_and(lane >= rr * room, lane < rr * room + room)
            ends = jnp.where(jnp.logical_and(mine, lane < feats), extra, 0.0).astype(BF16)
            ret_snd[b, h] = (
                dot(whole, away[h, pl.ds(0, WIDE), :]) + dot(ends, away[h, pl.ds(WIDE, WIDE), :]) + carried
            ).astype(BF16)

        for i in range(nb):
            for h in range(2):

                def away_go(b=b, i=i, h=h):
                    ret_copy(b, i, h, ret_send.at[0]).start()

                if (b, i, h) == (own_b, own_slot, 0):
                    pl.when(c == 1)(away_go)
                else:
                    away_go()
        if b == own_b:

            @pl.when(c == 0)
            def _():
                pltpu.make_async_copy(
                    ret_snd.at[own_b, 0, pl.ds(own_slot * MAIN, MAIN), :],
                    ret_rcv.at[pl.ds(NX * MAIN, MAIN), :],
                    ret_recv.at[own_b],
                ).start()

    n_rows = nslot * MAIN
    total = 0.0
    sums = []
    for b in range(2):
        part = pl.ds(b * n_rows, n_rows)
        pltpu.make_async_copy(ret_rcv.at[part], ret_rcv.at[part], ret_recv.at[b]).wait()
        got = ret_rcv[part, :]
        end = got[:, BACK - 128 :]
        widen = flag(iota((128, BACK), 0) == 128 - room + jnp.bitwise_and(iota((128, BACK), 1), room - 1))
        mine = lax.shift_right_logical(
            jnp.bitwise_and(iota((n_rows, BACK), 0), MAIN - 1), 1
        ) == lax.shift_right_logical(iota((n_rows, BACK), 1), room.bit_length() - 1)
        wide = jnp.where(mine, dot(end, widen), 0.0).astype(BF16)
        total = total + dot_tn(got, pick[part, :]) + dot_tn(wide, pick2[part, :])
        a, r = iota((nslot, n_rows), 0), iota((nslot, n_rows), 1)
        this = a == lax.shift_right_logical(r, 4)
        r = jnp.bitwise_and(r, MAIN - 1)
        sums.append(
            dot(flag(jnp.logical_and(this, r == MAIN - 2)), end)
            + dot(flag(jnp.logical_and(this, r == MAIN - 1)), end)
        )
    out_ref[...] = total[:feats].astype(BF16)

    at = hits[...]
    score = jnp.concatenate(sums, axis=0)
    found = jnp.zeros((ngroup, toks), F32)
    for q in range(CAP):
        col = 128 - room + q
        found = jnp.where(at == float(q), jnp.broadcast_to(score[:, col : col + 1], found.shape), found)
    ids = ids_ref[...]
    for k in range(top):
        same = jnp.broadcast_to(ids[k : k + 1, :], (ngroup, toks)) == jnp.broadcast_to(e_col, (ngroup, toks))
        value = jnp.sum(jnp.where(same, found, 0.0), axis=0, keepdims=True)
        gp_ref[pl.ds(k, 1), :] = value / prob_ref[pl.ds(k, 1), :]

    most = 2 * nslot - 1
    part = snd.at[pl.ds(0, most * MAIN), :]
    pltpu.make_async_copy(part, part, fwd_send.at[0]).wait()
    part = snd_n.at[pl.ds(0, most * MAIN), :]
    pltpu.make_async_copy(part, part, nbr_send.at[0]).wait()
    for copy in swaps + near:
        copy.wait_send()
    for b in range(2):
        for way in range(2):
            for s in range(hops[b][way]):
                for part in range(2):
                    rs_copy(b, way, s, part).wait_send()
            for s in range(ag_hops[b][way]):
                for part in range(2):
                    ag_copy(b, way, s, part).wait_send()
    for k in range(1, nz):
        sc_copy(k).wait_send()
    part = ret_rcv.at[pl.ds(0, most * MAIN), :]
    pltpu.make_async_copy(part, part, ret_send.at[0]).wait()

    @pl.when(c == 1)
    def _():
        one = snd.at[pl.ds(0, MAIN), :]
        pltpu.make_async_copy(one, one, fwd_send.at[1]).wait()
        one = snd_n.at[pl.ds(0, MAIN), :]
        pltpu.make_async_copy(one, one, nbr_send.at[1]).wait()
        one = ret_rcv.at[pl.ds(0, MAIN), :]
        pltpu.make_async_copy(one, one, ret_send.at[0]).wait()


def on_device(ny, nz, tokens, upstream, route_probs, expert_ids, w_gate, w_up, w_down):
    toks, feats = tokens.shape
    top = expert_ids.shape[1]
    wide_d, hid = w_gate.shape[1], w_gate.shape[2]
    ngroup = ny * NX
    nslot = ngroup // 2
    nb = nslot // 2
    main, rows = nb * MAIN, nb * CAP
    chunk = 2 * feats
    pad = WIDE - chunk
    half = nz // 2
    message = (WIDE // 128 - 1) * rows + -(-rows // 32) * 16
    dma = pltpu.SemaphoreType.DMA
    vmem = pl.BlockSpec(memory_space=pltpu.VMEM)
    hbm = pl.BlockSpec(memory_space=pltpu.HBM)
    out, gp = pl.pallas_call(
        functools.partial(kernel, ny, nz),
        out_shape=(jax.ShapeDtypeStruct((feats, toks), BF16), jax.ShapeDtypeStruct((top, toks), F32)),
        in_specs=[hbm] * 7,
        out_specs=(vmem, vmem),
        scratch_shapes=[
            pltpu.VMEM((top, toks), I32),
            pltpu.VMEM((top, toks), F32),
            pltpu.VMEM((3, 2, WIDE, toks), BF16),
            pltpu.VMEM((ngroup * MAIN, WIDE), BF16),
            pltpu.VMEM((ngroup * MAIN, 2 * WIDE), BF16),
            pltpu.VMEM((2, 2, main, WIDE), BF16),
            pltpu.VMEM((2, 2, main, 2 * WIDE), BF16),
            pltpu.VMEM((2, WIDE, 2 * chunk), BF16),
            pltpu.VMEM((2, 2 * WIDE, BACK), BF16),
            pltpu.VMEM((ngroup, toks), F32),
            pltpu.VMEM((ngroup * MAIN, toks), BF16),
            pltpu.VMEM((ngroup * MAIN, toks), BF16),
            pltpu.VMEM((2, nz, rows, 2 * chunk), BF16),
            pltpu.VMEM((wide_d + pad, 4 * hid), BF16),
            pltpu.VMEM((hid, wide_d), BF16),
            pltpu.VMEM((wide_d + pad, 2 * hid), BF16),
            pltpu.VMEM((2, rows, 4 * hid), F32),
            pltpu.VMEM((2, rows, 2 * hid), F32),
            pltpu.VMEM((2, rows, 4 * hid), BF16),
            pltpu.VMEM((2, 2, half, message, 128), BF16),
            pltpu.VMEM((2, 2, half, message, 128), BF16),
            pltpu.VMEM((nz, 8, BACK), F32),
            pltpu.VMEM((2, 2, main, BACK), BF16),
            pltpu.VMEM((ngroup * MAIN, BACK), BF16),
            dma((9,)),
            dma((3,)),
            dma((3,)),
            dma((2,)),
            dma((2,)),
            dma((2,)),
            dma((2,)),
            dma((2,)),
            dma((2,)),
            dma((2, 2, half, 2)),
            dma((2, 2, half, 2)),
            dma((2, 2, half, 2)),
            dma((2, 2, half, 2)),
            dma((nz,)),
            dma((nz,)),
            dma((1,)),
            dma((2,)),
        ],
        compiler_params=pltpu.CompilerParams(
            collective_id=0, has_side_effects=True, vmem_limit_bytes=60 * 1024 * 1024
        ),
    )(tokens.T, upstream.T, route_probs.T, expert_ids.T, w_gate[0], w_up[0], w_down[0])
    return out.T, gp.T


def solution(mesh):
    ny = mesh.shape["group"] // NX
    nz = mesh.shape["dev"] // 2
    placed = (
        P("group", "dev"),
        P("group", "dev"),
        P("group", None),
        P("group", None),
        P("group", None, "dev"),
        P("group", None, "dev"),
        P("group", "dev", None),
    )
    return jax.shard_map(
        functools.partial(on_device, ny, nz),
        mesh=mesh,
        in_specs=placed,
        out_specs=(P("group", "dev"), P("group", None)),
        check_vma=False,
    )
```

```python
import functools

import jax
import jax.numpy as jnp
from jax import lax
from jax.experimental import pallas as pl
from jax.experimental.pallas import tpu as pltpu
from jax.sharding import PartitionSpec as P

BF16 = jnp.bfloat16
F32 = jnp.float32
I32 = jnp.int32
MESH = pl.DeviceIdType.MESH

NX = 4
MAIN = 16
CAP = 18
WIDE = 512
BACK = 256


def iota(shape, axis):
    return lax.broadcasted_iota(I32, shape, axis)


def flag(mask):
    return jnp.where(mask, 1.0, 0.0).astype(BF16)


def dot(a, b):
    return lax.dot_general(a, b, (((1,), (0,)), ((), ())), preferred_element_type=F32)


def dot_nt(a, b):
    return lax.dot_general(a, b, (((1,), (1,)), ((), ())), preferred_element_type=F32)


def dot_tn(a, b):
    return lax.dot_general(a, b, (((0,), (0,)), ((), ())), preferred_element_type=F32)


def kernel(
    ny,
    nz,
    x_hbm,
    u_hbm,
    prob_hbm,
    ids_hbm,
    wg_hbm,
    wu_hbm,
    wd_hbm,
    out_ref,
    gp_ref,
    ids_ref,
    prob_ref,
    tt,
    snd,
    rcv,
    place,
    away,
    hits,
    pick,
    pick2,
    ag,
    wgu,
    wdraw,
    wdt,
    acc_gu,
    acc_b,
    dgu,
    rs_snd,
    rs_rcv,
    scores,
    ret_snd,
    ret_rcv,
    load_sem,
    swap_send,
    swap_recv,
    fwd_send,
    fwd_recv,
    ag_send,
    ag_recv,
    rs_send,
    rs_recv,
    sc_send,
    sc_recv,
    ret_send,
    ret_recv,
):
    feats, toks = x_hbm.shape
    top = ids_hbm.shape[0]
    hid = wd_hbm.shape[0]
    wide_d = wd_hbm.shape[1]
    ngroup = ny * NX
    nslot = ngroup // 2
    nb = nslot // 2
    main = nb * MAIN
    rows = nb * CAP
    chunk = 2 * feats
    pad = WIDE - chunk

    g = lax.axis_index("group")
    d = lax.axis_index("dev")
    y, x = lax.div(g, NX), lax.rem(g, NX)
    z, c = lax.div(d, 2), lax.rem(d, 2)
    sib = {"group": g, "dev": z * 2 + 1 - c}

    ys = [lax.rem(y + k, ny) * NX for k in range(ny)]
    xs = [lax.rem(x + k, NX) for k in range(NX)]
    back_x = [lax.rem(x + 2 * NX - 2 * k - c, NX) for k in range(NX // 2)]

    def target(n):
        p, dx = n // NX, n % NX
        return p, dx, ys[(p + ny - 1) % ny] + xs[dx]

    def home_of(s):
        p, k = s // 2, s % 2
        return p * NX + 2 * k + c, ys[(1 - p) % ny] + back_x[k]

    loads = [
        pltpu.make_async_copy(ids_hbm, ids_ref, load_sem.at[0]),
        pltpu.make_async_copy(prob_hbm, prob_ref, load_sem.at[1]),
        pltpu.make_async_copy(x_hbm, tt.at[0, pl.ds(0, feats), :], load_sem.at[2]),
        pltpu.make_async_copy(u_hbm, tt.at[0, pl.ds(feats, feats), :], load_sem.at[3]),
        pltpu.make_async_copy(x_hbm, tt.at[1, pl.ds(pad, feats), :], load_sem.at[4]),
        pltpu.make_async_copy(u_hbm, tt.at[1, pl.ds(pad + feats, feats), :], load_sem.at[5]),
        pltpu.make_async_copy(wd_hbm, wdraw, load_sem.at[6]),
        pltpu.make_async_copy(wg_hbm, wgu.at[pl.ds(0, wide_d), pl.ds(0, hid)], load_sem.at[7]),
        pltpu.make_async_copy(wu_hbm, wgu.at[pl.ds(0, wide_d), pl.ds(2 * hid, hid)], load_sem.at[8]),
    ]
    for copy in loads:
        copy.start()

    barrier = pltpu.get_barrier_semaphore()

    for n in range(ngroup):
        p, dx, e = target(n)

        def hello(e=e, core=dx % 2):
            pl.semaphore_signal(barrier, inc=1, device_id={"group": e, "dev": z * 2 + core}, device_id_type=MESH)

        if n == NX:
            pl.when(c == 1)(hello)
        else:
            hello()
    for n in range(ngroup // 2):
        p, k = n // 2, n % 2
        e = ys[p] + lax.rem(x + 2 * k + c, NX)
        pl.semaphore_signal(barrier, inc=1, device_id={"group": e, "dev": z * 2 + 1 - c}, device_id_type=MESH)
    for k in range(1, nz):
        pl.semaphore_signal(
            barrier, inc=1, device_id={"group": g, "dev": lax.rem(z + k, nz) * 2 + c}, device_id_type=MESH
        )
    greeted = ngroup + nslot + nz - 1 - (1 - c)

    zero = jnp.zeros((pad, toks), BF16)
    tt[0, pl.ds(chunk, pad), :] = zero
    tt[1, pl.ds(0, pad), :] = zero

    n_col = iota((ngroup, 1), 0)
    p_col = lax.shift_right_logical(n_col, 2)
    dx_col = jnp.bitwise_and(n_col, NX - 1)
    e_col = jnp.bitwise_and(y + p_col + ny - 1, ny - 1) * NX + jnp.bitwise_and(x + dx_col, NX - 1)
    loads[0].wait()
    loads[1].wait()
    ids = ids_ref[...]
    probs = prob_ref[...]
    hit = jnp.zeros((ngroup, toks), F32)
    prob_n = jnp.zeros((ngroup, toks), F32)
    for k in range(top):
        same = jnp.broadcast_to(ids[k : k + 1, :], (ngroup, toks)) == jnp.broadcast_to(e_col, (ngroup, toks))
        hit = hit + jnp.where(same, 1.0, 0.0)
        prob_n = prob_n + jnp.where(same, jnp.broadcast_to(probs[k : k + 1, :], (ngroup, toks)), 0.0)
    earlier = flag(iota((toks, toks), 0) < iota((toks, toks), 1))
    place_n = jnp.where(hit > 0.5, dot(hit.astype(BF16), earlier), -1.0)
    hits[...] = place_n
    place_bf = place_n.astype(BF16)
    part1 = prob_n.astype(BF16)
    rest = prob_n - part1.astype(F32)
    part2 = rest.astype(BF16)
    part3 = (rest - part2.astype(F32)).astype(BF16)

    step_rows = min(8, ngroup // 2) * MAIN

    def fill(i, carry):
        base = pl.multiple_of(i * step_rows, step_rows)
        row = iota((step_rows, 1), 0)
        rr = jnp.bitwise_and(row, MAIN - 1)
        spread = flag(lax.shift_right_logical(base + iota((step_rows, ngroup), 0), 4) == iota((step_rows, ngroup), 1))
        at = dot(spread, place_bf)
        pr = dot(spread, part1) + dot(spread, part2) + dot(spread, part3)
        m1 = at == jnp.broadcast_to(rr.astype(F32), at.shape)
        m2 = at == jnp.broadcast_to((MAIN + jnp.bitwise_and(rr, 1)).astype(F32), at.shape)
        pick1 = flag(m1)
        pickx = flag(m2)
        pick[pl.ds(base, step_rows), :] = pick1
        pick2[pl.ds(base, step_rows), :] = pickx
        pr1 = jnp.sum(jnp.where(m1, pr, 0.0), axis=1, keepdims=True)
        pr2 = jnp.sum(jnp.where(m2, pr, 0.0), axis=1, keepdims=True)
        got = dot_nt(pick1, tt[0])
        lane = iota((step_rows, WIDE), 1)
        got = jnp.where(jnp.logical_and(lane >= feats, lane < chunk), got * pr1, got)
        odd = dot_nt(pickx, tt[0])
        even = dot_nt(pickx, tt[1])
        part = lax.shift_right_logical(rr, 1)
        extra = jnp.zeros((step_rows, 128), F32)
        for tile in range(WIDE // 128):
            cut = slice(tile * 128, tile * 128 + 128)
            extra = jnp.where(part == 2 * tile, even[:, cut], extra)
            extra = jnp.where(part == 2 * tile + 1, odd[:, cut], extra)
        lane = iota((step_rows, 128), 1)
        extra = jnp.where(part * pad + lane - (128 - pad) >= feats, extra * pr2, extra)
        snd[pl.ds(base, step_rows), pl.ds(0, WIDE - 128)] = got[:, : WIDE - 128].astype(BF16)
        snd[pl.ds(base, step_rows), pl.ds(WIDE - 128, 128)] = jnp.where(
            lane >= 128 - pad, extra, got[:, WIDE - 128 :]
        ).astype(BF16)
        return carry

    for copy in loads[2:6]:
        copy.wait()
    steps = ngroup * MAIN // step_rows
    lax.fori_loop(0, steps // 2, fill, 0)
    pl.semaphore_wait(barrier, greeted)

    def fwd_copy(n, b, sem):
        p, dx, e = target(n)
        slot = p * 2 + dx // 2 - b * nb
        return pltpu.make_async_remote_copy(
            src_ref=snd.at[pl.ds(n * MAIN, MAIN), :],
            dst_ref=rcv.at[b, c, pl.ds(slot * MAIN, MAIN), :],
            send_sem=sem,
            recv_sem=fwd_recv.at[b],
            device_id={"group": e, "dev": z * 2 + dx % 2},
            device_id_type=MESH,
        )

    own_b, own_slot = (0, NX // 2) if ny > 2 else (1, 0)

    def send_batch(b):
        for n in range(b * nslot, (b + 1) * nslot):
            if n != NX:
                fwd_copy(n, b, fwd_send.at[0]).start()
        if b == own_b:

            @pl.when(c == 0)
            def _():
                pltpu.make_async_copy(
                    snd.at[pl.ds(NX * MAIN, MAIN), :],
                    rcv.at[own_b, 0, pl.ds(own_slot * MAIN, MAIN), :],
                    fwd_recv.at[own_b],
                ).start()

            @pl.when(c == 1)
            def _():
                fwd_copy(NX, own_b, fwd_send.at[1]).start()

    send_batch(0)
    lax.fori_loop(steps // 2, steps, fill, 0)

    swaps = [
        pltpu.make_async_remote_copy(
            src_ref=wg_hbm,
            dst_ref=wgu.at[pl.ds(0, wide_d), pl.ds(hid, hid)],
            send_sem=swap_send.at[0],
            recv_sem=swap_recv.at[0],
            device_id=sib,
            device_id_type=MESH,
        ),
        pltpu.make_async_remote_copy(
            src_ref=wu_hbm,
            dst_ref=wgu.at[pl.ds(0, wide_d), pl.ds(3 * hid, hid)],
            send_sem=swap_send.at[1],
            recv_sem=swap_recv.at[1],
            device_id=sib,
            device_id_type=MESH,
        ),
        pltpu.make_async_remote_copy(
            src_ref=wdt.at[pl.ds(pad, wide_d), pl.ds(0, hid)],
            dst_ref=wdt.at[pl.ds(pad, wide_d), pl.ds(hid, hid)],
            send_sem=swap_send.at[2],
            recv_sem=swap_recv.at[2],
            device_id=sib,
            device_id_type=MESH,
        ),
    ]
    swaps[0].start()
    swaps[1].start()

    loads[6].wait()

    def turn(i, carry):
        base = pl.multiple_of(i * 128, 128)
        wdt[pl.ds(pl.multiple_of(base + pad, pad), 128), pl.ds(0, hid)] = wdraw[:, pl.ds(base, 128)].T
        return carry

    lax.fori_loop(0, wide_d // 128, turn, 0)
    swaps[2].start()
    send_batch(1)

    wgu[pl.ds(wide_d, pad), :] = jnp.zeros((pad, 4 * hid), BF16)
    wdt[pl.ds(0, pad), :] = jnp.zeros((pad, 2 * hid), BF16)
    acc_gu[...] = jnp.zeros_like(acc_gu)
    acc_b[...] = jnp.zeros_like(acc_b)

    def set_place(i, carry):
        base = pl.multiple_of(i * 128, 128)
        a = base + iota((128, 2 * chunk), 0)
        f = iota((128, 2 * chunk), 1)
        goal = a + jnp.where(a >= feats, feats, 0)
        keep = a < chunk
        place[0, pl.ds(base, 128), :] = flag(jnp.logical_and(keep, f == goal))
        place[1, pl.ds(base, 128), :] = flag(jnp.logical_and(keep, f == goal + feats))
        return carry

    lax.fori_loop(0, WIDE // 128, set_place, 0)

    room = BACK - feats

    def set_away(h, carry):
        a, l = iota((WIDE, BACK), 0) - feats * h, iota((WIDE, BACK), 1)
        away[h, pl.ds(0, WIDE), :] = flag(jnp.logical_and(a == l, l < feats))
        inside = jnp.logical_and(a >= 0, a < feats)
        away[h, pl.ds(WIDE, WIDE), :] = flag(jnp.logical_and(inside, jnp.bitwise_and(a, room - 1) == l - feats))
        return carry

    def build(b):
        pltpu.make_async_copy(rcv.at[b], rcv.at[b], fwd_recv.at[b]).wait()
        widen = flag(iota((128, WIDE), 0) == 128 - pad + jnp.bitwise_and(iota((128, WIDE), 1), pad - 1))
        mine = lax.shift_right_logical(jnp.bitwise_and(iota((main, WIDE), 0), MAIN - 1), 1) == lax.shift_right_logical(
            iota((main, WIDE), 1), pad.bit_length() - 1
        )
        a, r = iota((2 * nb, main), 0), iota((2 * nb, main), 1)
        gather = flag(
            jnp.logical_and(
                lax.shift_right_logical(a, 1) == lax.shift_right_logical(r, 4),
                jnp.bitwise_and(a, 1) == jnp.bitwise_and(r, 1),
            )
        )
        whole, extra = 0.0, 0.0
        for h in range(2):
            got = rcv[b, h]
            wide = jnp.where(mine, dot(got[:, WIDE - 128 :], widen), 0.0).astype(BF16)
            last = dot(gather, wide).astype(BF16)
            whole = whole + dot(got, place[h])
            extra = extra + dot(last, place[h])
        ag[b, z, pl.ds(0, main), :] = whole.astype(BF16)
        ag[b, z, pl.ds(main, 2 * nb), :] = extra.astype(BF16)

    turn_to = 1 - 2 * c
    right = {"group": g, "dev": lax.rem(z + nz + turn_to, nz) * 2 + c}
    left = {"group": g, "dev": lax.rem(z + nz - turn_to, nz) * 2 + c}

    def along(k):
        return lax.rem(z + 2 * nz + k * turn_to, nz)

    half = nz // 2
    hops = [[half, nz - 1 - half], [nz - 1 - half, half]]

    fold = -(-rows // 32) * 16
    cuts = [pl.ds(0, fold), pl.ds(fold, rows - fold)]

    def ag_copy(b, way, s, part):
        which = along(-s) if way == 0 else along(s)
        return pltpu.make_async_remote_copy(
            src_ref=ag.at[b, which, cuts[part], :],
            dst_ref=ag.at[b, which, cuts[part], :],
            send_sem=ag_send.at[b, way, s, part],
            recv_sem=ag_recv.at[b, way, s, part],
            device_id=right if way == 0 else left,
            device_id_type=MESH,
        )

    def multiply(b, which):
        lane = iota((rows, 128), 1)
        mid = ag[b, which, :, pl.ds(WIDE - 128, 128)]
        none = jnp.zeros_like(mid)
        first = jnp.concatenate(
            [ag[b, which, :, pl.ds(0, WIDE - 128)], jnp.where(lane < 128 - pad, mid, none)], axis=1
        )
        second = jnp.concatenate(
            [jnp.where(lane >= 128 - pad, mid, none), ag[b, which, :, pl.ds(WIDE, WIDE - 128)]], axis=1
        )
        at = pl.ds(pl.multiple_of(which * chunk, pad), WIDE)
        acc_gu[b] += dot(first, wgu[at, :])
        acc_b[b] += dot(second, wdt[at, :])

    def ag_start(b, way):
        if hops[b][way] > 0:
            for part in range(2):
                ag_copy(b, way, 0, part).start()

    def ag_pass(*which):
        for part in range(2):
            for b, way, s in which:
                if s < hops[b][way]:
                    ag_copy(b, way, s, part).wait_recv()
                    if s + 1 < hops[b][way]:
                        ag_copy(b, way, s + 1, part).start()

    def ag_use(b, way, s):
        if s < hops[b][way]:
            multiply(b, along(-s - 1) if way == 0 else along(s + 1))

    tiles = WIDE // 128 - 1
    again_at = rows - fold
    halves = [pl.ds(0, 2 * rows), pl.ds(2 * rows, rs_snd.shape[3] - 2 * rows)]

    def rs_copy(b, way, s, part):
        return pltpu.make_async_remote_copy(
            src_ref=rs_snd.at[b, way, s, halves[part], :],
            dst_ref=rs_rcv.at[b, way, s, halves[part], :],
            send_sem=rs_send.at[b, way, s, part],
            recv_sem=rs_recv.at[b, way, s, part],
            device_id=right if way == 0 else left,
            device_id_type=MESH,
        )

    def term(b, which):
        return dot_nt(dgu[b], wgu[pl.ds(pl.multiple_of(which * chunk, pad), WIDE), :])

    def folded(total):
        tail = total[:, tiles * 128 :]
        lane = iota((fold, 128), 1)
        return jnp.where(lane < pad, tail[:fold], pltpu.roll(tail[again_at:], pad, 1))

    def rs_step(b, s):
        ways = [w for w in range(2) if s < hops[b][w]]
        totals = []
        for way in ways:
            over = hops[b][way] - s
            totals.append(term(b, along(over) if way == 0 else along(-over)))
        pieces = [[total[:, i * 128 : i * 128 + 128] for i in range(tiles)] + [folded(total)] for total in totals]
        for part in range(2):
            for way, piece in zip(ways, pieces):
                if s > 0:
                    rs_copy(b, way, s - 1, part).wait_recv()
                for i in (2 * part, 2 * part + 1):
                    at = pl.ds(i * rows, rows if i < tiles else fold)
                    value = piece[i]
                    if s > 0:
                        value = value + rs_rcv[b, way, s - 1, at, :].astype(F32)
                    rs_snd[b, way, s, at, :] = value.astype(BF16)
                rs_copy(b, way, s, part).start()

    def middle(b):
        gate, upper = acc_gu[b, :, pl.ds(0, 2 * hid)], acc_gu[b, :, pl.ds(2 * hid, 2 * hid)]
        back = acc_b[b]
        sig = 1.0 / (1.0 + jnp.exp(-gate))
        act = gate * sig
        slope = sig * (1.0 + gate * (1.0 - sig))
        dgu[b, :, pl.ds(0, 2 * hid)] = (back * upper * slope).astype(BF16)
        dgu[b, :, pl.ds(2 * hid, 2 * hid)] = (back * act).astype(BF16)
        acc_b[b] = act * upper * back

    def set_scores(b):
        row = lax.dot_general(
            jnp.ones((8, 2 * hid), F32),
            acc_b[b],
            (((1,), (1,)), ((), ())),
            preferred_element_type=F32,
            precision=lax.Precision.HIGHEST,
        )
        scores[z, pl.ds(4 * b, 4), pl.ds(0, rows)] = row[:4]

    def sc_copy(k):
        return pltpu.make_async_remote_copy(
            src_ref=scores.at[z],
            dst_ref=scores.at[z],
            send_sem=sc_send.at[k],
            recv_sem=sc_recv.at[k],
            device_id={"group": g, "dev": lax.rem(z + k, nz) * 2 + c},
            device_id_type=MESH,
        )

    build(0)
    ag_start(0, 0)
    ag_start(0, 1)
    scores[z] = jnp.zeros(scores.shape[1:], F32)
    lax.fori_loop(0, 2, set_away, 0)
    loads[7].wait()
    loads[8].wait()
    for copy in swaps:
        copy.wait_recv()
    multiply(0, z)

    ag_pass((0, 0, 0), (0, 1, 0))
    ag_use(0, 0, 0)
    ag_use(0, 1, 0)
    build(1)
    ag_start(1, 0)
    ag_start(1, 1)
    multiply(1, z)
    for s in range(1, half):
        ag_pass((0, 0, s), (0, 1, s))
        ag_use(0, 0, s)
        ag_use(0, 1, s)
        if s < half - 1:
            ag_pass((1, 0, s - 1), (1, 1, s - 1))
            ag_use(1, 0, s - 1)
            ag_use(1, 1, s - 1)
    middle(0)
    rs_step(0, 0)
    for s in range(max(half - 2, 0), half):
        ag_pass((1, 0, s), (1, 1, s))
        ag_use(1, 0, s)
        ag_use(1, 1, s)
        if s == half - 2:
            set_scores(0)
    if half == 1:
        set_scores(0)
    middle(1)
    rs_step(1, 0)
    if half > 1:
        rs_step(0, 1)
    set_scores(1)
    for k in range(1, nz):
        sc_copy(k).start()
    for s in range(1, half):
        rs_step(1, s)
        if s + 1 < half:
            rs_step(0, s + 1)

    for k in range(1, nz):
        sc_copy(k).wait_recv()
    score = scores[0]
    for k in range(1, nz):
        score = score + scores[k]

    def ret_copy(b, i, h, sem):
        n, home = home_of(b * nb + i)
        return pltpu.make_async_remote_copy(
            src_ref=ret_snd.at[b, h, pl.ds(i * MAIN, MAIN), :],
            dst_ref=ret_rcv.at[pl.ds(pl.multiple_of(n * MAIN, MAIN), MAIN), :],
            send_sem=sem,
            recv_sem=ret_recv.at[b],
            device_id={"group": home, "dev": z * 2 + h},
            device_id_type=MESH,
        )

    for b in range(2):
        total = term(b, z)
        tail = folded(total)
        parts = [total[:, i * 128 : i * 128 + 128] for i in range(tiles)] + [tail]
        for part in range(2):
            for way in range(2):
                if hops[b][way] > 0:
                    s = hops[b][way] - 1
                    rs_copy(b, way, s, part).wait_recv()
                    for i in (2 * part, 2 * part + 1):
                        at = pl.ds(i * rows, rows if i < tiles else fold)
                        parts[i] = parts[i] + rs_rcv[b, way, s, at, :].astype(F32)
        tail = parts.pop()
        lane = iota((rows, 128), 1)
        tail = jnp.concatenate([tail, pltpu.roll(tail, pad, 1)[fold - again_at :]], axis=0)
        parts.append(jnp.where(lane < pad, tail, 0.0))
        total = jnp.concatenate([part.astype(BF16) for part in parts], axis=1)
        whole, extra = total[:main], total[main:]

        row = iota((main, BACK), 0)
        lane = iota((main, BACK), 1)
        q = jnp.bitwise_and(row, MAIN - 1)
        value = jnp.broadcast_to(score[4 * b : 4 * b + 1, :], (main, BACK))
        upper = value.astype(BF16).astype(F32)
        lower = value - upper
        slot = jnp.where(lane < main, lax.shift_right_logical(lane, 4), lax.shift_right_logical(lane - main, 1))
        fits = jnp.logical_and(lax.shift_right_logical(row, 4) == slot, lane < rows)
        value = jnp.where(q == MAIN - 2, upper, jnp.where(q == MAIN - 1, lower, 0.0))
        value = jnp.where(fits, value, 0.0).astype(BF16)
        a, l = iota((BACK, BACK), 0), iota((BACK, BACK), 1)
        number = jnp.where(a < main, jnp.bitwise_and(a, MAIN - 1), MAIN + jnp.bitwise_and(a, 1))
        carried = dot(value, flag(l == feats + number))

        again = flag(
            jnp.logical_and(
                lax.shift_right_logical(iota((main, 2 * nb), 0), 4)
                == lax.shift_right_logical(iota((main, 2 * nb), 1), 1),
                jnp.bitwise_and(iota((main, 2 * nb), 0), 1) == jnp.bitwise_and(iota((main, 2 * nb), 1), 1),
            )
        )
        extra = dot(again, extra)
        for h in range(2):
            lane = iota((main, WIDE), 1) - feats * h
            rr = lax.shift_right_logical(jnp.bitwise_and(iota((main, WIDE), 0), MAIN - 1), 1)
            mine = jnp.logical_and(lane >= rr * room, lane < rr * room + room)
            ends = jnp.where(jnp.logical_and(mine, lane < feats), extra, 0.0).astype(BF16)
            ret_snd[b, h] = (
                dot(whole, away[h, pl.ds(0, WIDE), :]) + dot(ends, away[h, pl.ds(WIDE, WIDE), :]) + carried
            ).astype(BF16)

        for i in range(nb):
            for h in range(2):

                def away_go(b=b, i=i, h=h):
                    ret_copy(b, i, h, ret_send.at[0]).start()

                if (b, i, h) == (own_b, own_slot, 0):
                    pl.when(c == 1)(away_go)
                else:
                    away_go()
        if b == own_b:

            @pl.when(c == 0)
            def _():
                pltpu.make_async_copy(
                    ret_snd.at[own_b, 0, pl.ds(own_slot * MAIN, MAIN), :],
                    ret_rcv.at[pl.ds(NX * MAIN, MAIN), :],
                    ret_recv.at[own_b],
                ).start()

    n_rows = nslot * MAIN
    total = 0.0
    sums = []
    for b in range(2):
        part = pl.ds(b * n_rows, n_rows)
        pltpu.make_async_copy(ret_rcv.at[part], ret_rcv.at[part], ret_recv.at[b]).wait()
        got = ret_rcv[part, :]
        end = got[:, BACK - 128 :]
        widen = flag(iota((128, BACK), 0) == 128 - room + jnp.bitwise_and(iota((128, BACK), 1), room - 1))
        mine = lax.shift_right_logical(
            jnp.bitwise_and(iota((n_rows, BACK), 0), MAIN - 1), 1
        ) == lax.shift_right_logical(iota((n_rows, BACK), 1), room.bit_length() - 1)
        wide = jnp.where(mine, dot(end, widen), 0.0).astype(BF16)
        total = total + dot_tn(got, pick[part, :]) + dot_tn(wide, pick2[part, :])
        a, r = iota((nslot, n_rows), 0), iota((nslot, n_rows), 1)
        this = a == lax.shift_right_logical(r, 4)
        r = jnp.bitwise_and(r, MAIN - 1)
        sums.append(
            dot(flag(jnp.logical_and(this, r == MAIN - 2)), end)
            + dot(flag(jnp.logical_and(this, r == MAIN - 1)), end)
        )
    out_ref[...] = total[:feats].astype(BF16)

    at = hits[...]
    score = jnp.concatenate(sums, axis=0)
    found = jnp.zeros((ngroup, toks), F32)
    for q in range(CAP):
        col = 128 - room + q
        found = jnp.where(at == float(q), jnp.broadcast_to(score[:, col : col + 1], found.shape), found)
    ids = ids_ref[...]
    for k in range(top):
        same = jnp.broadcast_to(ids[k : k + 1, :], (ngroup, toks)) == jnp.broadcast_to(e_col, (ngroup, toks))
        value = jnp.sum(jnp.where(same, found, 0.0), axis=0, keepdims=True)
        gp_ref[pl.ds(k, 1), :] = value / prob_ref[pl.ds(k, 1), :]

    most = 2 * nslot - 1
    part = snd.at[pl.ds(0, most * MAIN), :]
    pltpu.make_async_copy(part, part, fwd_send.at[0]).wait()
    for copy in swaps:
        copy.wait_send()
    for b in range(2):
        for way in range(2):
            for s in range(hops[b][way]):
                for part in range(2):
                    ag_copy(b, way, s, part).wait_send()
                    rs_copy(b, way, s, part).wait_send()
    for k in range(1, nz):
        sc_copy(k).wait_send()
    part = ret_rcv.at[pl.ds(0, most * MAIN), :]
    pltpu.make_async_copy(part, part, ret_send.at[0]).wait()

    @pl.when(c == 1)
    def _():
        one = snd.at[pl.ds(0, MAIN), :]
        pltpu.make_async_copy(one, one, fwd_send.at[1]).wait()
        one = ret_rcv.at[pl.ds(0, MAIN), :]
        pltpu.make_async_copy(one, one, ret_send.at[0]).wait()


def on_device(ny, nz, tokens, upstream, route_probs, expert_ids, w_gate, w_up, w_down):
    toks, feats = tokens.shape
    top = expert_ids.shape[1]
    wide_d, hid = w_gate.shape[1], w_gate.shape[2]
    ngroup = ny * NX
    nslot = ngroup // 2
    nb = nslot // 2
    main, rows = nb * MAIN, nb * CAP
    chunk = 2 * feats
    pad = WIDE - chunk
    half = nz // 2
    message = (WIDE // 128 - 1) * rows + -(-rows // 32) * 16
    dma = pltpu.SemaphoreType.DMA
    vmem = pl.BlockSpec(memory_space=pltpu.VMEM)
    hbm = pl.BlockSpec(memory_space=pltpu.HBM)
    out, gp = pl.pallas_call(
        functools.partial(kernel, ny, nz),
        out_shape=(jax.ShapeDtypeStruct((feats, toks), BF16), jax.ShapeDtypeStruct((top, toks), F32)),
        in_specs=[hbm] * 7,
        out_specs=(vmem, vmem),
        scratch_shapes=[
            pltpu.VMEM((top, toks), I32),
            pltpu.VMEM((top, toks), F32),
            pltpu.VMEM((2, WIDE, toks), BF16),
            pltpu.VMEM((ngroup * MAIN, WIDE), BF16),
            pltpu.VMEM((2, 2, main, WIDE), BF16),
            pltpu.VMEM((2, WIDE, 2 * chunk), BF16),
            pltpu.VMEM((2, 2 * WIDE, BACK), BF16),
            pltpu.VMEM((ngroup, toks), F32),
            pltpu.VMEM((ngroup * MAIN, toks), BF16),
            pltpu.VMEM((ngroup * MAIN, toks), BF16),
            pltpu.VMEM((2, nz, rows, 2 * chunk), BF16),
            pltpu.VMEM((wide_d + pad, 4 * hid), BF16),
            pltpu.VMEM((hid, wide_d), BF16),
            pltpu.VMEM((wide_d + pad, 2 * hid), BF16),
            pltpu.VMEM((2, rows, 4 * hid), F32),
            pltpu.VMEM((2, rows, 2 * hid), F32),
            pltpu.VMEM((2, rows, 4 * hid), BF16),
            pltpu.VMEM((2, 2, half, message, 128), BF16),
            pltpu.VMEM((2, 2, half, message, 128), BF16),
            pltpu.VMEM((nz, 8, BACK), F32),
            pltpu.VMEM((2, 2, main, BACK), BF16),
            pltpu.VMEM((ngroup * MAIN, BACK), BF16),
            dma((9,)),
            dma((3,)),
            dma((3,)),
            dma((2,)),
            dma((2,)),
            dma((2, 2, half, 2)),
            dma((2, 2, half, 2)),
            dma((2, 2, half, 2)),
            dma((2, 2, half, 2)),
            dma((nz,)),
            dma((nz,)),
            dma((1,)),
            dma((2,)),
        ],
        compiler_params=pltpu.CompilerParams(
            collective_id=0, has_side_effects=True, vmem_limit_bytes=60 * 1024 * 1024
        ),
    )(tokens.T, upstream.T, route_probs.T, expert_ids.T, w_gate[0], w_up[0], w_down[0])
    return out.T, gp.T


def solution(mesh):
    ny = mesh.shape["group"] // NX
    nz = mesh.shape["dev"] // 2
    placed = (
        P("group", "dev"),
        P("group", "dev"),
        P("group", None),
        P("group", None),
        P("group", None, "dev"),
        P("group", None, "dev"),
        P("group", "dev", None),
    )
    return jax.shard_map(
        functools.partial(on_device, ny, nz),
        mesh=mesh,
        in_specs=placed,
        out_specs=(P("group", "dev"), P("group", None)),
        check_vma=False,
    )
```

```python
import functools

import jax
import jax.numpy as jnp
from jax import lax
from jax.experimental import pallas as pl
from jax.experimental.pallas import tpu as pltpu
from jax.sharding import PartitionSpec as P

BF16 = jnp.bfloat16
F32 = jnp.float32
I32 = jnp.int32
MESH = pl.DeviceIdType.MESH

NX = 4
MAIN = 16
CAP = 18
WIDE = 512
BACK = 256


def iota(shape, axis):
    return lax.broadcasted_iota(I32, shape, axis)


def flag(mask):
    return jnp.where(mask, 1.0, 0.0).astype(BF16)


def dot(a, b):
    return lax.dot_general(a, b, (((1,), (0,)), ((), ())), preferred_element_type=F32)


def dot_nt(a, b):
    return lax.dot_general(a, b, (((1,), (1,)), ((), ())), preferred_element_type=F32)


def dot_tn(a, b):
    return lax.dot_general(a, b, (((0,), (0,)), ((), ())), preferred_element_type=F32)


def kernel(
    ny,
    nz,
    x_hbm,
    u_hbm,
    prob_hbm,
    ids_hbm,
    wg_hbm,
    wu_hbm,
    wd_hbm,
    out_ref,
    gp_ref,
    ids_ref,
    prob_ref,
    tt,
    snd,
    rcv,
    place,
    away,
    hits,
    pick,
    pick2,
    ag,
    wgu,
    wdraw,
    wdt,
    acc_gu,
    acc_b,
    dgu,
    rs_snd,
    rs_rcv,
    scores,
    ret_snd,
    ret_rcv,
    load_sem,
    swap_send,
    swap_recv,
    fwd_send,
    fwd_recv,
    ag_send,
    ag_recv,
    rs_send,
    rs_recv,
    sc_send,
    sc_recv,
    ret_send,
    ret_recv,
):
    feats, toks = x_hbm.shape
    top = ids_hbm.shape[0]
    hid = wd_hbm.shape[0]
    wide_d = wd_hbm.shape[1]
    ngroup = ny * NX
    nslot = ngroup // 2
    nb = nslot // 2
    main = nb * MAIN
    rows = nb * CAP
    chunk = 2 * feats
    pad = WIDE - chunk

    g = lax.axis_index("group")
    d = lax.axis_index("dev")
    y, x = lax.div(g, NX), lax.rem(g, NX)
    z, c = lax.div(d, 2), lax.rem(d, 2)
    sib = {"group": g, "dev": z * 2 + 1 - c}

    ys = [lax.rem(y + k, ny) * NX for k in range(ny)]
    xs = [lax.rem(x + k, NX) for k in range(NX)]
    back_x = [lax.rem(x + 2 * NX - 2 * k - c, NX) for k in range(NX // 2)]

    def target(n):
        p, dx = n // NX, n % NX
        return p, dx, ys[(p + ny - 1) % ny] + xs[dx]

    def home_of(s):
        p, k = s // 2, s % 2
        return p * NX + 2 * k + c, ys[(1 - p) % ny] + back_x[k]

    loads = [
        pltpu.make_async_copy(ids_hbm, ids_ref, load_sem.at[0]),
        pltpu.make_async_copy(prob_hbm, prob_ref, load_sem.at[1]),
        pltpu.make_async_copy(x_hbm, tt.at[0, pl.ds(0, feats), :], load_sem.at[2]),
        pltpu.make_async_copy(u_hbm, tt.at[0, pl.ds(feats, feats), :], load_sem.at[3]),
        pltpu.make_async_copy(x_hbm, tt.at[1, pl.ds(pad, feats), :], load_sem.at[4]),
        pltpu.make_async_copy(u_hbm, tt.at[1, pl.ds(pad + feats, feats), :], load_sem.at[5]),
        pltpu.make_async_copy(wd_hbm, wdraw, load_sem.at[6]),
        pltpu.make_async_copy(wg_hbm, wgu.at[pl.ds(0, wide_d), pl.ds(0, hid)], load_sem.at[7]),
        pltpu.make_async_copy(wu_hbm, wgu.at[pl.ds(0, wide_d), pl.ds(2 * hid, hid)], load_sem.at[8]),
    ]
    for copy in loads:
        copy.start()

    barrier = pltpu.get_barrier_semaphore()

    for n in range(ngroup):
        p, dx, e = target(n)

        def hello(e=e, core=dx % 2):
            pl.semaphore_signal(barrier, inc=1, device_id={"group": e, "dev": z * 2 + core}, device_id_type=MESH)

        if n == NX:
            pl.when(c == 1)(hello)
        else:
            hello()
    for n in range(ngroup // 2):
        p, k = n // 2, n % 2
        e = ys[p] + lax.rem(x + 2 * k + c, NX)
        pl.semaphore_signal(barrier, inc=1, device_id={"group": e, "dev": z * 2 + 1 - c}, device_id_type=MESH)
    for k in range(1, nz):
        pl.semaphore_signal(
            barrier, inc=1, device_id={"group": g, "dev": lax.rem(z + k, nz) * 2 + c}, device_id_type=MESH
        )
    greeted = ngroup + nslot + nz - 1 - (1 - c)

    zero = jnp.zeros((pad, toks), BF16)
    tt[0, pl.ds(chunk, pad), :] = zero
    tt[1, pl.ds(0, pad), :] = zero

    n_col = iota((ngroup, 1), 0)
    p_col = lax.shift_right_logical(n_col, 2)
    dx_col = jnp.bitwise_and(n_col, NX - 1)
    e_col = jnp.bitwise_and(y + p_col + ny - 1, ny - 1) * NX + jnp.bitwise_and(x + dx_col, NX - 1)
    loads[0].wait()
    loads[1].wait()
    ids = ids_ref[...]
    probs = prob_ref[...]
    hit = jnp.zeros((ngroup, toks), F32)
    prob_n = jnp.zeros((ngroup, toks), F32)
    for k in range(top):
        same = jnp.broadcast_to(ids[k : k + 1, :], (ngroup, toks)) == jnp.broadcast_to(e_col, (ngroup, toks))
        hit = hit + jnp.where(same, 1.0, 0.0)
        prob_n = prob_n + jnp.where(same, jnp.broadcast_to(probs[k : k + 1, :], (ngroup, toks)), 0.0)
    earlier = flag(iota((toks, toks), 0) < iota((toks, toks), 1))
    place_n = jnp.where(hit > 0.5, dot(hit.astype(BF16), earlier), -1.0)
    hits[...] = place_n
    place_bf = place_n.astype(BF16)
    part1 = prob_n.astype(BF16)
    rest = prob_n - part1.astype(F32)
    part2 = rest.astype(BF16)
    part3 = (rest - part2.astype(F32)).astype(BF16)

    step_rows = min(8, ngroup // 2) * MAIN

    def fill(i, carry):
        base = pl.multiple_of(i * step_rows, step_rows)
        row = iota((step_rows, 1), 0)
        rr = jnp.bitwise_and(row, MAIN - 1)
        spread = flag(lax.shift_right_logical(base + iota((step_rows, ngroup), 0), 4) == iota((step_rows, ngroup), 1))
        at = dot(spread, place_bf)
        pr = dot(spread, part1) + dot(spread, part2) + dot(spread, part3)
        m1 = at == jnp.broadcast_to(rr.astype(F32), at.shape)
        m2 = at == jnp.broadcast_to((MAIN + jnp.bitwise_and(rr, 1)).astype(F32), at.shape)
        pick1 = flag(m1)
        pickx = flag(m2)
        pick[pl.ds(base, step_rows), :] = pick1
        pick2[pl.ds(base, step_rows), :] = pickx
        pr1 = jnp.sum(jnp.where(m1, pr, 0.0), axis=1, keepdims=True)
        pr2 = jnp.sum(jnp.where(m2, pr, 0.0), axis=1, keepdims=True)
        got = dot_nt(pick1, tt[0])
        lane = iota((step_rows, WIDE), 1)
        got = jnp.where(jnp.logical_and(lane >= feats, lane < chunk), got * pr1, got)
        odd = dot_nt(pickx, tt[0])
        even = dot_nt(pickx, tt[1])
        part = lax.shift_right_logical(rr, 1)
        extra = jnp.zeros((step_rows, 128), F32)
        for tile in range(WIDE // 128):
            cut = slice(tile * 128, tile * 128 + 128)
            extra = jnp.where(part == 2 * tile, even[:, cut], extra)
            extra = jnp.where(part == 2 * tile + 1, odd[:, cut], extra)
        lane = iota((step_rows, 128), 1)
        extra = jnp.where(part * pad + lane - (128 - pad) >= feats, extra * pr2, extra)
        snd[pl.ds(base, step_rows), pl.ds(0, WIDE - 128)] = got[:, : WIDE - 128].astype(BF16)
        snd[pl.ds(base, step_rows), pl.ds(WIDE - 128, 128)] = jnp.where(
            lane >= 128 - pad, extra, got[:, WIDE - 128 :]
        ).astype(BF16)
        return carry

    for copy in loads[2:6]:
        copy.wait()
    steps = ngroup * MAIN // step_rows
    lax.fori_loop(0, steps // 2, fill, 0)
    pl.semaphore_wait(barrier, greeted)

    def fwd_copy(n, b, sem):
        p, dx, e = target(n)
        slot = p * 2 + dx // 2 - b * nb
        return pltpu.make_async_remote_copy(
            src_ref=snd.at[pl.ds(n * MAIN, MAIN), :],
            dst_ref=rcv.at[b, c, pl.ds(slot * MAIN, MAIN), :],
            send_sem=sem,
            recv_sem=fwd_recv.at[b],
            device_id={"group": e, "dev": z * 2 + dx % 2},
            device_id_type=MESH,
        )

    own_b, own_slot = (0, NX // 2) if ny > 2 else (1, 0)

    def send_batch(b):
        for n in range(b * nslot, (b + 1) * nslot):
            if n != NX:
                fwd_copy(n, b, fwd_send.at[0]).start()
        if b == own_b:

            @pl.when(c == 0)
            def _():
                pltpu.make_async_copy(
                    snd.at[pl.ds(NX * MAIN, MAIN), :],
                    rcv.at[own_b, 0, pl.ds(own_slot * MAIN, MAIN), :],
                    fwd_recv.at[own_b],
                ).start()

            @pl.when(c == 1)
            def _():
                fwd_copy(NX, own_b, fwd_send.at[1]).start()

    send_batch(0)
    lax.fori_loop(steps // 2, steps, fill, 0)
    send_batch(1)

    swaps = [
        pltpu.make_async_remote_copy(
            src_ref=wg_hbm,
            dst_ref=wgu.at[pl.ds(0, wide_d), pl.ds(hid, hid)],
            send_sem=swap_send.at[0],
            recv_sem=swap_recv.at[0],
            device_id=sib,
            device_id_type=MESH,
        ),
        pltpu.make_async_remote_copy(
            src_ref=wu_hbm,
            dst_ref=wgu.at[pl.ds(0, wide_d), pl.ds(3 * hid, hid)],
            send_sem=swap_send.at[1],
            recv_sem=swap_recv.at[1],
            device_id=sib,
            device_id_type=MESH,
        ),
        pltpu.make_async_remote_copy(
            src_ref=wdt.at[pl.ds(pad, wide_d), pl.ds(0, hid)],
            dst_ref=wdt.at[pl.ds(pad, wide_d), pl.ds(hid, hid)],
            send_sem=swap_send.at[2],
            recv_sem=swap_recv.at[2],
            device_id=sib,
            device_id_type=MESH,
        ),
    ]
    swaps[0].start()
    swaps[1].start()

    loads[6].wait()

    def turn(i, carry):
        base = pl.multiple_of(i * 128, 128)
        wdt[pl.ds(pl.multiple_of(base + pad, pad), 128), pl.ds(0, hid)] = wdraw[:, pl.ds(base, 128)].T
        return carry

    lax.fori_loop(0, wide_d // 128, turn, 0)
    swaps[2].start()

    wgu[pl.ds(wide_d, pad), :] = jnp.zeros((pad, 4 * hid), BF16)
    wdt[pl.ds(0, pad), :] = jnp.zeros((pad, 2 * hid), BF16)
    acc_gu[...] = jnp.zeros_like(acc_gu)
    acc_b[...] = jnp.zeros_like(acc_b)

    def set_place(i, carry):
        base = pl.multiple_of(i * 128, 128)
        a = base + iota((128, 2 * chunk), 0)
        f = iota((128, 2 * chunk), 1)
        goal = a + jnp.where(a >= feats, feats, 0)
        keep = a < chunk
        place[0, pl.ds(base, 128), :] = flag(jnp.logical_and(keep, f == goal))
        place[1, pl.ds(base, 128), :] = flag(jnp.logical_and(keep, f == goal + feats))
        return carry

    lax.fori_loop(0, WIDE // 128, set_place, 0)

    room = BACK - feats

    def set_away(h, carry):
        a, l = iota((WIDE, BACK), 0) - feats * h, iota((WIDE, BACK), 1)
        away[h, pl.ds(0, WIDE), :] = flag(jnp.logical_and(a == l, l < feats))
        inside = jnp.logical_and(a >= 0, a < feats)
        away[h, pl.ds(WIDE, WIDE), :] = flag(jnp.logical_and(inside, jnp.bitwise_and(a, room - 1) == l - feats))
        return carry

    def build(b):
        pltpu.make_async_copy(rcv.at[b], rcv.at[b], fwd_recv.at[b]).wait()
        widen = flag(iota((128, WIDE), 0) == 128 - pad + jnp.bitwise_and(iota((128, WIDE), 1), pad - 1))
        mine = lax.shift_right_logical(jnp.bitwise_and(iota((main, WIDE), 0), MAIN - 1), 1) == lax.shift_right_logical(
            iota((main, WIDE), 1), pad.bit_length() - 1
        )
        a, r = iota((2 * nb, main), 0), iota((2 * nb, main), 1)
        gather = flag(
            jnp.logical_and(
                lax.shift_right_logical(a, 1) == lax.shift_right_logical(r, 4),
                jnp.bitwise_and(a, 1) == jnp.bitwise_and(r, 1),
            )
        )
        whole, extra = 0.0, 0.0
        for h in range(2):
            got = rcv[b, h]
            wide = jnp.where(mine, dot(got[:, WIDE - 128 :], widen), 0.0).astype(BF16)
            last = dot(gather, wide).astype(BF16)
            whole = whole + dot(got, place[h])
            extra = extra + dot(last, place[h])
        ag[b, z, pl.ds(0, main), :] = whole.astype(BF16)
        ag[b, z, pl.ds(main, 2 * nb), :] = extra.astype(BF16)

    turn_to = 1 - 2 * c
    right = {"group": g, "dev": lax.rem(z + nz + turn_to, nz) * 2 + c}
    left = {"group": g, "dev": lax.rem(z + nz - turn_to, nz) * 2 + c}

    def along(k):
        return lax.rem(z + 2 * nz + k * turn_to, nz)

    half = nz // 2
    hops = [[half, nz - 1 - half], [nz - 1 - half, half]]

    fold = -(-rows // 32) * 16
    cuts = [pl.ds(0, fold), pl.ds(fold, rows - fold)]

    def ag_copy(b, way, s, part):
        which = along(-s) if way == 0 else along(s)
        return pltpu.make_async_remote_copy(
            src_ref=ag.at[b, which, cuts[part], :],
            dst_ref=ag.at[b, which, cuts[part], :],
            send_sem=ag_send.at[b, way, s, part],
            recv_sem=ag_recv.at[b, way, s, part],
            device_id=right if way == 0 else left,
            device_id_type=MESH,
        )

    def multiply(b, which):
        lane = iota((rows, 128), 1)
        mid = ag[b, which, :, pl.ds(WIDE - 128, 128)]
        none = jnp.zeros_like(mid)
        first = jnp.concatenate(
            [ag[b, which, :, pl.ds(0, WIDE - 128)], jnp.where(lane < 128 - pad, mid, none)], axis=1
        )
        second = jnp.concatenate(
            [jnp.where(lane >= 128 - pad, mid, none), ag[b, which, :, pl.ds(WIDE, WIDE - 128)]], axis=1
        )
        at = pl.ds(pl.multiple_of(which * chunk, pad), WIDE)
        acc_gu[b] += dot(first, wgu[at, :])
        acc_b[b] += dot(second, wdt[at, :])

    def ag_start(b, way):
        if hops[b][way] > 0:
            for part in range(2):
                ag_copy(b, way, 0, part).start()

    def ag_pass(*which):
        for part in range(2):
            for b, way, s in which:
                if s < hops[b][way]:
                    ag_copy(b, way, s, part).wait_recv()
                    if s + 1 < hops[b][way]:
                        ag_copy(b, way, s + 1, part).start()

    def ag_use(b, way, s):
        if s < hops[b][way]:
            multiply(b, along(-s - 1) if way == 0 else along(s + 1))

    tiles = WIDE // 128 - 1
    again_at = rows - fold
    halves = [pl.ds(0, 2 * rows), pl.ds(2 * rows, rs_snd.shape[3] - 2 * rows)]

    def rs_copy(b, way, s, part):
        return pltpu.make_async_remote_copy(
            src_ref=rs_snd.at[b, way, s, halves[part], :],
            dst_ref=rs_rcv.at[b, way, s, halves[part], :],
            send_sem=rs_send.at[b, way, s, part],
            recv_sem=rs_recv.at[b, way, s, part],
            device_id=right if way == 0 else left,
            device_id_type=MESH,
        )

    def term(b, which):
        return dot_nt(dgu[b], wgu[pl.ds(pl.multiple_of(which * chunk, pad), WIDE), :])

    def folded(total):
        tail = total[:, tiles * 128 :]
        lane = iota((fold, 128), 1)
        return jnp.where(lane < pad, tail[:fold], pltpu.roll(tail[again_at:], pad, 1))

    def rs_step(b, s):
        ways = [w for w in range(2) if s < hops[b][w]]
        totals = []
        for way in ways:
            over = hops[b][way] - s
            totals.append(term(b, along(over) if way == 0 else along(-over)))
        pieces = [[total[:, i * 128 : i * 128 + 128] for i in range(tiles)] + [folded(total)] for total in totals]
        for part in range(2):
            for way, piece in zip(ways, pieces):
                if s > 0:
                    rs_copy(b, way, s - 1, part).wait_recv()
                for i in (2 * part, 2 * part + 1):
                    at = pl.ds(i * rows, rows if i < tiles else fold)
                    value = piece[i]
                    if s > 0:
                        value = value + rs_rcv[b, way, s - 1, at, :].astype(F32)
                    rs_snd[b, way, s, at, :] = value.astype(BF16)
                rs_copy(b, way, s, part).start()

    def middle(b):
        gate, upper = acc_gu[b, :, pl.ds(0, 2 * hid)], acc_gu[b, :, pl.ds(2 * hid, 2 * hid)]
        back = acc_b[b]
        sig = 1.0 / (1.0 + jnp.exp(-gate))
        act = gate * sig
        slope = sig * (1.0 + gate * (1.0 - sig))
        dgu[b, :, pl.ds(0, 2 * hid)] = (back * upper * slope).astype(BF16)
        dgu[b, :, pl.ds(2 * hid, 2 * hid)] = (back * act).astype(BF16)
        acc_b[b] = act * upper * back

    def set_scores(b):
        row = lax.dot_general(
            jnp.ones((8, 2 * hid), F32),
            acc_b[b],
            (((1,), (1,)), ((), ())),
            preferred_element_type=F32,
            precision=lax.Precision.HIGHEST,
        )
        scores[z, pl.ds(4 * b, 4), pl.ds(0, rows)] = row[:4]

    def sc_copy(k):
        return pltpu.make_async_remote_copy(
            src_ref=scores.at[z],
            dst_ref=scores.at[z],
            send_sem=sc_send.at[k],
            recv_sem=sc_recv.at[k],
            device_id={"group": g, "dev": lax.rem(z + k, nz) * 2 + c},
            device_id_type=MESH,
        )

    build(0)
    ag_start(0, 0)
    ag_start(0, 1)
    scores[z] = jnp.zeros(scores.shape[1:], F32)
    lax.fori_loop(0, 2, set_away, 0)
    loads[7].wait()
    loads[8].wait()
    for copy in swaps:
        copy.wait_recv()
    multiply(0, z)

    build(1)
    ag_start(1, 0)
    ag_start(1, 1)
    multiply(1, z)
    for s in range(half):
        ag_pass((0, 0, s), (0, 1, s))
        ag_use(0, 0, s)
        ag_use(0, 1, s)
        if s < half - 1:
            ag_pass((1, 0, s), (1, 1, s))
            ag_use(1, 0, s)
            ag_use(1, 1, s)
    middle(0)
    rs_step(0, 0)
    ag_pass((1, 0, half - 1), (1, 1, half - 1))
    ag_use(1, 0, half - 1)
    ag_use(1, 1, half - 1)
    set_scores(0)
    middle(1)
    rs_step(1, 0)
    if half > 1:
        rs_step(0, 1)
    set_scores(1)
    for k in range(1, nz):
        sc_copy(k).start()
    for s in range(1, half):
        rs_step(1, s)
        if s + 1 < half:
            rs_step(0, s + 1)

    for k in range(1, nz):
        sc_copy(k).wait_recv()
    score = scores[0]
    for k in range(1, nz):
        score = score + scores[k]

    def ret_copy(b, i, h, sem):
        n, home = home_of(b * nb + i)
        return pltpu.make_async_remote_copy(
            src_ref=ret_snd.at[b, h, pl.ds(i * MAIN, MAIN), :],
            dst_ref=ret_rcv.at[pl.ds(pl.multiple_of(n * MAIN, MAIN), MAIN), :],
            send_sem=sem,
            recv_sem=ret_recv.at[b],
            device_id={"group": home, "dev": z * 2 + h},
            device_id_type=MESH,
        )

    for b in range(2):
        total = term(b, z)
        tail = folded(total)
        parts = [total[:, i * 128 : i * 128 + 128] for i in range(tiles)] + [tail]
        for part in range(2):
            for way in range(2):
                if hops[b][way] > 0:
                    s = hops[b][way] - 1
                    rs_copy(b, way, s, part).wait_recv()
                    for i in (2 * part, 2 * part + 1):
                        at = pl.ds(i * rows, rows if i < tiles else fold)
                        parts[i] = parts[i] + rs_rcv[b, way, s, at, :].astype(F32)
        tail = parts.pop()
        lane = iota((rows, 128), 1)
        tail = jnp.concatenate([tail, pltpu.roll(tail, pad, 1)[fold - again_at :]], axis=0)
        parts.append(jnp.where(lane < pad, tail, 0.0))
        total = jnp.concatenate([part.astype(BF16) for part in parts], axis=1)
        whole, extra = total[:main], total[main:]

        row = iota((main, BACK), 0)
        lane = iota((main, BACK), 1)
        q = jnp.bitwise_and(row, MAIN - 1)
        value = jnp.broadcast_to(score[4 * b : 4 * b + 1, :], (main, BACK))
        upper = value.astype(BF16).astype(F32)
        lower = value - upper
        slot = jnp.where(lane < main, lax.shift_right_logical(lane, 4), lax.shift_right_logical(lane - main, 1))
        fits = jnp.logical_and(lax.shift_right_logical(row, 4) == slot, lane < rows)
        value = jnp.where(q == MAIN - 2, upper, jnp.where(q == MAIN - 1, lower, 0.0))
        value = jnp.where(fits, value, 0.0).astype(BF16)
        a, l = iota((BACK, BACK), 0), iota((BACK, BACK), 1)
        number = jnp.where(a < main, jnp.bitwise_and(a, MAIN - 1), MAIN + jnp.bitwise_and(a, 1))
        carried = dot(value, flag(l == feats + number))

        again = flag(
            jnp.logical_and(
                lax.shift_right_logical(iota((main, 2 * nb), 0), 4)
                == lax.shift_right_logical(iota((main, 2 * nb), 1), 1),
                jnp.bitwise_and(iota((main, 2 * nb), 0), 1) == jnp.bitwise_and(iota((main, 2 * nb), 1), 1),
            )
        )
        extra = dot(again, extra)
        for h in range(2):
            lane = iota((main, WIDE), 1) - feats * h
            rr = lax.shift_right_logical(jnp.bitwise_and(iota((main, WIDE), 0), MAIN - 1), 1)
            mine = jnp.logical_and(lane >= rr * room, lane < rr * room + room)
            ends = jnp.where(jnp.logical_and(mine, lane < feats), extra, 0.0).astype(BF16)
            ret_snd[b, h] = (
                dot(whole, away[h, pl.ds(0, WIDE), :]) + dot(ends, away[h, pl.ds(WIDE, WIDE), :]) + carried
            ).astype(BF16)

        for i in range(nb):
            for h in range(2):

                def away_go(b=b, i=i, h=h):
                    ret_copy(b, i, h, ret_send.at[0]).start()

                if (b, i, h) == (own_b, own_slot, 0):
                    pl.when(c == 1)(away_go)
                else:
                    away_go()
        if b == own_b:

            @pl.when(c == 0)
            def _():
                pltpu.make_async_copy(
                    ret_snd.at[own_b, 0, pl.ds(own_slot * MAIN, MAIN), :],
                    ret_rcv.at[pl.ds(NX * MAIN, MAIN), :],
                    ret_recv.at[own_b],
                ).start()

    n_rows = nslot * MAIN
    total = 0.0
    sums = []
    for b in range(2):
        part = pl.ds(b * n_rows, n_rows)
        pltpu.make_async_copy(ret_rcv.at[part], ret_rcv.at[part], ret_recv.at[b]).wait()
        got = ret_rcv[part, :]
        end = got[:, BACK - 128 :]
        widen = flag(iota((128, BACK), 0) == 128 - room + jnp.bitwise_and(iota((128, BACK), 1), room - 1))
        mine = lax.shift_right_logical(
            jnp.bitwise_and(iota((n_rows, BACK), 0), MAIN - 1), 1
        ) == lax.shift_right_logical(iota((n_rows, BACK), 1), room.bit_length() - 1)
        wide = jnp.where(mine, dot(end, widen), 0.0).astype(BF16)
        total = total + dot_tn(got, pick[part, :]) + dot_tn(wide, pick2[part, :])
        a, r = iota((nslot, n_rows), 0), iota((nslot, n_rows), 1)
        this = a == lax.shift_right_logical(r, 4)
        r = jnp.bitwise_and(r, MAIN - 1)
        sums.append(
            dot(flag(jnp.logical_and(this, r == MAIN - 2)), end)
            + dot(flag(jnp.logical_and(this, r == MAIN - 1)), end)
        )
    out_ref[...] = total[:feats].astype(BF16)

    at = hits[...]
    score = jnp.concatenate(sums, axis=0)
    found = jnp.zeros((ngroup, toks), F32)
    for q in range(CAP):
        col = 128 - room + q
        found = jnp.where(at == float(q), jnp.broadcast_to(score[:, col : col + 1], found.shape), found)
    ids = ids_ref[...]
    for k in range(top):
        same = jnp.broadcast_to(ids[k : k + 1, :], (ngroup, toks)) == jnp.broadcast_to(e_col, (ngroup, toks))
        value = jnp.sum(jnp.where(same, found, 0.0), axis=0, keepdims=True)
        gp_ref[pl.ds(k, 1), :] = value / prob_ref[pl.ds(k, 1), :]

    most = 2 * nslot - 1
    part = snd.at[pl.ds(0, most * MAIN), :]
    pltpu.make_async_copy(part, part, fwd_send.at[0]).wait()
    for copy in swaps:
        copy.wait_send()
    for b in range(2):
        for way in range(2):
            for s in range(hops[b][way]):
                for part in range(2):
                    ag_copy(b, way, s, part).wait_send()
                    rs_copy(b, way, s, part).wait_send()
    for k in range(1, nz):
        sc_copy(k).wait_send()
    part = ret_rcv.at[pl.ds(0, most * MAIN), :]
    pltpu.make_async_copy(part, part, ret_send.at[0]).wait()

    @pl.when(c == 1)
    def _():
        one = snd.at[pl.ds(0, MAIN), :]
        pltpu.make_async_copy(one, one, fwd_send.at[1]).wait()
        one = ret_rcv.at[pl.ds(0, MAIN), :]
        pltpu.make_async_copy(one, one, ret_send.at[0]).wait()


def on_device(ny, nz, tokens, upstream, route_probs, expert_ids, w_gate, w_up, w_down):
    toks, feats = tokens.shape
    top = expert_ids.shape[1]
    wide_d, hid = w_gate.shape[1], w_gate.shape[2]
    ngroup = ny * NX
    nslot = ngroup // 2
    nb = nslot // 2
    main, rows = nb * MAIN, nb * CAP
    chunk = 2 * feats
    pad = WIDE - chunk
    half = nz // 2
    message = (WIDE // 128 - 1) * rows + -(-rows // 32) * 16
    dma = pltpu.SemaphoreType.DMA
    vmem = pl.BlockSpec(memory_space=pltpu.VMEM)
    hbm = pl.BlockSpec(memory_space=pltpu.HBM)
    out, gp = pl.pallas_call(
        functools.partial(kernel, ny, nz),
        out_shape=(jax.ShapeDtypeStruct((feats, toks), BF16), jax.ShapeDtypeStruct((top, toks), F32)),
        in_specs=[hbm] * 7,
        out_specs=(vmem, vmem),
        scratch_shapes=[
            pltpu.VMEM((top, toks), I32),
            pltpu.VMEM((top, toks), F32),
            pltpu.VMEM((2, WIDE, toks), BF16),
            pltpu.VMEM((ngroup * MAIN, WIDE), BF16),
            pltpu.VMEM((2, 2, main, WIDE), BF16),
            pltpu.VMEM((2, WIDE, 2 * chunk), BF16),
            pltpu.VMEM((2, 2 * WIDE, BACK), BF16),
            pltpu.VMEM((ngroup, toks), F32),
            pltpu.VMEM((ngroup * MAIN, toks), BF16),
            pltpu.VMEM((ngroup * MAIN, toks), BF16),
            pltpu.VMEM((2, nz, rows, 2 * chunk), BF16),
            pltpu.VMEM((wide_d + pad, 4 * hid), BF16),
            pltpu.VMEM((hid, wide_d), BF16),
            pltpu.VMEM((wide_d + pad, 2 * hid), BF16),
            pltpu.VMEM((2, rows, 4 * hid), F32),
            pltpu.VMEM((2, rows, 2 * hid), F32),
            pltpu.VMEM((2, rows, 4 * hid), BF16),
            pltpu.VMEM((2, 2, half, message, 128), BF16),
            pltpu.VMEM((2, 2, half, message, 128), BF16),
            pltpu.VMEM((nz, 8, BACK), F32),
            pltpu.VMEM((2, 2, main, BACK), BF16),
            pltpu.VMEM((ngroup * MAIN, BACK), BF16),
            dma((9,)),
            dma((3,)),
            dma((3,)),
            dma((2,)),
            dma((2,)),
            dma((2, 2, half, 2)),
            dma((2, 2, half, 2)),
            dma((2, 2, half, 2)),
            dma((2, 2, half, 2)),
            dma((nz,)),
            dma((nz,)),
            dma((1,)),
            dma((2,)),
        ],
        compiler_params=pltpu.CompilerParams(
            collective_id=0, has_side_effects=True, vmem_limit_bytes=60 * 1024 * 1024
        ),
    )(tokens.T, upstream.T, route_probs.T, expert_ids.T, w_gate[0], w_up[0], w_down[0])
    return out.T, gp.T


def solution(mesh):
    ny = mesh.shape["group"] // NX
    nz = mesh.shape["dev"] // 2
    placed = (
        P("group", "dev"),
        P("group", "dev"),
        P("group", None),
        P("group", None),
        P("group", None, "dev"),
        P("group", None, "dev"),
        P("group", "dev", None),
    )
    return jax.shard_map(
        functools.partial(on_device, ny, nz),
        mesh=mesh,
        in_specs=placed,
        out_specs=(P("group", "dev"), P("group", None)),
        check_vma=False,
    )
```
